32 devices in a mesh: batch: 8 (over z, y), band: 4 (over x, core).
Axes of the slice: x: 2, y: 2, z: 4, core: 2. Of those that a mesh axis runs over, the one named last changes fastest.
Arguments:
- patches: bfloat16 [64, 256, 768], P('batch', 'band'), may hold values from -6 to 6
- queries: bfloat16 [64, 256, 768], P('batch', 'band'), may hold values from -6 to 6
- cotangent: bfloat16 [64, 256, 768], P('batch', 'band'), may hold values from -6 to 6
- counts: int32 [64], P('batch'), may hold values from 16 to 256, as said below
- masked: int32 [64, 256], P('batch', 'band'), may hold values from 0 to 1, as said below
- enc_gains: float32 [2, 768], replicated, may hold values from 0.5 to 1.5
- enc_shifts: float32 [6, 768], replicated, may hold values from -3 to 3
- enc_widebias: float32 [3072], replicated, may hold values from -3 to 3
- enc_scales: float32 [2, 768], replicated, may hold values from 0.5 to 1.5
- enc_project: bfloat16 [768, 2304], replicated, may hold values from -0.21875 to 0.21875
- enc_output: bfloat16 [768, 768], replicated, may hold values from -0.625 to 0.625
- enc_expand: bfloat16 [768, 3072], replicated, may hold values from -0.21875 to 0.21875
- enc_reduce: bfloat16 [3072, 768], replicated, may hold values from -0.109375 to 0.109375
- reg_gains: float32 [3, 768], replicated, may hold values from 0.5 to 1.5
- reg_shifts: float32 [7, 768], replicated, may hold values from -3 to 3
- reg_widebias: float32 [3072], replicated, may hold values from -3 to 3
- reg_scales: float32 [2, 768], replicated, may hold values from 0.5 to 1.5
- reg_query: bfloat16 [768, 768], replicated, may hold values from -0.21875 to 0.21875
- reg_keyval: bfloat16 [768, 1536], replicated, may hold values from -0.21875 to 0.21875
- reg_output: bfloat16 [768, 768], replicated, may hold values from -0.625 to 0.625
- reg_expand: bfloat16 [768, 3072], replicated, may hold values from -0.21875 to 0.21875
- reg_reduce: bfloat16 [3072, 768], replicated, may hold values from -0.109375 to 0.109375
Outputs:
- prediction: float32 [64, 256, 768], P('batch', 'band')
- patch_grad: float32 [64, 256, 768], P('batch', 'band')
- query_grad: float32 [64, 256, 768], P('batch', 'band')
- enc_gains_grad: float32 [2, 768], P(None, 'band')
- enc_shifts_grad: float32 [6, 768], P(None, 'band')
- enc_wide_grad: float32 [3072], P('band')
- enc_scales_grad: float32 [2, 768], P(None, 'band')
- enc_project_grad: float32 [768, 2304], P('band')
- enc_output_grad: float32 [768, 768], P('band')
- enc_expand_grad: float32 [768, 3072], P('band')
- enc_reduce_grad: float32 [3072, 768], P('band')
- reg_gains_grad: float32 [3, 768], P(None, 'band')
- reg_shifts_grad: float32 [7, 768], P(None, 'band')
- reg_wide_grad: float32 [3072], P('band')
- reg_scales_grad: float32 [2, 768], P(None, 'band')
- reg_query_grad: float32 [768, 768], P('band')
- reg_keyval_grad: float32 [768, 1536], P('band')
- reg_output_grad: float32 [768, 768], P('band')
- reg_expand_grad: float32 [768, 3072], P('band')
- reg_reduce_grad: float32 [3072, 768], P('band')
The draws below stay inside these ranges and needn't reach their ends.
Inputs may be any that keep to these rules, and one draw needn't show every extreme that they name: Slot p of image i is real when p < counts[i]; some image has all 256 slots real. 1 marks a masked slot; slot 0 of every image is never masked.
All inputs are finite; a program needn't handle non-finite values.
Results may differ from the reference program's by a relative error of at most 0.03.
Values may be sent and summed in bfloat16 or wider, within the bound.
No kernel may reach another device: no remote copies, remote signals or barrier semaphores. Data moves between devices by JAX's collectives and lax.ppermute only.
A program may use at most 256 MiB of HBM per device.

```python
import math
import jax
import jax.numpy as jnp
from jax import lax

D = 768
HEADS = 12
HD = 64
FF = 3072
GRID = 256
IMAGES = 64


def draw_counts(key, part):
    key = jax.random.fold_in(key, 11)
    first_key, second_key, third_key = jax.random.split(key, 3)
    divisor = jax.random.randint(first_key, (IMAGES,), 1, 17)
    jitter = jax.random.randint(second_key, (IMAGES,), 0, 16)
    raw_counts = jnp.minimum(GRID // divisor + jitter, GRID)
    full_image = jax.random.randint(third_key, (), 0, IMAGES)
    return jnp.where(jnp.arange(IMAGES) == full_image, GRID, raw_counts).astype(jnp.int32)


def draw_masked(key, part):
    key = jax.random.fold_in(key, 23)
    random_bits = jax.random.randint(key, (IMAGES, GRID), 0, 2)
    return jnp.where(jnp.arange(GRID)[None, :] == 0, 0, random_bits).astype(jnp.int32)


def steps_of(own_key, extent, pieces, smallest, high):
    loudness = 1.0
    for dim, parts in pieces:
        heights = jax.random.uniform(jax.random.fold_in(jax.random.fold_in(own_key, 6), dim), (parts,), jnp.float32, smallest / len(pieces), high / len(pieces))
        loudness = loudness * jnp.repeat(jnp.exp(heights), extent[dim] // parts).reshape((-1,) + (1,) * (len(extent) - 1 - dim))
    return loudness


def bell_draw(rng, shape, spread, bound, shards=(), kind=jnp.bfloat16):
    loudness = steps_of(rng, shape, shards, -0.22, 0.18) if shards else 1.0
    drawn = jax.random.normal(rng, shape, jnp.float32) * spread * loudness
    return jnp.minimum(jnp.maximum(drawn, -bound), bound).astype(kind)


def setup_inputs(seed: int = 0) -> dict:
    seeds = jax.random.split(jax.random.key(seed), 23)
    return {
        "patches": bell_draw(seeds[0], (IMAGES, GRID, D), 1.0, 6.0, ((0, 8), (1, 4))),
        "queries": bell_draw(seeds[1], (IMAGES, GRID, D), 1.0, 6.0, ((0, 8), (1, 4))),
        "cotangent": bell_draw(seeds[2], (IMAGES, GRID, D), 1.0, 6.0, ((0, 8), (1, 4))),
        "counts": draw_counts(jax.random.fold_in(seeds[22], 71), 0),
        "masked": draw_masked(jax.random.fold_in(seeds[22], 71), 0),
        "enc_gains": jnp.clip(1.0 + 0.1 * jax.random.normal(seeds[5], (2, D), jnp.float32), 0.5, 1.5),
        "enc_shifts": bell_draw(seeds[6], (6, D), 0.5, 3.0, (), jnp.float32),
        "enc_widebias": bell_draw(seeds[7], (FF,), 0.5, 3.0, (), jnp.float32),
        "enc_scales": jnp.clip(jnp.exp(jax.random.uniform(seeds[8], (2, D), jnp.float32, math.log(0.5), math.log(1.5))), 0.5, 1.5),
        "enc_project": bell_draw(seeds[9], (D, 3 * D), D ** -0.5, 0.21875),
        "enc_output": bell_draw(seeds[10], (D, D), (D // 8) ** -0.5, 0.625),
        "enc_expand": bell_draw(seeds[11], (D, FF), D ** -0.5, 0.21875),
        "enc_reduce": bell_draw(seeds[12], (FF, D), FF ** -0.5, 0.109375),
        "reg_gains": jnp.clip(1.0 + 0.1 * jax.random.normal(seeds[13], (3, D), jnp.float32), 0.5, 1.5),
        "reg_shifts": bell_draw(seeds[14], (7, D), 0.5, 3.0, (), jnp.float32),
        "reg_widebias": bell_draw(seeds[15], (FF,), 0.5, 3.0, (), jnp.float32),
        "reg_scales": jnp.clip(jnp.exp(jax.random.uniform(seeds[16], (2, D), jnp.float32, math.log(0.5), math.log(1.5))), 0.5, 1.5),
        "reg_query": bell_draw(seeds[17], (D, D), D ** -0.5, 0.21875),
        "reg_keyval": bell_draw(seeds[18], (D, 2 * D), D ** -0.5, 0.21875),
        "reg_output": bell_draw(seeds[19], (D, D), (D // 8) ** -0.5, 0.625),
        "reg_expand": bell_draw(seeds[20], (D, FF), D ** -0.5, 0.21875),
        "reg_reduce": bell_draw(seeds[21], (FF, D), FF ** -0.5, 0.109375),
    }


EPS = 1e-06
ROOT_HALF = 0.7071067811865476
NEG_LARGE = -1e+30

@jax.custom_vjp
def low(v):
    return lax.optimization_barrier(v.astype(jnp.bfloat16)).astype(jnp.float32)

@jax.custom_vjp
def low_back(v):
    return v

def low_keep(v):
    return (low(v), None)

def low_pass(kept, grad):
    return (grad,)

def back_keep(v):
    return (v, None)

def back_low(kept, grad):
    return (low(grad),)
low.defvjp(low_keep, low_pass)
low_back.defvjp(back_keep, back_low)

def layer_norm(values, norm_gain, norm_shift):
    row_mean = lax.optimization_barrier(jnp.mean(values, -1, keepdims=True))
    centred = values - row_mean
    variance = lax.optimization_barrier(jnp.mean(centred * centred, -1, keepdims=True))
    return centred * lax.rsqrt(variance + EPS) * norm_gain + norm_shift

def apply_weight(row_data, weight):
    return jnp.dot(row_data, weight, precision=lax.Precision.HIGHEST)

def smooth_gate(pre_act):
    return 0.5 * pre_act * (1.0 + lax.erf(pre_act * ROOT_HALF))

def heads_of(row_data):
    return row_data.reshape(row_data.shape[0], row_data.shape[1], HEADS, HD)

def attend(query_rows, key_rows, value_rows, keep_keys):
    raw_scores = jnp.einsum('nqhd,nkhd->nhqk', heads_of(query_rows), heads_of(key_rows), precision=lax.Precision.HIGHEST) * HD ** (-0.5)
    scores = jnp.where(keep_keys[:, None, None, :] > 0, low_back(raw_scores), NEG_LARGE)
    row_top = lax.optimization_barrier(jnp.max(scores, -1, keepdims=True))
    exp_scores = jnp.exp(scores - row_top)
    attn_weights = low(exp_scores / lax.optimization_barrier(jnp.sum(exp_scores, -1, keepdims=True)))
    mixed = jnp.einsum('nhqk,nkhd->nqhd', attn_weights, heads_of(value_rows), precision=lax.Precision.HIGHEST)
    return mixed.reshape(query_rows.shape)

def feed_forward(middle, norm_gain, norm_shift, expand, wide_bias, reduce_weight, out_bias):
    normed = low(layer_norm(middle, norm_gain, norm_shift))
    pre_act = low_back(apply_weight(normed, expand) + wide_bias)
    return low_back(apply_weight(low(smooth_gate(pre_act)), reduce_weight) + out_bias)

def two_blocks(params, patch_rows, query_rows, keep_keys, pick_rows):
    enc_gains, enc_shifts, enc_widebias, enc_scales, enc_project, enc_output, enc_expand, enc_reduce, reg_gains, reg_shifts, reg_widebias, reg_scales, reg_query, reg_keyval, reg_output, reg_expand, reg_reduce = params
    blank_row = jnp.zeros_like(enc_shifts[0])
    normed = low(low_back(layer_norm(patch_rows, enc_gains[0], enc_shifts[0])))
    triple = low(low_back(apply_weight(normed, enc_project) + jnp.concatenate([enc_shifts[1], blank_row, enc_shifts[2]])))
    mixed = low(low_back(attend(triple[..., :D], triple[..., D:2 * D], triple[..., 2 * D:], keep_keys)))
    branch = low(low_back(apply_weight(mixed, enc_output) + enc_shifts[3]))
    middle = patch_rows + enc_scales[0] * branch
    encoded = middle + enc_scales[1] * feed_forward(middle, enc_gains[1], enc_shifts[4], enc_expand, enc_widebias, enc_reduce, enc_shifts[5])
    query_normed = low(low_back(layer_norm(query_rows, reg_gains[0], reg_shifts[0])))
    pair_normed = low(low_back(layer_norm(encoded, reg_gains[1], reg_shifts[1])))
    query_proj = low(low_back(apply_weight(query_normed, reg_query) + reg_shifts[2]))
    pair_proj = low(low_back(apply_weight(pair_normed, reg_keyval) + jnp.concatenate([blank_row, reg_shifts[3]])))
    reg_mixed = low(low_back(attend(query_proj, pair_proj[..., :D], pair_proj[..., D:], keep_keys)))
    reg_branch = low(low_back(apply_weight(reg_mixed, reg_output) + reg_shifts[4]))
    reg_middle = query_rows + reg_scales[0] * reg_branch
    final_rows = reg_middle + reg_scales[1] * feed_forward(reg_middle, reg_gains[2], reg_shifts[5], reg_expand, reg_widebias, reg_reduce, reg_shifts[6])
    return final_rows * pick_rows[..., None]

def reference(patches, queries, cotangent, counts, masked, enc_gains, enc_shifts, enc_widebias, enc_scales, enc_project, enc_output, enc_expand, enc_reduce, reg_gains, reg_shifts, reg_widebias, reg_scales, reg_query, reg_keyval, reg_output, reg_expand, reg_reduce):
    slot_index = jnp.arange(GRID, dtype=jnp.int32)
    is_valid = slot_index[None, :] < counts[:, None]
    keep_keys = jnp.where(is_valid & (masked == 0), 1.0, 0.0).astype(jnp.float32)
    pick_rows = jnp.where(is_valid & (masked == 1), 1.0, 0.0).astype(jnp.float32)
    params = tuple((w.astype(jnp.float32) for w in (enc_gains, enc_shifts, enc_widebias, enc_scales, enc_project, enc_output, enc_expand, enc_reduce, reg_gains, reg_shifts, reg_widebias, reg_scales, reg_query, reg_keyval, reg_output, reg_expand, reg_reduce)))
    group_size = math.gcd(IMAGES, 16)
    group_count = IMAGES // group_size

    def shaped(values):
        return values.reshape((group_count, group_size) + values.shape[1:])
    group_data = (shaped(patches.astype(jnp.float32)), shaped(queries.astype(jnp.float32)), shaped(keep_keys), shaped(pick_rows), shaped(cotangent.astype(jnp.float32)))

    def one_group(running, item_data):
        patch_rows, query_rows, keep_rows, pick_part, cot_rows = item_data
        result, pull_back = jax.vjp(lambda p, a, b: two_blocks(p, a, b, keep_rows, pick_part), params, patch_rows, query_rows)
        param_grads, patch_part, query_part = pull_back(cot_rows)
        running = jax.tree.map(lambda c, g: c + g, running, param_grads)
        return (running, (result, patch_part, query_part))
    start_sums = jax.tree.map(jnp.zeros_like, params)
    summed, (prediction, patch_grad, query_grad) = lax.scan(one_group, start_sums, group_data)
    full_shape = (IMAGES, GRID, D)
    return (prediction.reshape(full_shape), patch_grad.reshape(full_shape), query_grad.reshape(full_shape), summed[0], summed[1], summed[2], summed[3], summed[4], summed[5], summed[6], summed[7], summed[8], summed[9], summed[10], summed[11], summed[12], summed[13], summed[14], summed[15], summed[16])
```

```python
import functools

import jax
import jax.numpy as jnp
from jax import lax
from jax.experimental import pallas as pl
from jax.experimental.pallas import tpu as pltpu
from jax.sharding import PartitionSpec as P

HEADS = 12
HD = 64
EPS = 1e-06
ROOT_HALF = 0.7071067811865476
INV_ROOT_TAU = 0.3989422804014327
NEG_LARGE = -1e30
F32 = jnp.float32
BF16 = jnp.bfloat16
VMEM_LIMIT = 56 * 1024 * 1024
LANES = 128


def dot(a, b):
    return lax.dot_general(a, b, (((1,), (0,)), ((), ())), preferred_element_type=F32)


def dot_nt(a, b):
    return lax.dot_general(a, b, (((1,), (1,)), ((), ())), preferred_element_type=F32)


def dot_tn(a, b):
    return lax.dot_general(a, b, (((0,), (0,)), ((), ())), preferred_element_type=F32)


def unit(values):
    row_mean = jnp.mean(values, -1, keepdims=True)
    centred = values - row_mean
    variance = jnp.mean(centred * centred, -1, keepdims=True)
    inv_std = lax.rsqrt(variance + EPS)
    return centred * inv_std, inv_std


def unit_back(grad_out, unit_rows, inv_std, gain):
    scaled = grad_out * gain
    first_term = jnp.mean(scaled, -1, keepdims=True)
    second_term = jnp.mean(scaled * unit_rows, -1, keepdims=True)
    return inv_std * (scaled - first_term - unit_rows * second_term)


def rows_sum(values):
    return jnp.sum(values, 0, keepdims=True)


def gate_and_slope(pre_act):
    bell = 0.5 * (1.0 + lax.erf(pre_act * ROOT_HALF))
    slope = bell + pre_act * INV_ROOT_TAU * jnp.exp(-0.5 * pre_act * pre_act)
    return (pre_act * bell).astype(BF16), slope.astype(BF16)


class Meta:
    def __init__(self, ref, images):
        self.ref, self.images = ref, images

    def bins(self):
        return self.ref[0]

    def band(self):
        return self.ref[1]

    def bin_of(self, image):
        return self.ref[2 + image]

    def keep_off(self, image):
        return self.ref[2 + self.images + image]

    def keep_count(self, image):
        return self.ref[2 + 2 * self.images + image]

    def pick_off(self, image):
        return self.ref[2 + 3 * self.images + image]

    def pick_count(self, image):
        return self.ref[2 + 4 * self.images + image]

    def segments(self, bin_now, kind, shape, dim, blank):
        rows = lax.broadcasted_iota(jnp.int32, shape, dim)
        owner = jnp.full(shape, blank, jnp.int32)
        for image in range(self.images):
            start = self.keep_off(image) if kind == "keep" else self.pick_off(image)
            count = self.keep_count(image) if kind == "keep" else self.pick_count(image)
            stop = start + jnp.where(self.bin_of(image) == bin_now, count, 0)
            owner = jnp.where((rows >= start) & (rows < stop), image, owner)
        return owner


def key_mask(meta, bin_now, query_kind, size):
    query_owner = meta.segments(bin_now, query_kind, (size, 1), 0, -2)
    key_owner = meta.segments(bin_now, "keep", (1, size), 1, -1)
    return query_owner == key_owner


def quarter_rows(meta, width, parts):
    part = width // parts
    row = lax.broadcasted_iota(jnp.int32, (part, width), 0) + meta.band() * part
    return (row == lax.broadcasted_iota(jnp.int32, (part, width), 1)).astype(BF16)


def lower_half():
    return lax.broadcasted_iota(jnp.int32, (1, LANES), 1) < HD


def attend_forward(query_of, key_of, value_of, mask_ref, store, size):
    low = lower_half()
    sides = (low.astype(BF16), (~low).astype(BF16))
    lane = lax.broadcasted_iota(jnp.int32, (size, LANES), 1)
    totals = jnp.zeros((size, LANES), F32)
    for pair in range(HEADS // 2):
        cols = slice(pair * LANES, (pair + 1) * LANES)
        query, key, value = query_of(cols), key_of(cols), value_of(cols)
        mixed = []
        for side in range(2):
            scores = dot_nt(query, key * sides[side]) * HD ** (-0.5)
            scores = jnp.where(mask_ref[...] > 0, scores, NEG_LARGE)
            row_top = jnp.max(scores, -1, keepdims=True)
            exp_scores = jnp.exp(scores - row_top)
            row_total = jnp.sum(exp_scores, -1, keepdims=True)
            weights = (exp_scores * (1.0 / row_total)).astype(BF16)
            totals = jnp.where(lane == 2 * pair + side, row_top + jnp.log(row_total), totals)
            mixed.append(dot(weights, value))
        store(cols, jnp.where(low, mixed[0], mixed[1]))
    return totals


def attend_backward(query_of, key_of, value_of, grad_of, totals, mask_ref, store):
    low = lower_half()
    sides = (low.astype(BF16), (~low).astype(BF16))
    for pair in range(HEADS // 2):
        cols = slice(pair * LANES, (pair + 1) * LANES)
        query, key, value, grad = query_of(cols), key_of(cols), value_of(cols), grad_of(cols)
        grad_query, grad_key, grad_value = [], [], []
        for side in range(2):
            head = 2 * pair + side
            scores = dot_nt(query, key * sides[side]) * HD ** (-0.5)
            scores = jnp.where(mask_ref[...] > 0, scores, NEG_LARGE)
            probs = jnp.exp(scores - totals[:, head : head + 1])
            grad_value.append(dot_tn(probs.astype(BF16), grad))
            grad_probs = dot_nt(grad, value * sides[side])
            inner = jnp.sum(grad_probs * probs, -1, keepdims=True)
            grad_scores = (probs * (grad_probs - inner)).astype(BF16)
            grad_query.append(dot(grad_scores, key))
            grad_key.append(dot_tn(grad_scores, query))
        store(
            cols,
            jnp.where(low, grad_query[0], grad_query[1]) * HD ** (-0.5),
            jnp.where(low, grad_key[0], grad_key[1]) * HD ** (-0.5),
            jnp.where(low, grad_value[0], grad_value[1]),
        )


def pack_rows(meta, bin_now, place_ref, sources, size):
    for _, packed in sources:
        packed[...] = jnp.zeros_like(packed)
    for image in range(meta.images):

        @pl.when(meta.bin_of(image) == bin_now)
        def _():
            row = lax.broadcasted_iota(jnp.int32, (size, size), 0)
            chosen = (row == place_ref[image : image + 1, :]).astype(BF16)
            for gathered, packed in sources:
                rows = jnp.concatenate(
                    [gathered[band, image] for band in range(gathered.shape[0])], 0
                )
                packed[...] += dot(chosen, rows)


class Weights:
    def __init__(self, sources, targets, sems):
        self.copies = [
            pltpu.make_async_copy(source, target, sems.at[i])
            for i, (source, target) in enumerate(zip(sources, targets, strict=True))
        ]

    def start(self):
        @pl.when(pl.program_id(0) == 0)
        def _():
            for copy in self.copies:
                copy.start()

    def wait(self, index):
        @pl.when(pl.program_id(0) == 0)
        def _():
            self.copies[index].wait()


def add_row(small_ref, row, values):
    small_ref[row : row + 1, :] += values


def first_step(refs):
    @pl.when(pl.program_id(0) == 0)
    def _():
        for ref in refs:
            ref[...] = jnp.zeros_like(ref)


def last_step(meta, write):
    @pl.when(pl.program_id(0) == meta.bins() - 1)
    def _():
        write()


def plan_kernel(images, counts_ref, band_ref, keep_ref, pick_ref, meta_ref, keep_place_ref, pick_place_ref, words):
    size = keep_ref.shape[1]
    before = (
        lax.broadcasted_iota(jnp.int32, (size, size), 0)
        <= lax.broadcasted_iota(jnp.int32, (size, size), 1)
    ).astype(BF16)
    keep, pick = keep_ref[...], pick_ref[...]
    keep_rank = dot(keep.astype(BF16), before).astype(jnp.int32) - 1
    pick_rank = dot(pick.astype(BF16), before).astype(jnp.int32) - 1
    for image in range(images):
        words[0, image] = jnp.sum(keep[image : image + 1, :]).astype(jnp.int32)
        words[1, image] = jnp.sum(pick[image : image + 1, :]).astype(jnp.int32)
        for row in (2, 3, 4):
            words[row, image] = 0

    def place(_, bins):
        def largest(image, best):
            open_now = words[4, image] == 0
            better = open_now & ((best < 0) | (counts_ref[image] > counts_ref[jnp.maximum(best, 0)]))
            return jnp.where(better, image, best)

        image = lax.fori_loop(0, images, largest, jnp.int32(-1))
        keep_count, pick_count = words[0, image], words[1, image]

        def first_fit(step, best):
            bin_now = images - 1 - step
            fits = (words[2, bin_now] + keep_count <= size) & (words[3, bin_now] + pick_count <= size)
            return jnp.where(fits, bin_now, best)

        bin_now = lax.fori_loop(0, images, first_fit, jnp.int32(0))
        meta_ref[2 + image] = bin_now
        meta_ref[2 + images + image] = words[2, bin_now]
        meta_ref[2 + 2 * images + image] = keep_count
        meta_ref[2 + 3 * images + image] = words[3, bin_now]
        meta_ref[2 + 4 * images + image] = pick_count
        words[2, bin_now] = words[2, bin_now] + keep_count
        words[3, bin_now] = words[3, bin_now] + pick_count
        words[4, image] = 1
        return jnp.maximum(bins, bin_now + 1)

    meta_ref[0] = lax.fori_loop(0, images, place, jnp.int32(0))
    meta_ref[1] = band_ref[0]
    for image in range(images):
        row = slice(image, image + 1)
        keep_place_ref[row, :] = jnp.where(
            keep[row, :] > 0, keep_rank[row, :] + meta_ref[2 + images + image], -1
        )
        pick_place_ref[row, :] = jnp.where(
            pick[row, :] > 0, pick_rank[row, :] + meta_ref[2 + 3 * images + image], -1
        )


def ffn_forward(normed, expand, wide_bias, reduce_weight, act_ref, slope_ref, width):
    total = None
    for start in range(0, expand.shape[1], width):
        cols = slice(start, start + width)
        act, slope = gate_and_slope(dot(normed, expand[:, cols]) + wide_bias[:, cols])
        act_ref[:, cols] = act
        slope_ref[:, cols] = slope
        part = dot(act, reduce_weight[cols, :])
        total = part if total is None else total + part
    return total


def ffn_backward(grad_low, slope_ref, normed_part, expand, reduce_weight, expand_acc, wide_ref, width):
    total = None
    for start in range(0, expand.shape[1], width):
        cols = slice(start, start + width)
        grad_act = dot_nt(grad_low, reduce_weight[cols, :])
        grad_pre = grad_act * slope_ref[:, cols].astype(F32)
        grad_pre_low = grad_pre.astype(BF16)
        wide_ref[0:1, cols] += rows_sum(grad_pre_low.astype(F32))
        expand_acc[:, cols] += dot(normed_part, grad_pre_low)
        part = dot_nt(grad_pre_low, expand[:, cols])
        total = part if total is None else total + part
    return total


def enc_forward_kernel(
    images,
    parts,
    meta_ref,
    place_ref,
    rows_ref,
    gains,
    shifts,
    wide_bias,
    scales,
    reg_gains,
    reg_shifts,
    project_hbm,
    output_hbm,
    expand_hbm,
    reduce_hbm,
    keyval_hbm,
    x_out,
    triple_out,
    totals_out,
    normed_t_out,
    mixed_t_out,
    branch_out,
    act_out,
    slope_out,
    middle_t_out,
    ffn_out,
    pair_t_out,
    pair_out,
    project,
    output,
    expand,
    reduce_weight,
    keyval,
    sems,
    packed,
    mask_ref,
    act_all,
    mixed_ref,
):
    meta = Meta(meta_ref, images)
    bin_now = pl.program_id(0)
    weights = Weights(
        (project_hbm, output_hbm, expand_hbm, reduce_hbm, keyval_hbm),
        (project, output, expand, reduce_weight, keyval),
        sems,
    )
    weights.start()
    size, width = packed.shape
    pack_rows(meta, bin_now, place_ref, ((rows_ref, packed),), size)
    mask_ref[...] = key_mask(meta, bin_now, "keep", size).astype(F32)
    part_of = quarter_rows(meta, width, parts)
    x = packed[...]
    x_out[...] = x.astype(BF16)
    unit_rows, _ = unit(x)
    normed = (unit_rows * gains[0:1, :] + shifts[0:1, :]).astype(BF16)
    normed_t_out[...] = dot_nt(part_of, normed).astype(BF16)
    weights.wait(0)
    triple_out[:, :width] = (dot(normed, project[:, :width]) + shifts[1:2, :]).astype(BF16)
    triple_out[:, width : 2 * width] = dot(normed, project[:, width : 2 * width]).astype(BF16)
    triple_out[:, 2 * width :] = (dot(normed, project[:, 2 * width :]) + shifts[2:3, :]).astype(BF16)

    def store(cols, mixed):
        mixed_ref[:, cols] = mixed.astype(BF16)

    totals_out[...] = attend_forward(
        lambda cols: triple_out[:, cols],
        lambda cols: triple_out[:, width + cols.start : width + cols.stop],
        lambda cols: triple_out[:, 2 * width + cols.start : 2 * width + cols.stop],
        mask_ref,
        store,
        size,
    )
    mixed = mixed_ref[...]
    mixed_t_out[...] = dot_nt(part_of, mixed).astype(BF16)
    weights.wait(1)
    branch = (dot(mixed, output[...]) + shifts[3:4, :]).astype(BF16)
    branch_out[...] = branch
    middle = x + scales[0:1, :] * branch.astype(F32)
    unit_rows, _ = unit(middle)
    normed = (unit_rows * gains[1:2, :] + shifts[4:5, :]).astype(BF16)
    middle_t_out[...] = dot_nt(part_of, normed).astype(BF16)
    weights.wait(2)
    weights.wait(3)
    part_width = expand.shape[1] // parts
    ffn = ffn_forward(normed, expand, wide_bias, reduce_weight, act_all, slope_out, part_width) + shifts[5:6, :]
    act_out[...] = act_all[:, pl.ds(pl.multiple_of(meta.band() * part_width, part_width), part_width)]
    ffn_out[...] = ffn
    encoded = middle + scales[1:2, :] * ffn
    unit_rows, _ = unit(encoded)
    pair_normed = (unit_rows * reg_gains[1:2, :] + reg_shifts[1:2, :]).astype(BF16)
    pair_t_out[...] = dot_nt(part_of, pair_normed).astype(BF16)
    weights.wait(4)
    pair_out[:, :width] = dot(pair_normed, keyval[:, :width]).astype(BF16)
    pair_out[:, width:] = (dot(pair_normed, keyval[:, width:]) + reg_shifts[3:4, :]).astype(BF16)


def reg_forward_kernel(
    images,
    parts,
    meta_ref,
    place_ref,
    rows_ref,
    grads_ref,
    pair_ref,
    gains,
    shifts,
    wide_bias,
    scales,
    query_hbm,
    output_hbm,
    expand_hbm,
    reduce_hbm,
    x_out,
    query_out,
    totals_out,
    normed_t_out,
    mixed_t_out,
    final_out,
    grad_mid_out,
    small_out,
    wide_out,
    grads_out,
    query_weight,
    output,
    expand,
    reduce_weight,
    sems,
    packed,
    packed_grad,
    mask_ref,
    act_all,
    slope_all,
    mixed_ref,
    expand_acc,
    reduce_acc,
):
    meta = Meta(meta_ref, images)
    bin_now = pl.program_id(0)
    weights = Weights(
        (query_hbm, output_hbm, expand_hbm, reduce_hbm),
        (query_weight, output, expand, reduce_weight),
        sems,
    )
    weights.start()
    first_step((small_out, wide_out, expand_acc, reduce_acc))
    size, width = packed.shape
    pack_rows(meta, bin_now, place_ref, ((rows_ref, packed), (grads_ref, packed_grad)), size)
    mask_ref[...] = key_mask(meta, bin_now, "pick", size).astype(F32)
    part_of = quarter_rows(meta, width, parts)
    z = packed[...]
    x_out[...] = z.astype(BF16)
    unit_rows, _ = unit(z)
    normed = (unit_rows * gains[0:1, :] + shifts[0:1, :]).astype(BF16)
    normed_t_out[...] = dot_nt(part_of, normed).astype(BF16)
    weights.wait(0)
    query_out[...] = (dot(normed, query_weight[...]) + shifts[2:3, :]).astype(BF16)

    def store(cols, mixed):
        mixed_ref[:, cols] = mixed.astype(BF16)

    totals_out[...] = attend_forward(
        lambda cols: query_out[:, cols],
        lambda cols: pair_ref[:, cols],
        lambda cols: pair_ref[:, width + cols.start : width + cols.stop],
        mask_ref,
        store,
        size,
    )
    mixed = mixed_ref[...]
    mixed_t_out[...] = dot_nt(part_of, mixed).astype(BF16)
    weights.wait(1)
    branch = (dot(mixed, output[...]) + shifts[4:5, :]).astype(BF16).astype(F32)
    middle = z + scales[0:1, :] * branch
    unit_rows, inv_std = unit(middle)
    normed = (unit_rows * gains[2:3, :] + shifts[5:6, :]).astype(BF16)
    normed_part = dot_nt(part_of, normed).astype(BF16)
    weights.wait(2)
    weights.wait(3)
    part_width = expand.shape[1] // parts
    ffn = ffn_forward(normed, expand, wide_bias, reduce_weight, act_all, slope_all, part_width) + shifts[6:7, :]
    final_out[...] = middle + scales[1:2, :] * ffn
    grad_final = packed_grad[...]
    add_row(small_out, 0, rows_sum(grad_final * ffn))
    grad_low = (scales[1:2, :] * grad_final).astype(BF16)
    add_row(small_out, 1, rows_sum(grad_low.astype(F32)))
    act_part = act_all[:, pl.ds(pl.multiple_of(meta.band() * part_width, part_width), part_width)]
    reduce_acc[...] += dot_tn(act_part, grad_low)
    grad_normed = ffn_backward(
        grad_low, slope_all, normed_part, expand, reduce_weight, expand_acc, wide_out, part_width
    )
    add_row(small_out, 2, rows_sum(grad_normed * unit_rows))
    add_row(small_out, 3, rows_sum(grad_normed))
    grad_mid = grad_final + unit_back(grad_normed, unit_rows, inv_std, gains[2:3, :])
    grad_mid_out[...] = grad_mid
    add_row(small_out, 4, rows_sum(grad_mid * branch))

    def write():
        rows = reduce_acc.shape[0]
        grads_out[:rows, :] = reduce_acc[...].astype(BF16)
        part = expand_acc.shape[0]
        for i in range(expand_acc.shape[1] // width):
            grads_out[rows + i * part : rows + (i + 1) * part, :] = expand_acc[
                :, i * width : (i + 1) * width
            ].astype(BF16)

    last_step(meta, write)


def reg_attention_kernel(
    images,
    parts,
    meta_ref,
    z_ref,
    query_ref,
    totals_ref,
    normed_t_ref,
    mixed_t_ref,
    grad_mid_ref,
    pair_ref,
    pair_t_ref,
    x_ref,
    enc_branch_ref,
    enc_ffn_ref,
    gains,
    scales,
    enc_scales,
    query_hbm,
    keyval_hbm,
    output_hbm,
    query_grad_out,
    encoded_grad_out,
    small_out,
    grads_out,
    query_weight,
    keyval,
    output,
    sems,
    mask_ref,
    mixed_grad_ref,
    query_back,
    pair_back,
    query_acc,
    pair_acc,
    output_acc,
):
    meta = Meta(meta_ref, images)
    bin_now = pl.program_id(0)
    weights = Weights((output_hbm, query_hbm, keyval_hbm), (output, query_weight, keyval), sems)
    weights.start()
    first_step((small_out, query_acc, pair_acc, output_acc))
    size, width = mixed_grad_ref.shape
    mask_ref[...] = key_mask(meta, bin_now, "pick", size).astype(F32)
    grad_mid = grad_mid_ref[...]
    branch_grad = (scales[0:1, :] * grad_mid).astype(BF16)
    output_acc[...] += dot(mixed_t_ref[...], branch_grad)
    add_row(small_out, 0, rows_sum(branch_grad.astype(F32)))
    weights.wait(0)
    mixed_grad_ref[...] = dot_nt(branch_grad, output[...]).astype(BF16)

    def store(cols, grad_query, grad_key, grad_value):
        query_back[:, cols] = grad_query.astype(BF16)
        pair_back[:, cols] = grad_key.astype(BF16)
        pair_back[:, width + cols.start : width + cols.stop] = grad_value.astype(BF16)

    attend_backward(
        lambda cols: query_ref[:, cols],
        lambda cols: pair_ref[:, cols],
        lambda cols: pair_ref[:, width + cols.start : width + cols.stop],
        lambda cols: mixed_grad_ref[:, cols],
        totals_ref[...],
        mask_ref,
        store,
    )
    grad_query, grad_pair = query_back[...], pair_back[...]
    query_acc[...] += dot(normed_t_ref[...], grad_query)
    pair_acc[...] += dot(pair_t_ref[...], grad_pair)
    add_row(small_out, 1, rows_sum(grad_query.astype(F32)))
    add_row(small_out, 2, rows_sum(grad_pair[:, width:].astype(F32)))
    weights.wait(1)
    query_side = dot_nt(grad_query, query_weight[...]).astype(BF16).astype(F32)
    weights.wait(2)
    pair_side = dot_nt(grad_pair, keyval[...]).astype(BF16).astype(F32)
    unit_rows, inv_std = unit(z_ref[...].astype(F32))
    add_row(small_out, 3, rows_sum(query_side * unit_rows))
    add_row(small_out, 4, rows_sum(query_side))
    query_grad_out[...] = grad_mid + unit_back(query_side, unit_rows, inv_std, gains[0:1, :])
    encoded = (
        x_ref[...].astype(F32)
        + enc_scales[0:1, :] * enc_branch_ref[...].astype(F32)
        + enc_scales[1:2, :] * enc_ffn_ref[...]
    )
    unit_rows, inv_std = unit(encoded)
    add_row(small_out, 5, rows_sum(pair_side * unit_rows))
    add_row(small_out, 6, rows_sum(pair_side))
    encoded_grad_out[...] = unit_back(pair_side, unit_rows, inv_std, gains[1:2, :])

    def write():
        part = query_acc.shape[0]
        grads_out[:part, :] = query_acc[...].astype(BF16)
        grads_out[part : 2 * part, :] = pair_acc[:, :width].astype(BF16)
        grads_out[2 * part : 3 * part, :] = pair_acc[:, width:].astype(BF16)
        grads_out[3 * part :, :] = output_acc[...].astype(BF16)

    last_step(meta, write)


def enc_ffn_kernel(
    images,
    parts,
    meta_ref,
    encoded_grad_ref,
    x_ref,
    branch_ref,
    ffn_ref,
    act_ref,
    slope_ref,
    middle_t_ref,
    gains,
    scales,
    expand_hbm,
    reduce_hbm,
    grad_mid_out,
    small_out,
    wide_out,
    grads_out,
    expand,
    reduce_weight,
    sems,
    expand_acc,
    reduce_acc,
):
    meta = Meta(meta_ref, images)
    weights = Weights((reduce_hbm, expand_hbm), (reduce_weight, expand), sems)
    weights.start()
    first_step((small_out, wide_out, expand_acc, reduce_acc))
    width = x_ref.shape[1]
    encoded_grad = encoded_grad_ref[...]
    add_row(small_out, 0, rows_sum(encoded_grad * ffn_ref[...]))
    grad_low = (scales[1:2, :] * encoded_grad).astype(BF16)
    add_row(small_out, 1, rows_sum(grad_low.astype(F32)))
    reduce_acc[...] += dot_tn(act_ref[...], grad_low)
    weights.wait(0)
    weights.wait(1)
    part_width = expand.shape[1] // parts
    grad_normed = ffn_backward(
        grad_low, slope_ref, middle_t_ref[...], expand, reduce_weight, expand_acc, wide_out, part_width
    )
    branch = branch_ref[...].astype(F32)
    unit_rows, inv_std = unit(x_ref[...].astype(F32) + scales[0:1, :] * branch)
    add_row(small_out, 2, rows_sum(grad_normed * unit_rows))
    add_row(small_out, 3, rows_sum(grad_normed))
    grad_mid = encoded_grad + unit_back(grad_normed, unit_rows, inv_std, gains[1:2, :])
    grad_mid_out[...] = grad_mid
    add_row(small_out, 4, rows_sum(grad_mid * branch))

    def write():
        rows = reduce_acc.shape[0]
        grads_out[:rows, :] = reduce_acc[...].astype(BF16)
        part = expand_acc.shape[0]
        for i in range(expand_acc.shape[1] // width):
            grads_out[rows + i * part : rows + (i + 1) * part, :] = expand_acc[
                :, i * width : (i + 1) * width
            ].astype(BF16)

    last_step(meta, write)


def enc_attention_kernel(
    images,
    parts,
    meta_ref,
    grad_mid_ref,
    x_ref,
    triple_ref,
    totals_ref,
    normed_t_ref,
    mixed_t_ref,
    gains,
    scales,
    output_hbm,
    project_hbm,
    patch_grad_out,
    small_out,
    grads_out,
    output,
    project,
    sems,
    mask_ref,
    mixed_grad_ref,
    triple_back,
    project_acc,
    output_acc,
):
    meta = Meta(meta_ref, images)
    bin_now = pl.program_id(0)
    weights = Weights((output_hbm, project_hbm), (output, project), sems)
    weights.start()
    first_step((small_out, project_acc, output_acc))
    size, width = mixed_grad_ref.shape
    mask_ref[...] = key_mask(meta, bin_now, "keep", size).astype(F32)
    grad_mid = grad_mid_ref[...]
    branch_grad = (scales[0:1, :] * grad_mid).astype(BF16)
    output_acc[...] += dot(mixed_t_ref[...], branch_grad)
    add_row(small_out, 0, rows_sum(branch_grad.astype(F32)))
    weights.wait(0)
    mixed_grad_ref[...] = dot_nt(branch_grad, output[...]).astype(BF16)

    def store(cols, grad_query, grad_key, grad_value):
        triple_back[:, cols] = grad_query.astype(BF16)
        triple_back[:, width + cols.start : width + cols.stop] = grad_key.astype(BF16)
        triple_back[:, 2 * width + cols.start : 2 * width + cols.stop] = grad_value.astype(BF16)

    attend_backward(
        lambda cols: triple_ref[:, cols],
        lambda cols: triple_ref[:, width + cols.start : width + cols.stop],
        lambda cols: triple_ref[:, 2 * width + cols.start : 2 * width + cols.stop],
        lambda cols: mixed_grad_ref[:, cols],
        totals_ref[...],
        mask_ref,
        store,
    )
    back = triple_back[...]
    project_acc[...] += dot(normed_t_ref[...], back)
    add_row(small_out, 1, rows_sum(back[:, :width].astype(F32)))
    add_row(small_out, 2, rows_sum(back[:, 2 * width :].astype(F32)))
    weights.wait(1)
    rows_grad = dot_nt(back, project[...]).astype(BF16).astype(F32)
    unit_rows, inv_std = unit(x_ref[...].astype(F32))
    add_row(small_out, 3, rows_sum(rows_grad * unit_rows))
    add_row(small_out, 4, rows_sum(rows_grad))
    patch_grad_out[...] = grad_mid + unit_back(rows_grad, unit_rows, inv_std, gains[0:1, :])

    def write():
        part = output_acc.shape[0]
        grads_out[:part, :] = output_acc[...].astype(BF16)
        for i in range(3):
            grads_out[(i + 1) * part : (i + 2) * part, :] = project_acc[
                :, i * width : (i + 1) * width
            ].astype(BF16)

    last_step(meta, write)


def unpack_kernel(meta_ref, keep_place, pick_place, final_ref, query_grad_ref, patch_grad_ref, final_out, query_grad_out, patch_grad_out):
    rows = keep_place.shape[0]
    size = final_ref.shape[0]
    lane = lax.broadcasted_iota(jnp.int32, (rows, size), 1)
    kept = (keep_place[...] == lane).astype(BF16)
    picked = (pick_place[...] == lane).astype(BF16)
    for chosen, source, target in (
        (picked, final_ref, final_out),
        (picked, query_grad_ref, query_grad_out),
        (kept, patch_grad_ref, patch_grad_out),
    ):
        values = source[...]
        high = values.astype(BF16)
        rest = (values - high.astype(F32)).astype(BF16)
        target[...] = dot(chosen, high) + dot(chosen, rest)


def whole(array):
    return pl.BlockSpec(array.shape, lambda *_: (0,) * array.ndim)


def by_bin(shape):
    return pl.BlockSpec((None,) + tuple(shape), lambda b, meta: (jnp.minimum(b, meta[0] - 1), 0, 0))


def for_used_bins(kernel):
    def guarded(meta_ref, *refs):
        @pl.when(pl.program_id(0) < meta_ref[0])
        def _():
            kernel(meta_ref, *refs)

    return guarded


IN_HBM = pl.BlockSpec(memory_space=pl.ANY)


def binned_call(kernel, name, images, meta, binned, full, hbm, binned_outs, full_outs, scratch, flops):
    operands = [meta] + [a for _, a in binned] + list(hbm)
    in_specs = [whole(a) if kind == "full" else by_bin(a.shape[1:]) for kind, a in binned]
    in_specs += [IN_HBM] * len(hbm)
    out_shape = [jax.ShapeDtypeStruct((images,) + s, t) for s, t in binned_outs]
    out_shape += [jax.ShapeDtypeStruct(s, t) for s, t in full_outs]
    out_specs = [by_bin(s) for s, _ in binned_outs]
    out_specs += [pl.BlockSpec(s, lambda *_: (0, 0)) for s, _ in full_outs]
    return pl.pallas_call(
        for_used_bins(kernel),
        name=name,
        out_shape=out_shape,
        grid_spec=pltpu.PrefetchScalarGridSpec(
            num_scalar_prefetch=1,
            grid=(images,),
            in_specs=in_specs,
            out_specs=out_specs,
            scratch_shapes=scratch,
        ),
        compiler_params=pltpu.CompilerParams(
            vmem_limit_bytes=VMEM_LIMIT, dimension_semantics=("arbitrary",)
        ),
        cost_estimate=pl.CostEstimate(flops=flops, bytes_accessed=20_000_000, transcendentals=0),
    )(*operands)


def body(
    batch_size,
    patches,
    queries,
    cotangent,
    counts,
    masked,
    enc_gains,
    enc_shifts,
    enc_widebias,
    enc_scales,
    enc_project,
    enc_output,
    enc_expand,
    enc_reduce,
    reg_gains,
    reg_shifts,
    reg_widebias,
    reg_scales,
    reg_query,
    reg_keyval,
    reg_output,
    reg_expand,
    reg_reduce,
):
    images, band_rows, width = patches.shape
    hidden = enc_expand.shape[1]
    band = lax.axis_index("band")
    masked_all = lax.all_gather(masked.astype(F32), "band", axis=1, tiled=True)
    size = masked_all.shape[1]
    parts = size // band_rows
    part, part_hidden = width // parts, hidden // parts
    patch_rows = lax.all_gather(patches, "band", axis=0)
    query_rows = lax.all_gather(queries, "band", axis=0)
    grad_rows = lax.all_gather(cotangent, "band", axis=0)

    real = lax.broadcasted_iota(jnp.int32, (images, size), 1) < counts[:, None]
    keep = jnp.where(real & (masked_all == 0), 1.0, 0.0).astype(F32)
    pick = jnp.where(real & (masked_all == 1), 1.0, 0.0).astype(F32)
    in_smem = pl.BlockSpec(memory_space=pltpu.SMEM)
    in_vmem = pl.BlockSpec(memory_space=pltpu.VMEM)
    meta, keep_place, pick_place = pl.pallas_call(
        functools.partial(plan_kernel, images),
        name="plan",
        out_shape=[
            jax.ShapeDtypeStruct((2 + 5 * images,), jnp.int32),
            jax.ShapeDtypeStruct((images, size), jnp.int32),
            jax.ShapeDtypeStruct((images, size), jnp.int32),
        ],
        in_specs=[in_smem, in_smem, in_vmem, in_vmem],
        out_specs=[in_smem, in_vmem, in_vmem],
        scratch_shapes=[pltpu.SMEM((5, images), jnp.int32)],
    )(counts, band.astype(jnp.int32).reshape(1), keep, pick)

    def both(*arrays):
        return [("full", a) for a in arrays]

    def cut(*arrays):
        return [("bin", a) for a in arrays]

    def vm(shape, dtype=BF16):
        return pltpu.VMEM(shape, dtype)

    enc_wide = enc_widebias.reshape(1, hidden)
    reg_wide = reg_widebias.reshape(1, hidden)
    (
        x,
        triple,
        enc_totals,
        enc_normed_t,
        enc_mixed_t,
        enc_branch,
        enc_act,
        enc_slope,
        enc_middle_t,
        enc_ffn,
        pair_t,
        pair,
    ) = binned_call(
        functools.partial(enc_forward_kernel, images, parts),
        "enc_forward",
        images,
        meta,
        both(keep_place, patch_rows, enc_gains, enc_shifts, enc_wide, enc_scales, reg_gains, reg_shifts),
        None,
        (enc_project, enc_output, enc_expand, enc_reduce, reg_keyval),
        [
            ((size, width), BF16),
            ((size, 3 * width), BF16),
            ((size, LANES), F32),
            ((part, size), BF16),
            ((part, size), BF16),
            ((size, width), BF16),
            ((size, part_hidden), BF16),
            ((size, hidden), BF16),
            ((part, size), BF16),
            ((size, width), F32),
            ((part, size), BF16),
            ((size, 2 * width), BF16),
        ],
        [],
        [
            vm(enc_project.shape),
            vm(enc_output.shape),
            vm(enc_expand.shape),
            vm(enc_reduce.shape),
            vm(reg_keyval.shape),
            pltpu.SemaphoreType.DMA((5,)),
            vm((size, width), F32),
            vm((size, size), F32),
            vm((size, hidden)),
            vm((size, width)),
        ],
        8_000_000_000,
    )
    small_rows = 8
    (
        z,
        reg_query_low,
        reg_totals,
        reg_normed_t,
        reg_mixed_t,
        final_rows,
        reg_grad_mid,
        reg_small,
        reg_wide_sum,
        reg_ffn_grads,
    ) = binned_call(
        functools.partial(reg_forward_kernel, images, parts),
        "reg_forward",
        images,
        meta,
        both(pick_place, query_rows, grad_rows)
        + cut(pair)
        + both(reg_gains, reg_shifts, reg_wide, reg_scales),
        None,
        (reg_query, reg_output, reg_expand, reg_reduce),
        [
            ((size, width), BF16),
            ((size, width), BF16),
            ((size, LANES), F32),
            ((part, size), BF16),
            ((part, size), BF16),
            ((size, width), F32),
            ((size, width), F32),
        ],
        [
            ((small_rows, width), F32),
            ((small_rows, hidden), F32),
            ((part_hidden + hidden // width * part, width), BF16),
        ],
        [
            vm(reg_query.shape),
            vm(reg_output.shape),
            vm(reg_expand.shape),
            vm(reg_reduce.shape),
            pltpu.SemaphoreType.DMA((4,)),
            vm((size, width), F32),
            vm((size, width), F32),
            vm((size, size), F32),
            vm((size, hidden)),
            vm((size, hidden)),
            vm((size, width)),
            vm((part, hidden), F32),
            vm((part_hidden, width), F32),
        ],
        8_000_000_000,
    )
    query_grad, encoded_grad, reg_attn_small, reg_attn_grads = binned_call(
        functools.partial(reg_attention_kernel, images, parts),
        "reg_attention_grad",
        images,
        meta,
        cut(z, reg_query_low, reg_totals, reg_normed_t, reg_mixed_t, reg_grad_mid, pair, pair_t, x, enc_branch, enc_ffn)
        + both(reg_gains, reg_scales, enc_scales),
        None,
        (reg_query, reg_keyval, reg_output),
        [((size, width), F32), ((size, width), F32)],
        [((small_rows, width), F32), ((4 * part, width), BF16)],
        [
            vm(reg_query.shape),
            vm(reg_keyval.shape),
            vm(reg_output.shape),
            pltpu.SemaphoreType.DMA((3,)),
            vm((size, size), F32),
            vm((size, width)),
            vm((size, width)),
            vm((size, 2 * width)),
            vm((part, width), F32),
            vm((part, 2 * width), F32),
            vm((part, width), F32),
        ],
        6_000_000_000,
    )
    enc_grad_mid, enc_small, enc_wide_sum, enc_ffn_grads = binned_call(
        functools.partial(enc_ffn_kernel, images, parts),
        "enc_ffn_grad",
        images,
        meta,
        cut(encoded_grad, x, enc_branch, enc_ffn, enc_act, enc_slope, enc_middle_t)
        + both(enc_gains, enc_scales),
        None,
        (enc_expand, enc_reduce),
        [((size, width), F32)],
        [
            ((small_rows, width), F32),
            ((small_rows, hidden), F32),
            ((part_hidden + hidden // width * part, width), BF16),
        ],
        [
            vm(enc_expand.shape),
            vm(enc_reduce.shape),
            pltpu.SemaphoreType.DMA((2,)),
            vm((part, hidden), F32),
            vm((part_hidden, width), F32),
        ],
        6_000_000_000,
    )
    patch_grad, enc_attn_small, enc_attn_grads = binned_call(
        functools.partial(enc_attention_kernel, images, parts),
        "enc_attention_grad",
        images,
        meta,
        cut(enc_grad_mid, x, triple, enc_totals, enc_normed_t, enc_mixed_t) + both(enc_gains, enc_scales),
        None,
        (enc_output, enc_project),
        [((size, width), F32)],
        [((small_rows, width), F32), ((4 * part, width), BF16)],
        [
            vm(enc_output.shape),
            vm(enc_project.shape),
            pltpu.SemaphoreType.DMA((2,)),
            vm((size, size), F32),
            vm((size, width)),
            vm((size, 3 * width)),
            vm((part, 3 * width), F32),
            vm((part, width), F32),
        ],
        6_000_000_000,
    )

    def own_places(places):
        mine = lax.dynamic_slice_in_dim(places, band * band_rows, band_rows, 1)
        return mine[:, :, None]

    by_image = pl.BlockSpec((None, band_rows, 1), lambda i, m: (i, 0, 0))
    bin_of_image = pl.BlockSpec((None, size, width), lambda i, m: (m[2 + i], 0, 0))
    image_out = pl.BlockSpec((None, band_rows, width), lambda i, m: (i, 0, 0))
    prediction, query_grad, patch_grad = pl.pallas_call(
        unpack_kernel,
        name="unpack",
        out_shape=[jax.ShapeDtypeStruct(patches.shape, F32)] * 3,
        grid_spec=pltpu.PrefetchScalarGridSpec(
            num_scalar_prefetch=1,
            grid=(images,),
            in_specs=[by_image, by_image, bin_of_image, bin_of_image, bin_of_image],
            out_specs=[image_out] * 3,
        ),
        compiler_params=pltpu.CompilerParams(vmem_limit_bytes=VMEM_LIMIT),
        cost_estimate=pl.CostEstimate(flops=2_000_000_000, bytes_accessed=20_000_000, transcendentals=0),
    )(meta, own_places(keep_place), own_places(pick_place), final_rows, query_grad, patch_grad)

    def reduce_batch(grads):
        return lax.psum(grads, "batch").astype(F32)

    def side_by_side(rows, pieces):
        return jnp.concatenate(jnp.split(rows, pieces, 0), 1)

    wide_pieces = hidden // width
    reg_ffn_grads = reduce_batch(reg_ffn_grads)
    reg_attn_grads = reduce_batch(reg_attn_grads)
    enc_ffn_grads = reduce_batch(enc_ffn_grads)
    enc_attn_grads = reduce_batch(enc_attn_grads)
    reg_reduce_grad = reg_ffn_grads[:part_hidden]
    reg_expand_grad = side_by_side(reg_ffn_grads[part_hidden:], wide_pieces)
    reg_query_grad = reg_attn_grads[:part]
    reg_keyval_grad = side_by_side(reg_attn_grads[part : 3 * part], 2)
    reg_output_grad = reg_attn_grads[3 * part :]
    enc_reduce_grad = enc_ffn_grads[:part_hidden]
    enc_expand_grad = side_by_side(enc_ffn_grads[part_hidden:], wide_pieces)
    enc_output_grad = enc_attn_grads[:part]
    enc_project_grad = side_by_side(enc_attn_grads[part:], 3)

    small = jnp.concatenate([reg_small, reg_attn_small, enc_small, enc_attn_small], 0)
    small = lax.dynamic_slice_in_dim(small, band * part, part, 1)
    wide = jnp.concatenate([reg_wide_sum[:1], enc_wide_sum[:1]], 0)
    wide = lax.dynamic_slice_in_dim(wide, band * part_hidden, part_hidden, 1)
    small, wide = lax.psum((small, wide), "batch")
    reg_s, reg_a, enc_s, enc_a = jnp.split(small, 4, 0)
    enc_gains_grad = jnp.stack([enc_a[3], enc_s[2]])
    enc_shifts_grad = jnp.stack([enc_a[4], enc_a[1], enc_a[2], enc_a[0], enc_s[3], enc_s[1]])
    enc_scales_grad = jnp.stack([enc_s[4], enc_s[0]])
    reg_gains_grad = jnp.stack([reg_a[3], reg_a[5], reg_s[2]])
    reg_shifts_grad = jnp.stack(
        [reg_a[4], reg_a[6], reg_a[1], reg_a[2], reg_a[0], reg_s[3], reg_s[1]]
    )
    reg_scales_grad = jnp.stack([reg_s[4], reg_s[0]])
    return (
        prediction,
        patch_grad,
        query_grad,
        enc_gains_grad,
        enc_shifts_grad,
        wide[1],
        enc_scales_grad,
        enc_project_grad,
        enc_output_grad,
        enc_expand_grad,
        enc_reduce_grad,
        reg_gains_grad,
        reg_shifts_grad,
        wide[0],
        reg_scales_grad,
        reg_query_grad,
        reg_keyval_grad,
        reg_output_grad,
        reg_expand_grad,
        reg_reduce_grad,
    )


def solution(mesh):
    token = P("batch", "band", None)
    in_specs = (token, token, token, P("batch"), P("batch", "band")) + (P(),) * 17
    by_row, by_col = P("band", None), P(None, "band")
    out_specs = (
        token,
        token,
        token,
        by_col,
        by_col,
        P("band"),
        by_col,
        by_row,
        by_row,
        by_row,
        by_row,
        by_col,
        by_col,
        P("band"),
        by_col,
        by_row,
        by_row,
        by_row,
        by_row,
        by_row,
    )
    return jax.shard_map(
        functools.partial(body, mesh.shape["batch"]),
        mesh=mesh,
        in_specs=in_specs,
        out_specs=out_specs,
        check_vma=False,
    )
```

```python
import functools

import jax
import jax.numpy as jnp
from jax import lax
from jax.experimental import pallas as pl
from jax.experimental.pallas import tpu as pltpu
from jax.sharding import PartitionSpec as P

HEADS = 12
HD = 64
EPS = 1e-06
ROOT_HALF = 0.7071067811865476
INV_ROOT_TAU = 0.3989422804014327
NEG_LARGE = -1e30
F32 = jnp.float32
BF16 = jnp.bfloat16
VMEM_LIMIT = 56 * 1024 * 1024
STEP_LIMIT = 16 * 1024 * 1024
LANES = 128
HEAD = 3


def dot(a, b):
    return lax.dot_general(a, b, (((1,), (0,)), ((), ())), preferred_element_type=F32)


def dot_nt(a, b):
    return lax.dot_general(a, b, (((1,), (1,)), ((), ())), preferred_element_type=F32)


def dot_tn(a, b):
    return lax.dot_general(a, b, (((0,), (0,)), ((), ())), preferred_element_type=F32)


def unit(values):
    row_mean = jnp.mean(values, -1, keepdims=True)
    centred = values - row_mean
    variance = jnp.mean(centred * centred, -1, keepdims=True)
    inv_std = lax.rsqrt(variance + EPS)
    return centred * inv_std, inv_std


def unit_back(grad_out, unit_rows, inv_std, gain):
    scaled = grad_out * gain
    first_term = jnp.mean(scaled, -1, keepdims=True)
    second_term = jnp.mean(scaled * unit_rows, -1, keepdims=True)
    return inv_std * (scaled - first_term - unit_rows * second_term)


def rows_sum(values):
    return jnp.sum(values, 0, keepdims=True)


def gate_and_slope(pre_act):
    bell = 0.5 * (1.0 + lax.erf(pre_act * ROOT_HALF))
    slope = bell + pre_act * INV_ROOT_TAU * jnp.exp(-0.5 * pre_act * pre_act)
    return (pre_act * bell).astype(BF16), slope.astype(BF16)


class Meta:
    def __init__(self, ref, images):
        self.ref, self.images = ref, images

    def bins(self):
        return self.ref[0]

    def band(self):
        return self.ref[1]

    def side(self):
        return self.ref[2]

    def bin_of(self, image):
        return self.ref[HEAD + image]

    def keep_off(self, image):
        return self.ref[HEAD + self.images + image]

    def keep_count(self, image):
        return self.ref[HEAD + 2 * self.images + image]

    def pick_off(self, image):
        return self.ref[HEAD + 3 * self.images + image]

    def pick_count(self, image):
        return self.ref[HEAD + 4 * self.images + image]

    def segments(self, bin_now, kind, shape, dim, blank):
        rows = lax.broadcasted_iota(jnp.int32, shape, dim)
        owner = jnp.full(shape, blank, jnp.int32)
        for image in range(self.images):
            start = self.keep_off(image) if kind == "keep" else self.pick_off(image)
            count = self.keep_count(image) if kind == "keep" else self.pick_count(image)
            stop = start + jnp.where(self.bin_of(image) == bin_now, count, 0)
            owner = jnp.where((rows >= start) & (rows < stop), image, owner)
        return owner


def key_mask(meta, bin_now, query_kind, size):
    query_owner = meta.segments(bin_now, query_kind, (size, 1), 0, -2)
    key_owner = meta.segments(bin_now, "keep", (1, size), 1, -1)
    return query_owner == key_owner


def quarter_rows(meta, width, parts):
    part = width // parts
    row = lax.broadcasted_iota(jnp.int32, (part, width), 0) + meta.band() * part
    return (row == lax.broadcasted_iota(jnp.int32, (part, width), 1)).astype(BF16)


def lower_half():
    return lax.broadcasted_iota(jnp.int32, (1, LANES), 1) < HD


def attend_forward(query_of, key_of, value_of, mask_ref, store, size):
    low = lower_half()
    sides = (low.astype(BF16), (~low).astype(BF16))
    lane = lax.broadcasted_iota(jnp.int32, (size, LANES), 1)
    totals = jnp.zeros((size, LANES), F32)
    for pair in range(HEADS // 2):
        cols = slice(pair * LANES, (pair + 1) * LANES)
        query, key, value = query_of(cols), key_of(cols), value_of(cols)
        mixed = []
        for side in range(2):
            scores = dot_nt(query, key * sides[side]) * HD ** (-0.5)
            scores = jnp.where(mask_ref[...] > 0, scores, NEG_LARGE)
            row_top = jnp.max(scores, -1, keepdims=True)
            exp_scores = jnp.exp(scores - row_top)
            row_total = jnp.sum(exp_scores, -1, keepdims=True)
            weights = (exp_scores * (1.0 / row_total)).astype(BF16)
            totals = jnp.where(lane == 2 * pair + side, row_top + jnp.log(row_total), totals)
            mixed.append(dot(weights, value))
        store(cols, jnp.where(low, mixed[0], mixed[1]))
    return totals


def attend_backward(query_of, key_of, value_of, grad_of, totals, mask_ref, store):
    low = lower_half()
    sides = (low.astype(BF16), (~low).astype(BF16))
    for pair in range(HEADS // 2):
        cols = slice(pair * LANES, (pair + 1) * LANES)
        query, key, value, grad = query_of(cols), key_of(cols), value_of(cols), grad_of(cols)
        grad_query, grad_key, grad_value = [], [], []
        for side in range(2):
            head = 2 * pair + side
            scores = dot_nt(query, key * sides[side]) * HD ** (-0.5)
            scores = jnp.where(mask_ref[...] > 0, scores, NEG_LARGE)
            probs = jnp.exp(scores - totals[:, head : head + 1])
            grad_value.append(dot_tn(probs.astype(BF16), grad))
            grad_probs = dot_nt(grad, value * sides[side])
            inner = jnp.sum(grad_probs * probs, -1, keepdims=True)
            grad_scores = (probs * (grad_probs - inner)).astype(BF16)
            grad_query.append(dot(grad_scores, key))
            grad_key.append(dot_tn(grad_scores, query))
        store(
            cols,
            jnp.where(low, grad_query[0], grad_query[1]) * HD ** (-0.5),
            jnp.where(low, grad_key[0], grad_key[1]) * HD ** (-0.5),
            jnp.where(low, grad_value[0], grad_value[1]),
        )


def pack_rows(meta, bin_now, place_ref, sources, size):
    for _, packed in sources:
        packed[...] = jnp.zeros_like(packed)
    for image in range(meta.images):

        @pl.when(meta.bin_of(image) == bin_now)
        def _():
            row = lax.broadcasted_iota(jnp.int32, (size, size), 0)
            chosen = (row == place_ref[image : image + 1, :]).astype(BF16)
            for gathered, packed in sources:
                rows = jnp.concatenate(
                    [gathered[band, image] for band in range(gathered.shape[0])], 0
                )
                packed[...] += dot(chosen, rows)


class Weights:
    def __init__(self, sources, targets, sems):
        self.copies = [
            pltpu.make_async_copy(source, target, sems.at[i])
            for i, (source, target) in enumerate(zip(sources, targets, strict=True))
        ]

    def start(self):
        @pl.when(pl.program_id(0) == 0)
        def _():
            for copy in self.copies:
                copy.start()

    def wait(self, index):
        @pl.when(pl.program_id(0) == 0)
        def _():
            self.copies[index].wait()


def add_row(small_ref, row, values):
    small_ref[row : row + 1, :] += values


def first_step(refs):
    @pl.when(pl.program_id(0) == 0)
    def _():
        for ref in refs:
            ref[...] = jnp.zeros_like(ref)


def write_halves(meta, keep_out, send_out, write_first, write_second):
    @pl.when(meta.side() == 0)
    def _():
        write_first(keep_out)
        write_second(send_out)

    @pl.when(meta.side() == 1)
    def _():
        write_first(send_out)
        write_second(keep_out)


def write_blocks(target, acc, start, stop, width, at=0):
    part = acc.shape[0]
    for i in range(start, stop):
        row = at + (i - start) * part
        target[row : row + part, :] = acc[:, i * width : (i + 1) * width].astype(BF16)


def last_step(meta, write):
    @pl.when(pl.program_id(0) == meta.bins() - 1)
    def _():
        write()


def plan_kernel(images, counts_ref, band_ref, keep_ref, pick_ref, meta_ref, keep_place_ref, pick_place_ref, words):
    size = keep_ref.shape[1]
    before = (
        lax.broadcasted_iota(jnp.int32, (size, size), 0)
        <= lax.broadcasted_iota(jnp.int32, (size, size), 1)
    ).astype(BF16)
    keep, pick = keep_ref[...], pick_ref[...]
    keep_rank = dot(keep.astype(BF16), before).astype(jnp.int32) - 1
    pick_rank = dot(pick.astype(BF16), before).astype(jnp.int32) - 1
    for image in range(images):
        words[0, image] = jnp.sum(keep[image : image + 1, :]).astype(jnp.int32)
        words[1, image] = jnp.sum(pick[image : image + 1, :]).astype(jnp.int32)
        for row in (2, 3, 4):
            words[row, image] = 0

    def place(_, bins):
        def largest(image, best):
            open_now = words[4, image] == 0
            better = open_now & ((best < 0) | (counts_ref[image] > counts_ref[jnp.maximum(best, 0)]))
            return jnp.where(better, image, best)

        image = lax.fori_loop(0, images, largest, jnp.int32(-1))
        keep_count, pick_count = words[0, image], words[1, image]

        def first_fit(step, best):
            bin_now = images - 1 - step
            fits = (words[2, bin_now] + keep_count <= size) & (words[3, bin_now] + pick_count <= size)
            return jnp.where(fits, bin_now, best)

        bin_now = lax.fori_loop(0, images, first_fit, jnp.int32(0))
        meta_ref[HEAD + image] = bin_now
        meta_ref[HEAD + images + image] = words[2, bin_now]
        meta_ref[HEAD + 2 * images + image] = keep_count
        meta_ref[HEAD + 3 * images + image] = words[3, bin_now]
        meta_ref[HEAD + 4 * images + image] = pick_count
        words[2, bin_now] = words[2, bin_now] + keep_count
        words[3, bin_now] = words[3, bin_now] + pick_count
        words[4, image] = 1
        return jnp.maximum(bins, bin_now + 1)

    meta_ref[0] = lax.fori_loop(0, images, place, jnp.int32(0))
    meta_ref[1] = band_ref[0]
    meta_ref[2] = band_ref[1]
    for image in range(images):
        row = slice(image, image + 1)
        keep_place_ref[row, :] = jnp.where(
            keep[row, :] > 0, keep_rank[row, :] + meta_ref[HEAD + images + image], -1
        )
        pick_place_ref[row, :] = jnp.where(
            pick[row, :] > 0, pick_rank[row, :] + meta_ref[HEAD + 3 * images + image], -1
        )


def ffn_forward(normed, expand, wide_bias, reduce_weight, act_ref, slope_ref, width):
    total = None
    for start in range(0, expand.shape[1], width):
        cols = slice(start, start + width)
        act, slope = gate_and_slope(dot(normed, expand[:, cols]) + wide_bias[:, cols])
        act_ref[:, cols] = act
        slope_ref[:, cols] = slope
        part = dot(act, reduce_weight[cols, :])
        total = part if total is None else total + part
    return total


def ffn_backward(grad_low, slope_ref, normed_part, expand, reduce_weight, expand_acc, wide_ref, width):
    total = None
    for start in range(0, expand.shape[1], width):
        cols = slice(start, start + width)
        grad_act = dot_nt(grad_low, reduce_weight[cols, :])
        grad_pre = grad_act * slope_ref[:, cols].astype(F32)
        grad_pre_low = grad_pre.astype(BF16)
        wide_ref[0:1, cols] += rows_sum(grad_pre_low.astype(F32))
        expand_acc[:, cols] += dot(normed_part, grad_pre_low)
        part = dot_nt(grad_pre_low, expand[:, cols])
        total = part if total is None else total + part
    return total


def enc_forward_kernel(
    images,
    parts,
    meta_ref,
    place_ref,
    rows_ref,
    gains,
    shifts,
    wide_bias,
    scales,
    reg_gains,
    reg_shifts,
    project_hbm,
    output_hbm,
    expand_hbm,
    reduce_hbm,
    keyval_hbm,
    x_out,
    triple_out,
    totals_out,
    normed_t_out,
    mixed_t_out,
    branch_out,
    act_out,
    slope_out,
    middle_t_out,
    ffn_out,
    pair_t_out,
    pair_out,
    project,
    output,
    expand,
    reduce_weight,
    keyval,
    sems,
    packed,
    mask_ref,
    act_all,
    mixed_ref,
):
    meta = Meta(meta_ref, images)
    bin_now = pl.program_id(0)
    weights = Weights(
        (project_hbm, output_hbm, expand_hbm, reduce_hbm, keyval_hbm),
        (project, output, expand, reduce_weight, keyval),
        sems,
    )
    weights.start()
    size, width = packed.shape
    pack_rows(meta, bin_now, place_ref, ((rows_ref, packed),), size)
    mask_ref[...] = key_mask(meta, bin_now, "keep", size).astype(F32)
    part_of = quarter_rows(meta, width, parts)
    x = packed[...]
    x_out[...] = x.astype(BF16)
    unit_rows, _ = unit(x)
    normed = (unit_rows * gains[0:1, :] + shifts[0:1, :]).astype(BF16)
    normed_t_out[...] = dot_nt(part_of, normed).astype(BF16)
    weights.wait(0)
    triple_out[:, :width] = (dot(normed, project[:, :width]) + shifts[1:2, :]).astype(BF16)
    triple_out[:, width : 2 * width] = dot(normed, project[:, width : 2 * width]).astype(BF16)
    triple_out[:, 2 * width :] = (dot(normed, project[:, 2 * width :]) + shifts[2:3, :]).astype(BF16)

    def store(cols, mixed):
        mixed_ref[:, cols] = mixed.astype(BF16)

    totals_out[...] = attend_forward(
        lambda cols: triple_out[:, cols],
        lambda cols: triple_out[:, width + cols.start : width + cols.stop],
        lambda cols: triple_out[:, 2 * width + cols.start : 2 * width + cols.stop],
        mask_ref,
        store,
        size,
    )
    mixed = mixed_ref[...]
    mixed_t_out[...] = dot_nt(part_of, mixed).astype(BF16)
    weights.wait(1)
    branch = (dot(mixed, output[...]) + shifts[3:4, :]).astype(BF16)
    branch_out[...] = branch
    middle = x + scales[0:1, :] * branch.astype(F32)
    unit_rows, _ = unit(middle)
    normed = (unit_rows * gains[1:2, :] + shifts[4:5, :]).astype(BF16)
    middle_t_out[...] = dot_nt(part_of, normed).astype(BF16)
    weights.wait(2)
    weights.wait(3)
    part_width = expand.shape[1] // parts
    ffn = ffn_forward(normed, expand, wide_bias, reduce_weight, act_all, slope_out, part_width) + shifts[5:6, :]
    act_out[...] = act_all[:, pl.ds(pl.multiple_of(meta.band() * part_width, part_width), part_width)]
    ffn_out[...] = ffn
    encoded = middle + scales[1:2, :] * ffn
    unit_rows, _ = unit(encoded)
    pair_normed = (unit_rows * reg_gains[1:2, :] + reg_shifts[1:2, :]).astype(BF16)
    pair_t_out[...] = dot_nt(part_of, pair_normed).astype(BF16)
    weights.wait(4)
    pair_out[:, :width] = dot(pair_normed, keyval[:, :width]).astype(BF16)
    pair_out[:, width:] = (dot(pair_normed, keyval[:, width:]) + reg_shifts[3:4, :]).astype(BF16)


def reg_forward_kernel(
    images,
    parts,
    meta_ref,
    place_ref,
    rows_ref,
    grads_ref,
    pair_ref,
    gains,
    shifts,
    wide_bias,
    scales,
    query_hbm,
    output_hbm,
    expand_hbm,
    reduce_hbm,
    x_out,
    query_out,
    totals_out,
    normed_t_out,
    mixed_t_out,
    final_out,
    grad_mid_out,
    small_out,
    wide_out,
    keep_out,
    send_out,
    query_weight,
    output,
    expand,
    reduce_weight,
    sems,
    packed,
    packed_grad,
    mask_ref,
    act_all,
    slope_all,
    mixed_ref,
    expand_acc,
    reduce_acc,
):
    meta = Meta(meta_ref, images)
    bin_now = pl.program_id(0)
    weights = Weights(
        (query_hbm, output_hbm, expand_hbm, reduce_hbm),
        (query_weight, output, expand, reduce_weight),
        sems,
    )
    weights.start()
    first_step((small_out, wide_out, expand_acc, reduce_acc))
    size, width = packed.shape
    pack_rows(meta, bin_now, place_ref, ((rows_ref, packed), (grads_ref, packed_grad)), size)
    mask_ref[...] = key_mask(meta, bin_now, "pick", size).astype(F32)
    part_of = quarter_rows(meta, width, parts)
    z = packed[...]
    x_out[...] = z.astype(BF16)
    unit_rows, _ = unit(z)
    normed = (unit_rows * gains[0:1, :] + shifts[0:1, :]).astype(BF16)
    normed_t_out[...] = dot_nt(part_of, normed).astype(BF16)
    weights.wait(0)
    query_out[...] = (dot(normed, query_weight[...]) + shifts[2:3, :]).astype(BF16)

    def store(cols, mixed):
        mixed_ref[:, cols] = mixed.astype(BF16)

    totals_out[...] = attend_forward(
        lambda cols: query_out[:, cols],
        lambda cols: pair_ref[:, cols],
        lambda cols: pair_ref[:, width + cols.start : width + cols.stop],
        mask_ref,
        store,
        size,
    )
    mixed = mixed_ref[...]
    mixed_t_out[...] = dot_nt(part_of, mixed).astype(BF16)
    weights.wait(1)
    branch = (dot(mixed, output[...]) + shifts[4:5, :]).astype(BF16).astype(F32)
    middle = z + scales[0:1, :] * branch
    unit_rows, inv_std = unit(middle)
    normed = (unit_rows * gains[2:3, :] + shifts[5:6, :]).astype(BF16)
    normed_part = dot_nt(part_of, normed).astype(BF16)
    weights.wait(2)
    weights.wait(3)
    part_width = expand.shape[1] // parts
    ffn = ffn_forward(normed, expand, wide_bias, reduce_weight, act_all, slope_all, part_width) + shifts[6:7, :]
    final_out[...] = middle + scales[1:2, :] * ffn
    grad_final = packed_grad[...]
    add_row(small_out, 0, rows_sum(grad_final * ffn))
    grad_low = (scales[1:2, :] * grad_final).astype(BF16)
    add_row(small_out, 1, rows_sum(grad_low.astype(F32)))
    act_part = act_all[:, pl.ds(pl.multiple_of(meta.band() * part_width, part_width), part_width)]
    reduce_acc[...] += dot_tn(act_part, grad_low)
    grad_normed = ffn_backward(
        grad_low, slope_all, normed_part, expand, reduce_weight, expand_acc, wide_out, part_width
    )
    add_row(small_out, 2, rows_sum(grad_normed * unit_rows))
    add_row(small_out, 3, rows_sum(grad_normed))
    grad_mid = grad_final + unit_back(grad_normed, unit_rows, inv_std, gains[2:3, :])
    grad_mid_out[...] = grad_mid
    add_row(small_out, 4, rows_sum(grad_mid * branch))

    last_step(
        meta,
        lambda: write_halves(
            meta,
            keep_out,
            send_out,
            lambda out: write_blocks(out, reduce_acc, 0, 1, width),
            lambda out: write_blocks(out, expand_acc, 0, parts, width),
        ),
    )


def reg_attention_kernel(
    images,
    parts,
    meta_ref,
    z_ref,
    query_ref,
    totals_ref,
    normed_t_ref,
    mixed_t_ref,
    grad_mid_ref,
    pair_ref,
    pair_t_ref,
    x_ref,
    enc_branch_ref,
    enc_ffn_ref,
    gains,
    scales,
    enc_scales,
    query_hbm,
    keyval_hbm,
    output_hbm,
    query_grad_out,
    encoded_grad_out,
    small_out,
    keep_out,
    send_out,
    query_weight,
    keyval,
    output,
    sems,
    mask_ref,
    mixed_grad_ref,
    query_back,
    pair_back,
    query_acc,
    pair_acc,
    output_acc,
):
    meta = Meta(meta_ref, images)
    bin_now = pl.program_id(0)
    weights = Weights((output_hbm, query_hbm, keyval_hbm), (output, query_weight, keyval), sems)
    weights.start()
    first_step((small_out, query_acc, pair_acc, output_acc))
    size, width = mixed_grad_ref.shape
    mask_ref[...] = key_mask(meta, bin_now, "pick", size).astype(F32)
    grad_mid = grad_mid_ref[...]
    branch_grad = (scales[0:1, :] * grad_mid).astype(BF16)
    output_acc[...] += dot(mixed_t_ref[...], branch_grad)
    add_row(small_out, 0, rows_sum(branch_grad.astype(F32)))
    weights.wait(0)
    mixed_grad_ref[...] = dot_nt(branch_grad, output[...]).astype(BF16)

    def store(cols, grad_query, grad_key, grad_value):
        query_back[:, cols] = grad_query.astype(BF16)
        pair_back[:, cols] = grad_key.astype(BF16)
        pair_back[:, width + cols.start : width + cols.stop] = grad_value.astype(BF16)

    attend_backward(
        lambda cols: query_ref[:, cols],
        lambda cols: pair_ref[:, cols],
        lambda cols: pair_ref[:, width + cols.start : width + cols.stop],
        lambda cols: mixed_grad_ref[:, cols],
        totals_ref[...],
        mask_ref,
        store,
    )
    grad_query, grad_pair = query_back[...], pair_back[...]
    query_acc[...] += dot(normed_t_ref[...], grad_query)
    pair_acc[...] += dot(pair_t_ref[...], grad_pair)
    add_row(small_out, 1, rows_sum(grad_query.astype(F32)))
    add_row(small_out, 2, rows_sum(grad_pair[:, width:].astype(F32)))
    weights.wait(1)
    query_side = dot_nt(grad_query, query_weight[...]).astype(BF16).astype(F32)
    weights.wait(2)
    pair_side = dot_nt(grad_pair, keyval[...]).astype(BF16).astype(F32)
    unit_rows, inv_std = unit(z_ref[...].astype(F32))
    add_row(small_out, 3, rows_sum(query_side * unit_rows))
    add_row(small_out, 4, rows_sum(query_side))
    query_grad_out[...] = grad_mid + unit_back(query_side, unit_rows, inv_std, gains[0:1, :])
    encoded = (
        x_ref[...].astype(F32)
        + enc_scales[0:1, :] * enc_branch_ref[...].astype(F32)
        + enc_scales[1:2, :] * enc_ffn_ref[...]
    )
    unit_rows, inv_std = unit(encoded)
    add_row(small_out, 5, rows_sum(pair_side * unit_rows))
    add_row(small_out, 6, rows_sum(pair_side))
    encoded_grad_out[...] = unit_back(pair_side, unit_rows, inv_std, gains[1:2, :])

    def write_first(out):
        write_blocks(out, query_acc, 0, 1, width)
        write_blocks(out, output_acc, 0, 1, width, query_acc.shape[0])

    last_step(
        meta,
        lambda: write_halves(
            meta, keep_out, send_out, write_first, lambda out: write_blocks(out, pair_acc, 0, 2, width)
        ),
    )


def enc_ffn_kernel(
    images,
    parts,
    meta_ref,
    encoded_grad_ref,
    x_ref,
    branch_ref,
    ffn_ref,
    act_ref,
    slope_ref,
    middle_t_ref,
    gains,
    scales,
    expand_hbm,
    reduce_hbm,
    grad_mid_out,
    small_out,
    wide_out,
    keep_out,
    send_out,
    expand,
    reduce_weight,
    sems,
    expand_acc,
    reduce_acc,
):
    meta = Meta(meta_ref, images)
    weights = Weights((reduce_hbm, expand_hbm), (reduce_weight, expand), sems)
    weights.start()
    first_step((small_out, wide_out, expand_acc, reduce_acc))
    width = x_ref.shape[1]
    encoded_grad = encoded_grad_ref[...]
    add_row(small_out, 0, rows_sum(encoded_grad * ffn_ref[...]))
    grad_low = (scales[1:2, :] * encoded_grad).astype(BF16)
    add_row(small_out, 1, rows_sum(grad_low.astype(F32)))
    reduce_acc[...] += dot_tn(act_ref[...], grad_low)
    weights.wait(0)
    weights.wait(1)
    part_width = expand.shape[1] // parts
    grad_normed = ffn_backward(
        grad_low, slope_ref, middle_t_ref[...], expand, reduce_weight, expand_acc, wide_out, part_width
    )
    branch = branch_ref[...].astype(F32)
    unit_rows, inv_std = unit(x_ref[...].astype(F32) + scales[0:1, :] * branch)
    add_row(small_out, 2, rows_sum(grad_normed * unit_rows))
    add_row(small_out, 3, rows_sum(grad_normed))
    grad_mid = encoded_grad + unit_back(grad_normed, unit_rows, inv_std, gains[1:2, :])
    grad_mid_out[...] = grad_mid
    add_row(small_out, 4, rows_sum(grad_mid * branch))

    last_step(
        meta,
        lambda: write_halves(
            meta,
            keep_out,
            send_out,
            lambda out: write_blocks(out, reduce_acc, 0, 1, width),
            lambda out: write_blocks(out, expand_acc, 0, parts, width),
        ),
    )


def enc_attention_kernel(
    images,
    parts,
    meta_ref,
    grad_mid_ref,
    x_ref,
    triple_ref,
    totals_ref,
    normed_t_ref,
    mixed_t_ref,
    gains,
    scales,
    reg_small,
    reg_attn_small,
    enc_small,
    reg_wide,
    enc_wide,
    output_hbm,
    project_hbm,
    patch_grad_out,
    small_out,
    keep_out,
    send_out,
    output,
    project,
    sems,
    mask_ref,
    mixed_grad_ref,
    triple_back,
    project_acc,
    output_acc,
):
    meta = Meta(meta_ref, images)
    bin_now = pl.program_id(0)
    weights = Weights((output_hbm, project_hbm), (output, project), sems)
    weights.start()
    first_step((small_out, project_acc, output_acc))
    size, width = mixed_grad_ref.shape
    mask_ref[...] = key_mask(meta, bin_now, "keep", size).astype(F32)
    grad_mid = grad_mid_ref[...]
    branch_grad = (scales[0:1, :] * grad_mid).astype(BF16)
    output_acc[...] += dot(mixed_t_ref[...], branch_grad)
    add_row(small_out, 0, rows_sum(branch_grad.astype(F32)))
    weights.wait(0)
    mixed_grad_ref[...] = dot_nt(branch_grad, output[...]).astype(BF16)

    def store(cols, grad_query, grad_key, grad_value):
        triple_back[:, cols] = grad_query.astype(BF16)
        triple_back[:, width + cols.start : width + cols.stop] = grad_key.astype(BF16)
        triple_back[:, 2 * width + cols.start : 2 * width + cols.stop] = grad_value.astype(BF16)

    attend_backward(
        lambda cols: triple_ref[:, cols],
        lambda cols: triple_ref[:, width + cols.start : width + cols.stop],
        lambda cols: triple_ref[:, 2 * width + cols.start : 2 * width + cols.stop],
        lambda cols: mixed_grad_ref[:, cols],
        totals_ref[...],
        mask_ref,
        store,
    )
    back = triple_back[...]
    project_acc[...] += dot(normed_t_ref[...], back)
    add_row(small_out, 1, rows_sum(back[:, :width].astype(F32)))
    add_row(small_out, 2, rows_sum(back[:, 2 * width :].astype(F32)))
    weights.wait(1)
    rows_grad = dot_nt(back, project[...]).astype(BF16).astype(F32)
    unit_rows, inv_std = unit(x_ref[...].astype(F32))
    add_row(small_out, 3, rows_sum(rows_grad * unit_rows))
    add_row(small_out, 4, rows_sum(rows_grad))
    patch_grad_out[...] = grad_mid + unit_back(rows_grad, unit_rows, inv_std, gains[0:1, :])

    def write_first(out):
        part = output_acc.shape[0]
        write_blocks(out, output_acc, 0, 1, width)
        write_blocks(out, project_acc, 0, 1, width, part)
        out[2 * part :, :] = jnp.zeros_like(out[2 * part :, :])
        part_of = quarter_rows(meta, width, parts)
        at = 2 * part
        for small in (reg_small, reg_attn_small, enc_small, small_out):
            rows = small.shape[0]
            out[at : at + rows, :part] = dot_nt(small[...].astype(BF16), part_of).astype(BF16)
            at += rows
        mine = pl.ds(pl.multiple_of(meta.band() * width, width), width)
        out[at : at + 8, :] = reg_wide[:, mine].astype(BF16)
        out[at + 8 : at + 16, :] = enc_wide[:, mine].astype(BF16)

    def write_second(out):
        part = output_acc.shape[0]
        write_blocks(out, project_acc, 1, 3, width)
        out[2 * part :, :] = jnp.zeros_like(out[2 * part :, :])

    last_step(meta, lambda: write_halves(meta, keep_out, send_out, write_first, write_second))


def unpack_kernel(meta_ref, _, keep_place, pick_place, final_ref, query_grad_ref, patch_grad_ref, final_out, query_grad_out, patch_grad_out):
    rows = keep_place.shape[0]
    size = final_ref.shape[0]
    lane = lax.broadcasted_iota(jnp.int32, (rows, size), 1)
    kept = (keep_place[...] == lane).astype(BF16)
    picked = (pick_place[...] == lane).astype(BF16)
    for chosen, source, target in (
        (picked, final_ref, final_out),
        (picked, query_grad_ref, query_grad_out),
        (kept, patch_grad_ref, patch_grad_out),
    ):
        values = source[...]
        high = values.astype(BF16)
        rest = (values - high.astype(F32)).astype(BF16)
        target[...] = dot(chosen, high) + dot(chosen, rest)


def whole(array):
    return pl.BlockSpec(array.shape, lambda *_: (0,) * array.ndim)


def by_bin(shape):
    return pl.BlockSpec((None,) + tuple(shape), lambda b, meta: (jnp.minimum(b, meta[0] - 1), 0, 0))


def for_used_bins(kernel):
    def guarded(meta_ref, _, *refs):
        @pl.when(pl.program_id(0) < meta_ref[0])
        def _():
            kernel(meta_ref, *refs)

    return guarded


IN_HBM = pl.BlockSpec(memory_space=pl.ANY)
SHORT = pl.CostEstimate(flops=2_000_000_000, bytes_accessed=1_000_000, transcendentals=0)
LONG = pl.CostEstimate(flops=20_000_000_000, bytes_accessed=10_000_000, transcendentals=0)


def binned_call(kernel, name, images, chain, meta, binned, hbm, binned_outs, full_outs, scratch):
    operands = [meta, chain.last] + [a for _, a in binned] + list(hbm)
    in_specs = [IN_HBM] + [whole(a) if kind == "full" else by_bin(a.shape[1:]) for kind, a in binned]
    in_specs += [IN_HBM] * len(hbm)
    out_shape = [jax.ShapeDtypeStruct((images,) + s, t) for s, t in binned_outs]
    out_shape += [jax.ShapeDtypeStruct(s, t) for s, t in full_outs]
    out_specs = [by_bin(s) for s, _ in binned_outs]
    out_specs += [pl.BlockSpec(s, lambda *_: (0, 0)) for s, _ in full_outs]
    outs = pl.pallas_call(
        for_used_bins(kernel),
        name=name,
        out_shape=out_shape,
        grid_spec=pltpu.PrefetchScalarGridSpec(
            num_scalar_prefetch=1,
            grid=(images,),
            in_specs=in_specs,
            out_specs=out_specs,
            scratch_shapes=scratch,
        ),
        compiler_params=pltpu.CompilerParams(
            vmem_limit_bytes=VMEM_LIMIT, dimension_semantics=("arbitrary",)
        ),
        cost_estimate=LONG,
    )(*operands)
    chain.last = outs[-1]
    return outs


def merge_kernel(bit, place, mine, got, own, send):
    rows = own.shape[0]

    def half(side):
        at = pl.ds(pl.multiple_of(side * rows, rows), rows)
        return (mine[at, :].astype(F32) + got[at, :].astype(F32)).astype(BF16)

    own[...] = half(place[bit])
    send[...] = half(1 - place[bit])


def deal_kernel(place, mine, got, own, *sends):
    rows = own.shape[0]
    for offset, out in enumerate((own,) + sends):
        at = pl.ds(pl.multiple_of((place[3] ^ offset) * rows, rows), rows)
        out[...] = (mine[at, :].astype(F32) + got[at, :].astype(F32)).astype(BF16)


def add_kernel(place, mine, *refs):
    *parts, out = refs
    total = mine[...].astype(F32)
    for part in parts:
        total += part[...].astype(F32)
    out[...] = total.astype(BF16)


def assemble_kernel(bit, place, mine, got, out):
    rows = mine.shape[0]
    out[pl.ds(pl.multiple_of(place[bit] * rows, rows), rows), :] = mine[...]
    out[pl.ds(pl.multiple_of((1 - place[bit]) * rows, rows), rows), :] = got[...]


def gather_kernel(place, *refs):
    *pieces, out = refs
    rows = pieces[0].shape[0]
    for offset, piece in enumerate(pieces):
        out[pl.ds(pl.multiple_of((place[3] ^ offset) * rows, rows), rows), :] = piece[...]


def finish_kernel(layouts, place, half, got, *outs):
    def write(halves):
        targets = iter(outs)
        for layout, source in zip(layouts, halves, strict=True):
            for kind, start, count in layout:
                out = next(targets)
                if kind == "rows":
                    out[...] = source[start : start + count, :].astype(F32)
                else:
                    rows, width = out.shape[0], source.shape[1]
                    for i in range(count):
                        out[:, i * width : (i + 1) * width] = source[
                            start + i * rows : start + (i + 1) * rows, :
                        ].astype(F32)

    @pl.when(place[0] == 0)
    def _():
        write((half, got))

    @pl.when(place[0] == 1)
    def _():
        write((got, half))


class Chain:
    def __init__(self, first):
        self.last = first


class Reduction:
    def __init__(self, batch_size, chain, place, name, halves, layouts, outs):
        self.batch_size, self.chain, self.place, self.name = batch_size, chain, place, name
        self.layouts, self.outs = layouts, outs
        self.mine, send = halves
        self.line = batch_size // 2 == 4
        self.got = self.exchange(send, 1)

    def exchange(self, array, offset):
        return lax.ppermute(array, "batch", [(i, i ^ offset) for i in range(self.batch_size)])

    def call(self, kernel, step, out_shape, *arrays):
        count = len(arrays)

        def copied_in(place, _, *refs):
            sources, outs = refs[:count], refs[count : -count - 1]
            copies, sems = refs[-count - 1 : -1], refs[-1]
            moves = [
                pltpu.make_async_copy(source, copy, sems.at[i])
                for i, (source, copy) in enumerate(zip(sources, copies, strict=True))
            ]
            for move in moves:
                move.start()
            for move in moves:
                move.wait()
            kernel(place, *copies, *outs)

        in_vmem = pl.BlockSpec(memory_space=pltpu.VMEM)
        out = pl.pallas_call(
            copied_in,
            name=self.name + "_" + step,
            out_shape=out_shape,
            in_specs=[pl.BlockSpec(memory_space=pltpu.SMEM)] + [IN_HBM] * (count + 1),
            out_specs=jax.tree.map(lambda _: in_vmem, out_shape),
            scratch_shapes=[pltpu.VMEM(a.shape, a.dtype) for a in arrays]
            + [pltpu.SemaphoreType.DMA((count,))],
            compiler_params=pltpu.CompilerParams(vmem_limit_bytes=STEP_LIMIT),
            cost_estimate=SHORT,
        )(self.place, self.chain.last, *arrays)
        self.chain.last = out[0] if isinstance(out, (list, tuple)) else out
        return out

    def shape(self, numerator, denominator):
        rows, width = self.mine.shape
        return jax.ShapeDtypeStruct((rows * numerator // denominator, width), BF16)

    def merge(self, bit):
        if not self.line:
            if bit == 1:
                self.sum_line()
            return
        self.mine, send = self.call(
            functools.partial(merge_kernel, bit), f"merge{bit}", [self.shape(1, 2)] * 2, self.mine, self.got
        )
        self.got = self.exchange(send, 1 << bit)

    def add(self):
        if self.line:
            self.mine = self.call(add_kernel, "add", self.shape(1, 1), self.mine, self.got)
            self.got = self.exchange(self.mine, 4)

    def assemble(self, bit):
        if self.line:
            self.mine = self.call(
                functools.partial(assemble_kernel, bit), f"assemble{bit}", self.shape(2, 1), self.mine, self.got
            )
        if self.line or bit == 1:
            self.got = self.exchange(self.mine, 1 << (bit - 1))

    def sum_line(self):
        groups = [list(range(first, self.batch_size, 2)) for first in range(2)]
        self.mine = lax.psum(self.mine + self.got, "batch", axis_index_groups=groups)

    def deal(self):
        if not self.line:
            self.sum_line()
            return
        self.mine, *sends = self.call(deal_kernel, "deal", [self.shape(1, 4)] * 4, self.mine, self.got)
        self.parts = [self.exchange(send, 2 * (i + 1)) for i, send in enumerate(sends)]

    def total(self):
        if self.line:
            self.mine = self.call(add_kernel, "total", self.shape(1, 1), self.mine, *self.parts)
            self.parts = [self.exchange(self.mine, 2 * (i + 1)) for i in range(3)]

    def gather(self):
        if self.line:
            self.mine = self.call(gather_kernel, "gather", self.shape(4, 1), self.mine, *self.parts)
        self.got = self.exchange(self.mine, 1)

    def finish(self):
        return self.call(
            functools.partial(finish_kernel, self.layouts), "finish", list(self.outs), self.mine, self.got
        )


def body(
    batch_size,
    patches,
    queries,
    cotangent,
    counts,
    masked,
    enc_gains,
    enc_shifts,
    enc_widebias,
    enc_scales,
    enc_project,
    enc_output,
    enc_expand,
    enc_reduce,
    reg_gains,
    reg_shifts,
    reg_widebias,
    reg_scales,
    reg_query,
    reg_keyval,
    reg_output,
    reg_expand,
    reg_reduce,
):
    images, band_rows, width = patches.shape
    hidden = enc_expand.shape[1]
    band = lax.axis_index("band")
    batch = lax.axis_index("batch")
    side = lax.rem(batch, 2)
    masked_all = lax.all_gather(masked.astype(F32), "band", axis=1, tiled=True)
    size = masked_all.shape[1]
    parts = size // band_rows
    part, part_hidden = width // parts, hidden // parts
    token_rows = lax.all_gather(jnp.where(masked[:, :, None] == 0, patches, queries), "band", axis=0)
    grad_rows = lax.all_gather(cotangent, "band", axis=0)

    real = lax.broadcasted_iota(jnp.int32, (images, size), 1) < counts[:, None]
    keep = jnp.where(real & (masked_all == 0), 1.0, 0.0).astype(F32)
    pick = jnp.where(real & (masked_all == 1), 1.0, 0.0).astype(F32)
    in_smem = pl.BlockSpec(memory_space=pltpu.SMEM)
    in_vmem = pl.BlockSpec(memory_space=pltpu.VMEM)
    meta, keep_place, pick_place = pl.pallas_call(
        functools.partial(plan_kernel, images),
        name="plan",
        out_shape=[
            jax.ShapeDtypeStruct((HEAD + 5 * images,), jnp.int32),
            jax.ShapeDtypeStruct((images, size), jnp.int32),
            jax.ShapeDtypeStruct((images, size), jnp.int32),
        ],
        in_specs=[in_smem, in_smem, in_vmem, in_vmem],
        out_specs=[in_smem, in_vmem, in_vmem],
        scratch_shapes=[pltpu.SMEM((5, images), jnp.int32)],
    )(counts, jnp.stack([band, side]), keep, pick)

    chain = Chain(keep_place)
    place = jnp.stack([side, lax.rem(batch // 2, 2), lax.rem(batch // 4, 2), batch // 2])
    weight = functools.partial(jax.ShapeDtypeStruct, dtype=F32)

    def reduction(name, halves, layouts, outs):
        return Reduction(batch_size, chain, place, name, halves, layouts, outs)

    ffn_layout = ([("rows", 0, part_hidden)], [("blocks", 0, parts)])
    ffn_outs = (weight((part_hidden, width)), weight((part, hidden)))

    def both(*arrays):
        return [("full", a) for a in arrays]

    def cut(*arrays):
        return [("bin", a) for a in arrays]

    def vm(shape, dtype=BF16):
        return pltpu.VMEM(shape, dtype)

    enc_wide = enc_widebias.reshape(1, hidden)
    reg_wide = reg_widebias.reshape(1, hidden)
    (
        x,
        triple,
        enc_totals,
        enc_normed_t,
        enc_mixed_t,
        enc_branch,
        enc_act,
        enc_slope,
        enc_middle_t,
        enc_ffn,
        pair_t,
        pair,
    ) = binned_call(
        functools.partial(enc_forward_kernel, images, parts),
        "enc_forward",
        images,
        chain,
        meta,
        both(keep_place, token_rows, enc_gains, enc_shifts, enc_wide, enc_scales, reg_gains, reg_shifts),
        (enc_project, enc_output, enc_expand, enc_reduce, reg_keyval),
        [
            ((size, width), BF16),
            ((size, 3 * width), BF16),
            ((size, LANES), F32),
            ((part, size), BF16),
            ((part, size), BF16),
            ((size, width), BF16),
            ((size, part_hidden), BF16),
            ((size, hidden), BF16),
            ((part, size), BF16),
            ((size, width), F32),
            ((part, size), BF16),
            ((size, 2 * width), BF16),
        ],
        [],
        [
            vm(enc_project.shape),
            vm(enc_output.shape),
            vm(enc_expand.shape),
            vm(enc_reduce.shape),
            vm(reg_keyval.shape),
            pltpu.SemaphoreType.DMA((5,)),
            vm((size, width), F32),
            vm((size, size), F32),
            vm((size, hidden)),
            vm((size, width)),
        ],
    )
    small_rows, extra = 8, 64
    (
        z,
        reg_query_low,
        reg_totals,
        reg_normed_t,
        reg_mixed_t,
        final_rows,
        reg_grad_mid,
        reg_small,
        reg_wide_sum,
        *reg_ffn_grads,
    ) = binned_call(
        functools.partial(reg_forward_kernel, images, parts),
        "reg_forward",
        images,
        chain,
        meta,
        both(pick_place, token_rows, grad_rows)
        + cut(pair)
        + both(reg_gains, reg_shifts, reg_wide, reg_scales),
        (reg_query, reg_output, reg_expand, reg_reduce),
        [
            ((size, width), BF16),
            ((size, width), BF16),
            ((size, LANES), F32),
            ((part, size), BF16),
            ((part, size), BF16),
            ((size, width), F32),
            ((size, width), F32),
        ],
        [
            ((small_rows, width), F32),
            ((small_rows, hidden), F32),
            ((part_hidden, width), BF16),
            ((part_hidden, width), BF16),
        ],
        [
            vm(reg_query.shape),
            vm(reg_output.shape),
            vm(reg_expand.shape),
            vm(reg_reduce.shape),
            pltpu.SemaphoreType.DMA((4,)),
            vm((size, width), F32),
            vm((size, width), F32),
            vm((size, size), F32),
            vm((size, hidden)),
            vm((size, hidden)),
            vm((size, width)),
            vm((part, hidden), F32),
            vm((part_hidden, width), F32),
        ],
    )
    reg_ffn = reduction("reg_ffn", reg_ffn_grads, ffn_layout, ffn_outs)
    query_grad, encoded_grad, reg_attn_small, *reg_attn_grads = binned_call(
        functools.partial(reg_attention_kernel, images, parts),
        "reg_attention_grad",
        images,
        chain,
        meta,
        cut(z, reg_query_low, reg_totals, reg_normed_t, reg_mixed_t, reg_grad_mid, pair, pair_t, x, enc_branch, enc_ffn)
        + both(reg_gains, reg_scales, enc_scales),
        (reg_query, reg_keyval, reg_output),
        [((size, width), F32), ((size, width), F32)],
        [((small_rows, width), F32)] + [((2 * part, width), BF16)] * 2,
        [
            vm(reg_query.shape),
            vm(reg_keyval.shape),
            vm(reg_output.shape),
            pltpu.SemaphoreType.DMA((3,)),
            vm((size, size), F32),
            vm((size, width)),
            vm((size, width)),
            vm((size, 2 * width)),
            vm((part, width), F32),
            vm((part, 2 * width), F32),
            vm((part, width), F32),
        ],
    )
    reg_attn = reduction(
        "reg_attention",
        reg_attn_grads,
        ([("rows", 0, part), ("rows", part, part)], [("blocks", 0, 2)]),
        (weight((part, width)), weight((part, width)), weight((part, 2 * width))),
    )
    reg_ffn.deal()
    enc_grad_mid, enc_small, enc_wide_sum, *enc_ffn_grads = binned_call(
        functools.partial(enc_ffn_kernel, images, parts),
        "enc_ffn_grad",
        images,
        chain,
        meta,
        cut(encoded_grad, x, enc_branch, enc_ffn, enc_act, enc_slope, enc_middle_t)
        + both(enc_gains, enc_scales),
        (enc_expand, enc_reduce),
        [((size, width), F32)],
        [
            ((small_rows, width), F32),
            ((small_rows, hidden), F32),
            ((part_hidden, width), BF16),
            ((part_hidden, width), BF16),
        ],
        [
            vm(enc_expand.shape),
            vm(enc_reduce.shape),
            pltpu.SemaphoreType.DMA((2,)),
            vm((part, hidden), F32),
            vm((part_hidden, width), F32),
        ],
    )
    enc_ffn_sum = reduction("enc_ffn", enc_ffn_grads, ffn_layout, ffn_outs)
    reg_ffn.total()
    reg_attn.deal()
    patch_grad, _, *enc_attn_grads = binned_call(
        functools.partial(enc_attention_kernel, images, parts),
        "enc_attention_grad",
        images,
        chain,
        meta,
        cut(enc_grad_mid, x, triple, enc_totals, enc_normed_t, enc_mixed_t)
        + both(enc_gains, enc_scales, reg_small, reg_attn_small, enc_small, reg_wide_sum, enc_wide_sum),
        (enc_output, enc_project),
        [((size, width), F32)],
        [((small_rows, width), F32)] + [((2 * part + extra, width), BF16)] * 2,
        [
            vm(enc_output.shape),
            vm(enc_project.shape),
            pltpu.SemaphoreType.DMA((2,)),
            vm((size, size), F32),
            vm((size, width)),
            vm((size, 3 * width)),
            vm((part, 3 * width), F32),
            vm((part, width), F32),
        ],
    )

    enc_attn = reduction(
        "enc_attention",
        enc_attn_grads,
        ([("rows", 0, part), ("rows", part, part), ("rows", 2 * part, extra)], [("blocks", 0, 2)]),
        (weight((part, width)), weight((part, width)), weight((extra, width)), weight((part, 2 * width))),
    )
    reg_ffn.gather()
    reg_attn.total()
    enc_ffn_sum.merge(1)
    enc_attn.merge(1)
    reg_attn.gather()
    enc_ffn_sum.merge(2)
    enc_attn.merge(2)
    reg_reduce_grad, reg_expand_grad = reg_ffn.finish()
    enc_ffn_sum.add()
    enc_attn.add()

    def own_places(places):
        mine = lax.dynamic_slice_in_dim(places, band * band_rows, band_rows, 1)
        return mine[:, :, None]

    by_image = pl.BlockSpec((None, band_rows, 1), lambda i, m: (i, 0, 0))
    bin_of_image = pl.BlockSpec((None, size, width), lambda i, m: (m[HEAD + i], 0, 0))
    image_out = pl.BlockSpec((None, band_rows, width), lambda i, m: (i, 0, 0))
    prediction, query_grad, patch_grad = pl.pallas_call(
        unpack_kernel,
        name="unpack",
        out_shape=[jax.ShapeDtypeStruct(patches.shape, F32)] * 3,
        grid_spec=pltpu.PrefetchScalarGridSpec(
            num_scalar_prefetch=1,
            grid=(images,),
            in_specs=[IN_HBM, by_image, by_image, bin_of_image, bin_of_image, bin_of_image],
            out_specs=[image_out] * 3,
        ),
        compiler_params=pltpu.CompilerParams(vmem_limit_bytes=VMEM_LIMIT),
        cost_estimate=LONG,
    )(meta, chain.last, own_places(keep_place), own_places(pick_place), final_rows, query_grad, patch_grad)

    chain.last = prediction
    enc_ffn_sum.assemble(2)
    enc_attn.assemble(2)
    reg_query_grad, reg_output_grad, reg_keyval_grad = reg_attn.finish()
    enc_ffn_sum.assemble(1)
    enc_attn.assemble(1)
    enc_reduce_grad, enc_expand_grad = enc_ffn_sum.finish()
    enc_output_grad, project_query, vectors, project_rest = enc_attn.finish()
    enc_project_grad = jnp.concatenate([project_query, project_rest], 1)
    reg_s, reg_a, enc_s, enc_a = jnp.split(vectors[: 4 * small_rows, :part], 4, 0)
    reg_wide_grad, enc_wide_grad = vectors[4 * small_rows], vectors[5 * small_rows]
    enc_gains_grad = jnp.stack([enc_a[3], enc_s[2]])
    enc_shifts_grad = jnp.stack([enc_a[4], enc_a[1], enc_a[2], enc_a[0], enc_s[3], enc_s[1]])
    enc_scales_grad = jnp.stack([enc_s[4], enc_s[0]])
    reg_gains_grad = jnp.stack([reg_a[3], reg_a[5], reg_s[2]])
    reg_shifts_grad = jnp.stack(
        [reg_a[4], reg_a[6], reg_a[1], reg_a[2], reg_a[0], reg_s[3], reg_s[1]]
    )
    reg_scales_grad = jnp.stack([reg_s[4], reg_s[0]])
    return (
        prediction,
        patch_grad,
        query_grad,
        enc_gains_grad,
        enc_shifts_grad,
        enc_wide_grad,
        enc_scales_grad,
        enc_project_grad,
        enc_output_grad,
        enc_expand_grad,
        enc_reduce_grad,
        reg_gains_grad,
        reg_shifts_grad,
        reg_wide_grad,
        reg_scales_grad,
        reg_query_grad,
        reg_keyval_grad,
        reg_output_grad,
        reg_expand_grad,
        reg_reduce_grad,
    )


def solution(mesh):
    token = P("batch", "band", None)
    in_specs = (token, token, token, P("batch"), P("batch", "band")) + (P(),) * 17
    by_row, by_col = P("band", None), P(None, "band")
    out_specs = (
        token,
        token,
        token,
        by_col,
        by_col,
        P("band"),
        by_col,
        by_row,
        by_row,
        by_row,
        by_row,
        by_col,
        by_col,
        P("band"),
        by_col,
        by_row,
        by_row,
        by_row,
        by_row,
        by_row,
    )
    return jax.shard_map(
        functools.partial(body, mesh.shape["batch"]),
        mesh=mesh,
        in_specs=in_specs,
        out_specs=out_specs,
        check_vma=False,
    )
```

```python
import functools

import jax
import jax.numpy as jnp
from jax import lax
from jax.experimental import pallas as pl
from jax.experimental.pallas import tpu as pltpu
from jax.sharding import PartitionSpec as P

HEADS = 12
HD = 64
EPS = 1e-06
ROOT_HALF = 0.7071067811865476
INV_ROOT_TAU = 0.3989422804014327
NEG_LARGE = -1e30
F32 = jnp.float32
BF16 = jnp.bfloat16
VMEM_LIMIT = 56 * 1024 * 1024
STEP_LIMIT = 16 * 1024 * 1024
LANES = 128
HEAD = 4


def dot(a, b):
    return lax.dot_general(a, b, (((1,), (0,)), ((), ())), preferred_element_type=F32)


def dot_nt(a, b):
    return lax.dot_general(a, b, (((1,), (1,)), ((), ())), preferred_element_type=F32)


def dot_tn(a, b):
    return lax.dot_general(a, b, (((0,), (0,)), ((), ())), preferred_element_type=F32)


def unit(values):
    row_mean = jnp.mean(values, -1, keepdims=True)
    centred = values - row_mean
    variance = jnp.mean(centred * centred, -1, keepdims=True)
    inv_std = lax.rsqrt(variance + EPS)
    return centred * inv_std, inv_std


def unit_back(grad_out, unit_rows, inv_std, gain):
    scaled = grad_out * gain
    first_term = jnp.mean(scaled, -1, keepdims=True)
    second_term = jnp.mean(scaled * unit_rows, -1, keepdims=True)
    return inv_std * (scaled - first_term - unit_rows * second_term)


def rows_sum(values):
    return jnp.sum(values, 0, keepdims=True)


def gate_and_slope(pre_act):
    bell = 0.5 * (1.0 + lax.erf(pre_act * ROOT_HALF))
    slope = bell + pre_act * INV_ROOT_TAU * jnp.exp(-0.5 * pre_act * pre_act)
    return (pre_act * bell).astype(BF16), slope.astype(BF16)


class Meta:
    def __init__(self, ref, images):
        self.ref, self.images = ref, images

    def bins(self):
        return self.ref[0]

    def band(self):
        return self.ref[1]

    def bits(self):
        return self.ref[2], self.ref[3]

    def bin_of(self, image):
        return self.ref[HEAD + image]

    def keep_off(self, image):
        return self.ref[HEAD + self.images + image]

    def keep_count(self, image):
        return self.ref[HEAD + 2 * self.images + image]

    def pick_off(self, image):
        return self.ref[HEAD + 3 * self.images + image]

    def pick_count(self, image):
        return self.ref[HEAD + 4 * self.images + image]

    def segments(self, bin_now, kind, shape, dim, blank):
        rows = lax.broadcasted_iota(jnp.int32, shape, dim)
        owner = jnp.full(shape, blank, jnp.int32)
        for image in range(self.images):
            start = self.keep_off(image) if kind == "keep" else self.pick_off(image)
            count = self.keep_count(image) if kind == "keep" else self.pick_count(image)
            stop = start + jnp.where(self.bin_of(image) == bin_now, count, 0)
            owner = jnp.where((rows >= start) & (rows < stop), image, owner)
        return owner


def key_mask(meta, bin_now, query_kind, size):
    query_owner = meta.segments(bin_now, query_kind, (size, 1), 0, -2)
    key_owner = meta.segments(bin_now, "keep", (1, size), 1, -1)
    return query_owner == key_owner


def quarter_rows(meta, width, parts):
    part = width // parts
    row = lax.broadcasted_iota(jnp.int32, (part, width), 0) + meta.band() * part
    return (row == lax.broadcasted_iota(jnp.int32, (part, width), 1)).astype(BF16)


def lower_half():
    return lax.broadcasted_iota(jnp.int32, (1, LANES), 1) < HD


def attend_forward(query_of, key_of, value_of, mask_ref, store, size):
    low = lower_half()
    sides = (low.astype(BF16), (~low).astype(BF16))
    lane = lax.broadcasted_iota(jnp.int32, (size, LANES), 1)
    totals = jnp.zeros((size, LANES), F32)
    for pair in range(HEADS // 2):
        cols = slice(pair * LANES, (pair + 1) * LANES)
        query, key, value = query_of(cols), key_of(cols), value_of(cols)
        mixed = []
        for side in range(2):
            scores = dot_nt(query, key * sides[side]) * HD ** (-0.5)
            scores = jnp.where(mask_ref[...] > 0, scores, NEG_LARGE)
            row_top = jnp.max(scores, -1, keepdims=True)
            exp_scores = jnp.exp(scores - row_top)
            row_total = jnp.sum(exp_scores, -1, keepdims=True)
            weights = (exp_scores * (1.0 / row_total)).astype(BF16)
            totals = jnp.where(lane == 2 * pair + side, row_top + jnp.log(row_total), totals)
            mixed.append(dot(weights, value))
        store(cols, jnp.where(low, mixed[0], mixed[1]))
    return totals


def attend_backward(query_of, key_of, value_of, grad_of, totals, mask_ref, store):
    low = lower_half()
    sides = (low.astype(BF16), (~low).astype(BF16))
    for pair in range(HEADS // 2):
        cols = slice(pair * LANES, (pair + 1) * LANES)
        query, key, value, grad = query_of(cols), key_of(cols), value_of(cols), grad_of(cols)
        grad_query, grad_key, grad_value = [], [], []
        for side in range(2):
            head = 2 * pair + side
            scores = dot_nt(query, key * sides[side]) * HD ** (-0.5)
            scores = jnp.where(mask_ref[...] > 0, scores, NEG_LARGE)
            probs = jnp.exp(scores - totals[:, head : head + 1])
            grad_value.append(dot_tn(probs.astype(BF16), grad))
            grad_probs = dot_nt(grad, value * sides[side])
            inner = jnp.sum(grad_probs * probs, -1, keepdims=True)
            grad_scores = (probs * (grad_probs - inner)).astype(BF16)
            grad_query.append(dot(grad_scores, key))
            grad_key.append(dot_tn(grad_scores, query))
        store(
            cols,
            jnp.where(low, grad_query[0], grad_query[1]) * HD ** (-0.5),
            jnp.where(low, grad_key[0], grad_key[1]) * HD ** (-0.5),
            jnp.where(low, grad_value[0], grad_value[1]),
        )


def pack_rows(meta, bin_now, place_ref, sources, size):
    for _, packed in sources:
        packed[...] = jnp.zeros_like(packed)
    for image in range(meta.images):

        @pl.when(meta.bin_of(image) == bin_now)
        def _():
            row = lax.broadcasted_iota(jnp.int32, (size, size), 0)
            chosen = (row == place_ref[image : image + 1, :]).astype(BF16)
            for gathered, packed in sources:
                rows = jnp.concatenate(
                    [gathered[band, image] for band in range(gathered.shape[0])], 0
                )
                packed[...] += dot(chosen, rows)


class Weights:
    def __init__(self, sources, targets, sems):
        self.copies = [
            pltpu.make_async_copy(source, target, sems.at[i])
            for i, (source, target) in enumerate(zip(sources, targets, strict=True))
        ]

    def start(self):
        @pl.when(pl.program_id(0) == 0)
        def _():
            for copy in self.copies:
                copy.start()

    def wait(self, index):
        @pl.when(pl.program_id(0) == 0)
        def _():
            self.copies[index].wait()


def add_row(small_ref, row, values):
    small_ref[row : row + 1, :] += values


def first_step(refs):
    @pl.when(pl.program_id(0) == 0)
    def _():
        for ref in refs:
            ref[...] = jnp.zeros_like(ref)


def write_halves(bit, keep_out, send_out, write):
    @pl.when(bit == 0)
    def _():
        write(0, keep_out)
        write(1, send_out)

    @pl.when(bit == 1)
    def _():
        write(1, keep_out)
        write(0, send_out)


def write_blocks(target, acc, start, stop, width, at=0):
    part = acc.shape[0]
    for i in range(start, stop):
        row = at + (i - start) * part
        target[row : row + part, :] = acc[:, i * width : (i + 1) * width].astype(BF16)


def write_rows(target, acc, half):
    rows = target.shape[0]
    target[...] = acc[half * rows : (half + 1) * rows, :].astype(BF16)


def last_step(meta, write):
    @pl.when(pl.program_id(0) == meta.bins() - 1)
    def _():
        write()


def plan_kernel(images, counts_ref, band_ref, keep_ref, pick_ref, meta_ref, keep_place_ref, pick_place_ref, words):
    size = keep_ref.shape[1]
    before = (
        lax.broadcasted_iota(jnp.int32, (size, size), 0)
        <= lax.broadcasted_iota(jnp.int32, (size, size), 1)
    ).astype(BF16)
    keep, pick = keep_ref[...], pick_ref[...]
    keep_rank = dot(keep.astype(BF16), before).astype(jnp.int32) - 1
    pick_rank = dot(pick.astype(BF16), before).astype(jnp.int32) - 1
    for image in range(images):
        words[0, image] = jnp.sum(keep[image : image + 1, :]).astype(jnp.int32)
        words[1, image] = jnp.sum(pick[image : image + 1, :]).astype(jnp.int32)
        for row in (2, 3, 4):
            words[row, image] = 0

    def place(_, bins):
        def largest(image, best):
            open_now = words[4, image] == 0
            better = open_now & ((best < 0) | (counts_ref[image] > counts_ref[jnp.maximum(best, 0)]))
            return jnp.where(better, image, best)

        image = lax.fori_loop(0, images, largest, jnp.int32(-1))
        keep_count, pick_count = words[0, image], words[1, image]

        def first_fit(step, best):
            bin_now = images - 1 - step
            fits = (words[2, bin_now] + keep_count <= size) & (words[3, bin_now] + pick_count <= size)
            return jnp.where(fits, bin_now, best)

        bin_now = lax.fori_loop(0, images, first_fit, jnp.int32(0))
        meta_ref[HEAD + image] = bin_now
        meta_ref[HEAD + images + image] = words[2, bin_now]
        meta_ref[HEAD + 2 * images + image] = keep_count
        meta_ref[HEAD + 3 * images + image] = words[3, bin_now]
        meta_ref[HEAD + 4 * images + image] = pick_count
        words[2, bin_now] = words[2, bin_now] + keep_count
        words[3, bin_now] = words[3, bin_now] + pick_count
        words[4, image] = 1
        return jnp.maximum(bins, bin_now + 1)

    meta_ref[0] = lax.fori_loop(0, images, place, jnp.int32(0))
    meta_ref[1] = band_ref[0]
    meta_ref[2] = band_ref[1]
    meta_ref[3] = band_ref[2]
    for image in range(images):
        row = slice(image, image + 1)
        keep_place_ref[row, :] = jnp.where(
            keep[row, :] > 0, keep_rank[row, :] + meta_ref[HEAD + images + image], -1
        )
        pick_place_ref[row, :] = jnp.where(
            pick[row, :] > 0, pick_rank[row, :] + meta_ref[HEAD + 3 * images + image], -1
        )


def ffn_forward(normed, expand, wide_bias, reduce_weight, act_ref, slope_ref, width):
    total = None
    for start in range(0, expand.shape[1], width):
        cols = slice(start, start + width)
        act, slope = gate_and_slope(dot(normed, expand[:, cols]) + wide_bias[:, cols])
        act_ref[:, cols] = act
        slope_ref[:, cols] = slope
        part = dot(act, reduce_weight[cols, :])
        total = part if total is None else total + part
    return total


def ffn_backward(grad_low, slope_ref, normed_part, expand, reduce_weight, expand_acc, wide_ref, width):
    total = None
    for start in range(0, expand.shape[1], width):
        cols = slice(start, start + width)
        grad_act = dot_nt(grad_low, reduce_weight[cols, :])
        grad_pre = grad_act * slope_ref[:, cols].astype(F32)
        grad_pre_low = grad_pre.astype(BF16)
        wide_ref[0:1, cols] += rows_sum(grad_pre_low.astype(F32))
        expand_acc[:, cols] += dot(normed_part, grad_pre_low)
        part = dot_nt(grad_pre_low, expand[:, cols])
        total = part if total is None else total + part
    return total


def enc_forward_kernel(
    images,
    parts,
    meta_ref,
    place_ref,
    rows_ref,
    gains,
    shifts,
    wide_bias,
    scales,
    reg_gains,
    reg_shifts,
    project_hbm,
    output_hbm,
    expand_hbm,
    reduce_hbm,
    keyval_hbm,
    x_out,
    triple_out,
    totals_out,
    normed_t_out,
    mixed_t_out,
    branch_out,
    act_out,
    slope_out,
    middle_t_out,
    ffn_out,
    pair_t_out,
    pair_out,
    project,
    output,
    expand,
    reduce_weight,
    keyval,
    sems,
    packed,
    mask_ref,
    act_all,
    mixed_ref,
):
    meta = Meta(meta_ref, images)
    bin_now = pl.program_id(0)
    weights = Weights(
        (project_hbm, output_hbm, expand_hbm, reduce_hbm, keyval_hbm),
        (project, output, expand, reduce_weight, keyval),
        sems,
    )
    weights.start()
    size, width = packed.shape
    pack_rows(meta, bin_now, place_ref, ((rows_ref, packed),), size)
    mask_ref[...] = key_mask(meta, bin_now, "keep", size).astype(F32)
    part_of = quarter_rows(meta, width, parts)
    x = packed[...]
    x_out[...] = x.astype(BF16)
    unit_rows, _ = unit(x)
    normed = (unit_rows * gains[0:1, :] + shifts[0:1, :]).astype(BF16)
    normed_t_out[...] = dot_nt(part_of, normed).astype(BF16)
    weights.wait(0)
    triple_out[:, :width] = (dot(normed, project[:, :width]) + shifts[1:2, :]).astype(BF16)
    triple_out[:, width : 2 * width] = dot(normed, project[:, width : 2 * width]).astype(BF16)
    triple_out[:, 2 * width :] = (dot(normed, project[:, 2 * width :]) + shifts[2:3, :]).astype(BF16)

    def store(cols, mixed):
        mixed_ref[:, cols] = mixed.astype(BF16)

    totals_out[...] = attend_forward(
        lambda cols: triple_out[:, cols],
        lambda cols: triple_out[:, width + cols.start : width + cols.stop],
        lambda cols: triple_out[:, 2 * width + cols.start : 2 * width + cols.stop],
        mask_ref,
        store,
        size,
    )
    mixed = mixed_ref[...]
    mixed_t_out[...] = dot_nt(part_of, mixed).astype(BF16)
    weights.wait(1)
    branch = (dot(mixed, output[...]) + shifts[3:4, :]).astype(BF16)
    branch_out[...] = branch
    middle = x + scales[0:1, :] * branch.astype(F32)
    unit_rows, _ = unit(middle)
    normed = (unit_rows * gains[1:2, :] + shifts[4:5, :]).astype(BF16)
    middle_t_out[...] = dot_nt(part_of, normed).astype(BF16)
    weights.wait(2)
    weights.wait(3)
    part_width = expand.shape[1] // parts
    ffn = ffn_forward(normed, expand, wide_bias, reduce_weight, act_all, slope_out, part_width) + shifts[5:6, :]
    act_out[...] = act_all[:, pl.ds(pl.multiple_of(meta.band() * part_width, part_width), part_width)]
    ffn_out[...] = ffn
    encoded = middle + scales[1:2, :] * ffn
    unit_rows, _ = unit(encoded)
    pair_normed = (unit_rows * reg_gains[1:2, :] + reg_shifts[1:2, :]).astype(BF16)
    pair_t_out[...] = dot_nt(part_of, pair_normed).astype(BF16)
    weights.wait(4)
    pair_out[:, :width] = dot(pair_normed, keyval[:, :width]).astype(BF16)
    pair_out[:, width:] = (dot(pair_normed, keyval[:, width:]) + reg_shifts[3:4, :]).astype(BF16)


def reg_forward_kernel(
    images,
    parts,
    meta_ref,
    place_ref,
    rows_ref,
    grads_ref,
    pair_ref,
    gains,
    shifts,
    wide_bias,
    scales,
    query_hbm,
    output_hbm,
    expand_hbm,
    reduce_hbm,
    x_out,
    query_out,
    totals_out,
    normed_t_out,
    mixed_t_out,
    final_out,
    grad_mid_out,
    small_out,
    wide_out,
    keep_out,
    send_out,
    other_keep_out,
    other_send_out,
    query_weight,
    output,
    expand,
    reduce_weight,
    sems,
    packed,
    packed_grad,
    mask_ref,
    act_all,
    slope_all,
    mixed_ref,
    expand_acc,
    reduce_acc,
):
    meta = Meta(meta_ref, images)
    bin_now = pl.program_id(0)
    weights = Weights(
        (query_hbm, output_hbm, expand_hbm, reduce_hbm),
        (query_weight, output, expand, reduce_weight),
        sems,
    )
    weights.start()
    first_step((small_out, wide_out, expand_acc, reduce_acc))
    size, width = packed.shape
    pack_rows(meta, bin_now, place_ref, ((rows_ref, packed), (grads_ref, packed_grad)), size)
    mask_ref[...] = key_mask(meta, bin_now, "pick", size).astype(F32)
    part_of = quarter_rows(meta, width, parts)
    z = packed[...]
    x_out[...] = z.astype(BF16)
    unit_rows, _ = unit(z)
    normed = (unit_rows * gains[0:1, :] + shifts[0:1, :]).astype(BF16)
    normed_t_out[...] = dot_nt(part_of, normed).astype(BF16)
    weights.wait(0)
    query_out[...] = (dot(normed, query_weight[...]) + shifts[2:3, :]).astype(BF16)

    def store(cols, mixed):
        mixed_ref[:, cols] = mixed.astype(BF16)

    totals_out[...] = attend_forward(
        lambda cols: query_out[:, cols],
        lambda cols: pair_ref[:, cols],
        lambda cols: pair_ref[:, width + cols.start : width + cols.stop],
        mask_ref,
        store,
        size,
    )
    mixed = mixed_ref[...]
    mixed_t_out[...] = dot_nt(part_of, mixed).astype(BF16)
    weights.wait(1)
    branch = (dot(mixed, output[...]) + shifts[4:5, :]).astype(BF16).astype(F32)
    middle = z + scales[0:1, :] * branch
    unit_rows, inv_std = unit(middle)
    normed = (unit_rows * gains[2:3, :] + shifts[5:6, :]).astype(BF16)
    normed_part = dot_nt(part_of, normed).astype(BF16)
    weights.wait(2)
    weights.wait(3)
    part_width = expand.shape[1] // parts
    ffn = ffn_forward(normed, expand, wide_bias, reduce_weight, act_all, slope_all, part_width) + shifts[6:7, :]
    final_out[...] = middle + scales[1:2, :] * ffn
    grad_final = packed_grad[...]
    add_row(small_out, 0, rows_sum(grad_final * ffn))
    grad_low = (scales[1:2, :] * grad_final).astype(BF16)
    add_row(small_out, 1, rows_sum(grad_low.astype(F32)))
    act_part = act_all[:, pl.ds(pl.multiple_of(meta.band() * part_width, part_width), part_width)]
    reduce_acc[...] += dot_tn(act_part, grad_low)
    grad_normed = ffn_backward(
        grad_low, slope_all, normed_part, expand, reduce_weight, expand_acc, wide_out, part_width
    )
    add_row(small_out, 2, rows_sum(grad_normed * unit_rows))
    add_row(small_out, 3, rows_sum(grad_normed))
    grad_mid = grad_final + unit_back(grad_normed, unit_rows, inv_std, gains[2:3, :])
    grad_mid_out[...] = grad_mid
    add_row(small_out, 4, rows_sum(grad_mid * branch))

    def write():
        low, high = meta.bits()
        write_halves(low, keep_out, send_out, lambda half, out: write_rows(out, reduce_acc, half))
        write_halves(
            high,
            other_keep_out,
            other_send_out,
            lambda half, out: write_blocks(out, expand_acc, half * parts // 2, (half + 1) * parts // 2, width),
        )

    last_step(meta, write)


def reg_attention_kernel(
    images,
    parts,
    meta_ref,
    z_ref,
    query_ref,
    totals_ref,
    normed_t_ref,
    mixed_t_ref,
    grad_mid_ref,
    pair_ref,
    pair_t_ref,
    x_ref,
    enc_branch_ref,
    enc_ffn_ref,
    gains,
    scales,
    enc_scales,
    query_hbm,
    keyval_hbm,
    output_hbm,
    query_grad_out,
    encoded_grad_out,
    small_out,
    keep_out,
    send_out,
    other_keep_out,
    other_send_out,
    query_weight,
    keyval,
    output,
    sems,
    mask_ref,
    mixed_grad_ref,
    query_back,
    pair_back,
    query_acc,
    pair_acc,
    output_acc,
):
    meta = Meta(meta_ref, images)
    bin_now = pl.program_id(0)
    weights = Weights((output_hbm, query_hbm, keyval_hbm), (output, query_weight, keyval), sems)
    weights.start()
    first_step((small_out, query_acc, pair_acc, output_acc))
    size, width = mixed_grad_ref.shape
    mask_ref[...] = key_mask(meta, bin_now, "pick", size).astype(F32)
    grad_mid = grad_mid_ref[...]
    branch_grad = (scales[0:1, :] * grad_mid).astype(BF16)
    output_acc[...] += dot(mixed_t_ref[...], branch_grad)
    add_row(small_out, 0, rows_sum(branch_grad.astype(F32)))
    weights.wait(0)
    mixed_grad_ref[...] = dot_nt(branch_grad, output[...]).astype(BF16)

    def store(cols, grad_query, grad_key, grad_value):
        query_back[:, cols] = grad_query.astype(BF16)
        pair_back[:, cols] = grad_key.astype(BF16)
        pair_back[:, width + cols.start : width + cols.stop] = grad_value.astype(BF16)

    attend_backward(
        lambda cols: query_ref[:, cols],
        lambda cols: pair_ref[:, cols],
        lambda cols: pair_ref[:, width + cols.start : width + cols.stop],
        lambda cols: mixed_grad_ref[:, cols],
        totals_ref[...],
        mask_ref,
        store,
    )
    grad_query, grad_pair = query_back[...], pair_back[...]
    query_acc[...] += dot(normed_t_ref[...], grad_query)
    pair_acc[...] += dot(pair_t_ref[...], grad_pair)
    add_row(small_out, 1, rows_sum(grad_query.astype(F32)))
    add_row(small_out, 2, rows_sum(grad_pair[:, width:].astype(F32)))
    weights.wait(1)
    query_side = dot_nt(grad_query, query_weight[...]).astype(BF16).astype(F32)
    weights.wait(2)
    pair_side = dot_nt(grad_pair, keyval[...]).astype(BF16).astype(F32)
    unit_rows, inv_std = unit(z_ref[...].astype(F32))
    add_row(small_out, 3, rows_sum(query_side * unit_rows))
    add_row(small_out, 4, rows_sum(query_side))
    query_grad_out[...] = grad_mid + unit_back(query_side, unit_rows, inv_std, gains[0:1, :])
    encoded = (
        x_ref[...].astype(F32)
        + enc_scales[0:1, :] * enc_branch_ref[...].astype(F32)
        + enc_scales[1:2, :] * enc_ffn_ref[...]
    )
    unit_rows, inv_std = unit(encoded)
    add_row(small_out, 5, rows_sum(pair_side * unit_rows))
    add_row(small_out, 6, rows_sum(pair_side))
    encoded_grad_out[...] = unit_back(pair_side, unit_rows, inv_std, gains[1:2, :])

    def write():
        low, high = meta.bits()
        write_halves(
            low,
            keep_out,
            send_out,
            lambda half, out: write_blocks(out, (query_acc, output_acc)[half], 0, 1, width),
        )
        write_halves(
            high,
            other_keep_out,
            other_send_out,
            lambda half, out: write_blocks(out, pair_acc, half, half + 1, width),
        )

    last_step(meta, write)


def enc_ffn_kernel(
    images,
    parts,
    meta_ref,
    encoded_grad_ref,
    x_ref,
    branch_ref,
    ffn_ref,
    act_ref,
    slope_ref,
    middle_t_ref,
    gains,
    scales,
    expand_hbm,
    reduce_hbm,
    grad_mid_out,
    small_out,
    wide_out,
    keep_out,
    send_out,
    other_keep_out,
    other_send_out,
    expand,
    reduce_weight,
    sems,
    expand_acc,
    reduce_acc,
):
    meta = Meta(meta_ref, images)
    weights = Weights((reduce_hbm, expand_hbm), (reduce_weight, expand), sems)
    weights.start()
    first_step((small_out, wide_out, expand_acc, reduce_acc))
    width = x_ref.shape[1]
    encoded_grad = encoded_grad_ref[...]
    add_row(small_out, 0, rows_sum(encoded_grad * ffn_ref[...]))
    grad_low = (scales[1:2, :] * encoded_grad).astype(BF16)
    add_row(small_out, 1, rows_sum(grad_low.astype(F32)))
    reduce_acc[...] += dot_tn(act_ref[...], grad_low)
    weights.wait(0)
    weights.wait(1)
    part_width = expand.shape[1] // parts
    grad_normed = ffn_backward(
        grad_low, slope_ref, middle_t_ref[...], expand, reduce_weight, expand_acc, wide_out, part_width
    )
    branch = branch_ref[...].astype(F32)
    unit_rows, inv_std = unit(x_ref[...].astype(F32) + scales[0:1, :] * branch)
    add_row(small_out, 2, rows_sum(grad_normed * unit_rows))
    add_row(small_out, 3, rows_sum(grad_normed))
    grad_mid = encoded_grad + unit_back(grad_normed, unit_rows, inv_std, gains[1:2, :])
    grad_mid_out[...] = grad_mid
    add_row(small_out, 4, rows_sum(grad_mid * branch))

    def write():
        low, high = meta.bits()
        write_halves(low, keep_out, send_out, lambda half, out: write_rows(out, reduce_acc, half))
        write_halves(
            high,
            other_keep_out,
            other_send_out,
            lambda half, out: write_blocks(out, expand_acc, half * parts // 2, (half + 1) * parts // 2, width),
        )

    last_step(meta, write)


def enc_attention_kernel(
    images,
    parts,
    meta_ref,
    grad_mid_ref,
    x_ref,
    triple_ref,
    totals_ref,
    normed_t_ref,
    mixed_t_ref,
    gains,
    scales,
    reg_small,
    reg_attn_small,
    enc_small,
    reg_wide,
    enc_wide,
    output_hbm,
    project_hbm,
    patch_grad_out,
    small_out,
    keep_out,
    send_out,
    other_keep_out,
    other_send_out,
    output,
    project,
    sems,
    mask_ref,
    mixed_grad_ref,
    triple_back,
    project_acc,
    output_acc,
):
    meta = Meta(meta_ref, images)
    bin_now = pl.program_id(0)
    weights = Weights((output_hbm, project_hbm), (output, project), sems)
    weights.start()
    first_step((small_out, project_acc, output_acc))
    size, width = mixed_grad_ref.shape
    mask_ref[...] = key_mask(meta, bin_now, "keep", size).astype(F32)
    grad_mid = grad_mid_ref[...]
    branch_grad = (scales[0:1, :] * grad_mid).astype(BF16)
    output_acc[...] += dot(mixed_t_ref[...], branch_grad)
    add_row(small_out, 0, rows_sum(branch_grad.astype(F32)))
    weights.wait(0)
    mixed_grad_ref[...] = dot_nt(branch_grad, output[...]).astype(BF16)

    def store(cols, grad_query, grad_key, grad_value):
        triple_back[:, cols] = grad_query.astype(BF16)
        triple_back[:, width + cols.start : width + cols.stop] = grad_key.astype(BF16)
        triple_back[:, 2 * width + cols.start : 2 * width + cols.stop] = grad_value.astype(BF16)

    attend_backward(
        lambda cols: triple_ref[:, cols],
        lambda cols: triple_ref[:, width + cols.start : width + cols.stop],
        lambda cols: triple_ref[:, 2 * width + cols.start : 2 * width + cols.stop],
        lambda cols: mixed_grad_ref[:, cols],
        totals_ref[...],
        mask_ref,
        store,
    )
    back = triple_back[...]
    project_acc[...] += dot(normed_t_ref[...], back)
    add_row(small_out, 1, rows_sum(back[:, :width].astype(F32)))
    add_row(small_out, 2, rows_sum(back[:, 2 * width :].astype(F32)))
    weights.wait(1)
    rows_grad = dot_nt(back, project[...]).astype(BF16).astype(F32)
    unit_rows, inv_std = unit(x_ref[...].astype(F32))
    add_row(small_out, 3, rows_sum(rows_grad * unit_rows))
    add_row(small_out, 4, rows_sum(rows_grad))
    patch_grad_out[...] = grad_mid + unit_back(rows_grad, unit_rows, inv_std, gains[0:1, :])

    def write_one(half, out):
        part = output_acc.shape[0]
        out[part:, :] = jnp.zeros_like(out[part:, :])
        if half == 1:
            write_blocks(out, project_acc, 0, 1, width)
            return
        write_blocks(out, output_acc, 0, 1, width)
        part_of = quarter_rows(meta, width, parts)
        at = part
        for small in (reg_small, reg_attn_small, enc_small, small_out):
            rows = small.shape[0]
            out[at : at + rows, :part] = dot_nt(small[...].astype(BF16), part_of).astype(BF16)
            at += rows
        mine = pl.ds(pl.multiple_of(meta.band() * width, width), width)
        out[at : at + 8, :] = reg_wide[:, mine].astype(BF16)
        out[at + 8 : at + 16, :] = enc_wide[:, mine].astype(BF16)

    def write():
        low, high = meta.bits()
        write_halves(low, keep_out, send_out, write_one)
        write_halves(
            high,
            other_keep_out,
            other_send_out,
            lambda half, out: write_blocks(out, project_acc, 1 + half, 2 + half, width),
        )

    last_step(meta, write)


def unpack_kernel(meta_ref, _, keep_place, pick_place, final_ref, query_grad_ref, patch_grad_ref, final_out, query_grad_out, patch_grad_out):
    rows = keep_place.shape[0]
    size = final_ref.shape[0]
    lane = lax.broadcasted_iota(jnp.int32, (rows, size), 1)
    kept = (keep_place[...] == lane).astype(BF16)
    picked = (pick_place[...] == lane).astype(BF16)
    for chosen, source, target in (
        (picked, final_ref, final_out),
        (picked, query_grad_ref, query_grad_out),
        (kept, patch_grad_ref, patch_grad_out),
    ):
        values = source[...]
        high = values.astype(BF16)
        rest = (values - high.astype(F32)).astype(BF16)
        target[...] = dot(chosen, high) + dot(chosen, rest)


def whole(array):
    return pl.BlockSpec(array.shape, lambda *_: (0,) * array.ndim)


def by_bin(shape):
    return pl.BlockSpec((None,) + tuple(shape), lambda b, meta: (jnp.minimum(b, meta[0] - 1), 0, 0))


def for_used_bins(kernel):
    def guarded(meta_ref, _, *refs):
        @pl.when(pl.program_id(0) < meta_ref[0])
        def _():
            kernel(meta_ref, *refs)

    return guarded


IN_HBM = pl.BlockSpec(memory_space=pl.ANY)
SHORT = pl.CostEstimate(flops=2_000_000_000, bytes_accessed=1_000_000, transcendentals=0)
LONG = pl.CostEstimate(flops=20_000_000_000, bytes_accessed=10_000_000, transcendentals=0)


def binned_call(kernel, name, images, chain, meta, binned, hbm, binned_outs, full_outs, scratch):
    operands = [meta, chain.last] + [a for _, a in binned] + list(hbm)
    in_specs = [IN_HBM] + [whole(a) if kind == "full" else by_bin(a.shape[1:]) for kind, a in binned]
    in_specs += [IN_HBM] * len(hbm)
    out_shape = [jax.ShapeDtypeStruct((images,) + s, t) for s, t in binned_outs]
    out_shape += [jax.ShapeDtypeStruct(s, t) for s, t in full_outs]
    out_specs = [by_bin(s) for s, _ in binned_outs]
    out_specs += [pl.BlockSpec(s, lambda *_: (0, 0)) for s, _ in full_outs]
    outs = pl.pallas_call(
        for_used_bins(kernel),
        name=name,
        out_shape=out_shape,
        grid_spec=pltpu.PrefetchScalarGridSpec(
            num_scalar_prefetch=1,
            grid=(images,),
            in_specs=in_specs,
            out_specs=out_specs,
            scratch_shapes=scratch,
        ),
        compiler_params=pltpu.CompilerParams(
            vmem_limit_bytes=VMEM_LIMIT, dimension_semantics=("arbitrary",)
        ),
        cost_estimate=LONG,
    )(*operands)
    chain.last = outs[-1]
    return outs


def summed(mine, got, at):
    return (mine[at, :].astype(F32) + got[at, :].astype(F32)).astype(BF16)


def rows_at(index, rows):
    return pl.ds(pl.multiple_of(index * rows, rows), rows)


def turn_kernel(place, mine, got, other_mine, other_got, own, send, other_own, other_send):
    for bit, a, b, keep, out in ((1, mine, got, own, send), (0, other_mine, other_got, other_own, other_send)):
        rows = keep.shape[0]
        keep[...] = summed(a, b, rows_at(place[bit], rows))
        out[...] = summed(a, b, rows_at(1 - place[bit], rows))


def join_kernel(place, mine, got, other_mine, other_got, own, send):
    at = 0
    for a, b in ((mine, got), (other_mine, other_got)):
        rows = a.shape[0] // 2
        own[at : at + rows, :] = summed(a, b, rows_at(place[2], rows))
        send[at : at + rows, :] = summed(a, b, rows_at(1 - place[2], rows))
        at += rows


def add_kernel(place, mine, got, out):
    out[...] = summed(mine, got, slice(None))


def part_kernel(place, mine, got, out, other_out):
    at = 0
    for target in (out, other_out):
        rows = target.shape[0] // 2
        target[rows_at(place[2], rows), :] = mine[at : at + rows, :]
        target[rows_at(1 - place[2], rows), :] = got[at : at + rows, :]
        at += rows


def widen_kernel(place, mine, got, other_mine, other_got, out, other_out):
    for bit, a, b, target in ((1, mine, got, out), (0, other_mine, other_got, other_out)):
        rows = a.shape[0]
        target[rows_at(place[bit], rows), :] = a[...]
        target[rows_at(1 - place[bit], rows), :] = b[...]


def finish_kernel(layouts, place, mine, got, other_mine, other_got, *outs):
    def write(layout, source):
        at = 0
        for index, rows, blocks in layout:
            out = outs[index]
            for row, column in blocks:
                out[row : row + rows, column : column + source.shape[1]] = source[at : at + rows, :].astype(F32)
                at += rows

    for bit, a, b, pair in ((0, mine, got, layouts[:2]), (1, other_mine, other_got, layouts[2:])):
        for side in range(2):

            @pl.when(place[bit] == side)
            def _():
                write(pair[0], (a, b)[side])
                write(pair[1], (b, a)[side])


class Chain:
    def __init__(self, first):
        self.last = first


class Reduction:
    def __init__(self, batch_size, chain, place, name, halves, layouts, outs):
        self.batch_size, self.chain, self.place, self.name = batch_size, chain, place, name
        self.layouts, self.outs = layouts, outs
        self.mine, send, self.other, other_send = halves
        self.by_hand = batch_size == 8
        self.got, self.other_got = self.exchange(send, 1), self.exchange(other_send, 2)

    def exchange(self, array, offset):
        return lax.ppermute(array, "batch", [(i, i ^ offset) for i in range(self.batch_size)])

    def call(self, kernel, step, out_shape, *arrays):
        count = len(arrays)

        def copied_in(place, _, *refs):
            sources, outs = refs[:count], refs[count : -count - 1]
            copies, sems = refs[-count - 1 : -1], refs[-1]
            moves = [
                pltpu.make_async_copy(source, copy, sems.at[i])
                for i, (source, copy) in enumerate(zip(sources, copies, strict=True))
            ]
            for move in moves:
                move.start()
            for move in moves:
                move.wait()
            kernel(place, *copies, *outs)

        in_vmem = pl.BlockSpec(memory_space=pltpu.VMEM)
        out = pl.pallas_call(
            copied_in,
            name=self.name + "_" + step,
            out_shape=out_shape,
            in_specs=[pl.BlockSpec(memory_space=pltpu.SMEM)] + [IN_HBM] * (count + 1),
            out_specs=jax.tree.map(lambda _: in_vmem, out_shape),
            scratch_shapes=[pltpu.VMEM(a.shape, a.dtype) for a in arrays]
            + [pltpu.SemaphoreType.DMA((count,))],
            compiler_params=pltpu.CompilerParams(vmem_limit_bytes=STEP_LIMIT),
            cost_estimate=SHORT,
        )(self.place, self.chain.last, *arrays)
        self.chain.last = out[0] if isinstance(out, (list, tuple)) else out
        return out

    def both(self):
        return self.mine, self.got, self.other, self.other_got

    def turn(self):
        if not self.by_hand:
            size = self.batch_size
            low = [[i for i in range(size) if i % 2 == side] for side in range(2)]
            high = [[i for i in range(size) if i // 2 % 2 == side] for side in range(2)]
            self.mine = lax.psum(self.mine + self.got, "batch", axis_index_groups=low)
            self.other = lax.psum(self.other + self.other_got, "batch", axis_index_groups=high)
            return
        shapes = [half_of(a) for a in (self.mine, self.mine, self.other, self.other)]
        self.mine, send, self.other, other_send = self.call(turn_kernel, "turn", shapes, *self.both())
        self.got, self.other_got = self.exchange(send, 2), self.exchange(other_send, 1)

    def join(self):
        if self.by_hand:
            rows = (self.mine.shape[0] + self.other.shape[0]) // 2
            shape = jax.ShapeDtypeStruct((rows, self.mine.shape[1]), BF16)
            self.counts = self.mine.shape[0], self.other.shape[0]
            self.joined, send = self.call(join_kernel, "join", [shape] * 2, *self.both())
            self.joined_got = self.exchange(send, 4)

    def add(self):
        if self.by_hand:
            shape = jax.ShapeDtypeStruct(self.joined.shape, BF16)
            self.joined = self.call(add_kernel, "add", shape, self.joined, self.joined_got)
            self.joined_got = self.exchange(self.joined, 4)

    def part(self):
        if self.by_hand:
            shapes = [jax.ShapeDtypeStruct((rows, self.joined.shape[1]), BF16) for rows in self.counts]
            self.mine, self.other = self.call(part_kernel, "part", shapes, self.joined, self.joined_got)
            self.got, self.other_got = self.exchange(self.mine, 2), self.exchange(self.other, 1)

    def widen(self):
        if self.by_hand:
            shapes = [jax.ShapeDtypeStruct((2 * a.shape[0], a.shape[1]), BF16) for a in (self.mine, self.other)]
            self.mine, self.other = self.call(widen_kernel, "widen", shapes, *self.both())
        self.got, self.other_got = self.exchange(self.mine, 1), self.exchange(self.other, 2)

    def finish(self):
        return self.call(
            functools.partial(finish_kernel, self.layouts), "finish", list(self.outs), *self.both()
        )


def half_of(array):
    return jax.ShapeDtypeStruct((array.shape[0] // 2, array.shape[1]), BF16)


def body(
    batch_size,
    patches,
    queries,
    cotangent,
    counts,
    masked,
    enc_gains,
    enc_shifts,
    enc_widebias,
    enc_scales,
    enc_project,
    enc_output,
    enc_expand,
    enc_reduce,
    reg_gains,
    reg_shifts,
    reg_widebias,
    reg_scales,
    reg_query,
    reg_keyval,
    reg_output,
    reg_expand,
    reg_reduce,
):
    images, band_rows, width = patches.shape
    hidden = enc_expand.shape[1]
    band = lax.axis_index("band")
    batch = lax.axis_index("batch")
    place = jnp.stack([lax.rem(batch // bit, 2) for bit in (1, 2, 4)])
    masked_all = lax.all_gather(masked.astype(F32), "band", axis=1, tiled=True)
    size = masked_all.shape[1]
    parts = size // band_rows
    part, part_hidden = width // parts, hidden // parts
    token_rows = lax.all_gather(jnp.where(masked[:, :, None] == 0, patches, queries), "band", axis=0)
    grad_rows = lax.all_gather(cotangent, "band", axis=0)

    real = lax.broadcasted_iota(jnp.int32, (images, size), 1) < counts[:, None]
    keep = jnp.where(real & (masked_all == 0), 1.0, 0.0).astype(F32)
    pick = jnp.where(real & (masked_all == 1), 1.0, 0.0).astype(F32)
    in_smem = pl.BlockSpec(memory_space=pltpu.SMEM)
    in_vmem = pl.BlockSpec(memory_space=pltpu.VMEM)
    meta, keep_place, pick_place = pl.pallas_call(
        functools.partial(plan_kernel, images),
        name="plan",
        out_shape=[
            jax.ShapeDtypeStruct((HEAD + 5 * images,), jnp.int32),
            jax.ShapeDtypeStruct((images, size), jnp.int32),
            jax.ShapeDtypeStruct((images, size), jnp.int32),
        ],
        in_specs=[in_smem, in_smem, in_vmem, in_vmem],
        out_specs=[in_smem, in_vmem, in_vmem],
        scratch_shapes=[pltpu.SMEM((5, images), jnp.int32)],
    )(counts, jnp.stack([band, place[0], place[1]]), keep, pick)

    chain = Chain(keep_place)
    weight = functools.partial(jax.ShapeDtypeStruct, dtype=F32)

    def reduction(name, halves, layouts, outs):
        return Reduction(batch_size, chain, place, name, halves, layouts, outs)

    top, pieces = part_hidden // 2, parts // 2
    ffn_layout = (
        [(0, top, [(0, 0)])],
        [(0, top, [(top, 0)])],
        [(1, part, [(0, i * width) for i in range(pieces)])],
        [(1, part, [(0, i * width) for i in range(pieces, parts)])],
    )
    ffn_outs = (weight((part_hidden, width)), weight((part, hidden)))

    def both(*arrays):
        return [("full", a) for a in arrays]

    def cut(*arrays):
        return [("bin", a) for a in arrays]

    def vm(shape, dtype=BF16):
        return pltpu.VMEM(shape, dtype)

    enc_wide = enc_widebias.reshape(1, hidden)
    reg_wide = reg_widebias.reshape(1, hidden)
    (
        x,
        triple,
        enc_totals,
        enc_normed_t,
        enc_mixed_t,
        enc_branch,
        enc_act,
        enc_slope,
        enc_middle_t,
        enc_ffn,
        pair_t,
        pair,
    ) = binned_call(
        functools.partial(enc_forward_kernel, images, parts),
        "enc_forward",
        images,
        chain,
        meta,
        both(keep_place, token_rows, enc_gains, enc_shifts, enc_wide, enc_scales, reg_gains, reg_shifts),
        (enc_project, enc_output, enc_expand, enc_reduce, reg_keyval),
        [
            ((size, width), BF16),
            ((size, 3 * width), BF16),
            ((size, LANES), F32),
            ((part, size), BF16),
            ((part, size), BF16),
            ((size, width), BF16),
            ((size, part_hidden), BF16),
            ((size, hidden), BF16),
            ((part, size), BF16),
            ((size, width), F32),
            ((part, size), BF16),
            ((size, 2 * width), BF16),
        ],
        [],
        [
            vm(enc_project.shape),
            vm(enc_output.shape),
            vm(enc_expand.shape),
            vm(enc_reduce.shape),
            vm(reg_keyval.shape),
            pltpu.SemaphoreType.DMA((5,)),
            vm((size, width), F32),
            vm((size, size), F32),
            vm((size, hidden)),
            vm((size, width)),
        ],
    )
    small_rows, extra = 8, 64
    (
        z,
        reg_query_low,
        reg_totals,
        reg_normed_t,
        reg_mixed_t,
        final_rows,
        reg_grad_mid,
        reg_small,
        reg_wide_sum,
        *reg_ffn_grads,
    ) = binned_call(
        functools.partial(reg_forward_kernel, images, parts),
        "reg_forward",
        images,
        chain,
        meta,
        both(pick_place, token_rows, grad_rows)
        + cut(pair)
        + both(reg_gains, reg_shifts, reg_wide, reg_scales),
        (reg_query, reg_output, reg_expand, reg_reduce),
        [
            ((size, width), BF16),
            ((size, width), BF16),
            ((size, LANES), F32),
            ((part, size), BF16),
            ((part, size), BF16),
            ((size, width), F32),
            ((size, width), F32),
        ],
        [
            ((small_rows, width), F32),
            ((small_rows, hidden), F32),
        ]
        + [((part_hidden // 2, width), BF16)] * 4,
        [
            vm(reg_query.shape),
            vm(reg_output.shape),
            vm(reg_expand.shape),
            vm(reg_reduce.shape),
            pltpu.SemaphoreType.DMA((4,)),
            vm((size, width), F32),
            vm((size, width), F32),
            vm((size, size), F32),
            vm((size, hidden)),
            vm((size, hidden)),
            vm((size, width)),
            vm((part, hidden), F32),
            vm((part_hidden, width), F32),
        ],
    )
    reg_ffn = reduction("reg_ffn", reg_ffn_grads, ffn_layout, ffn_outs)
    query_grad, encoded_grad, reg_attn_small, *reg_attn_grads = binned_call(
        functools.partial(reg_attention_kernel, images, parts),
        "reg_attention_grad",
        images,
        chain,
        meta,
        cut(z, reg_query_low, reg_totals, reg_normed_t, reg_mixed_t, reg_grad_mid, pair, pair_t, x, enc_branch, enc_ffn)
        + both(reg_gains, reg_scales, enc_scales),
        (reg_query, reg_keyval, reg_output),
        [((size, width), F32), ((size, width), F32)],
        [((small_rows, width), F32)] + [((part, width), BF16)] * 4,
        [
            vm(reg_query.shape),
            vm(reg_keyval.shape),
            vm(reg_output.shape),
            pltpu.SemaphoreType.DMA((3,)),
            vm((size, size), F32),
            vm((size, width)),
            vm((size, width)),
            vm((size, 2 * width)),
            vm((part, width), F32),
            vm((part, 2 * width), F32),
            vm((part, width), F32),
        ],
    )
    reg_attn = reduction(
        "reg_attention",
        reg_attn_grads,
        (
            [(0, part, [(0, 0)])],
            [(1, part, [(0, 0)])],
            [(2, part, [(0, 0)])],
            [(2, part, [(0, width)])],
        ),
        (weight((part, width)), weight((part, width)), weight((part, 2 * width))),
    )
    reg_ffn.turn()
    enc_grad_mid, enc_small, enc_wide_sum, *enc_ffn_grads = binned_call(
        functools.partial(enc_ffn_kernel, images, parts),
        "enc_ffn_grad",
        images,
        chain,
        meta,
        cut(encoded_grad, x, enc_branch, enc_ffn, enc_act, enc_slope, enc_middle_t)
        + both(enc_gains, enc_scales),
        (enc_expand, enc_reduce),
        [((size, width), F32)],
        [
            ((small_rows, width), F32),
            ((small_rows, hidden), F32),
        ]
        + [((part_hidden // 2, width), BF16)] * 4,
        [
            vm(enc_expand.shape),
            vm(enc_reduce.shape),
            pltpu.SemaphoreType.DMA((2,)),
            vm((part, hidden), F32),
            vm((part_hidden, width), F32),
        ],
    )
    enc_ffn_sum = reduction("enc_ffn", enc_ffn_grads, ffn_layout, ffn_outs)
    reg_ffn.join()
    reg_attn.turn()
    patch_grad, _, *enc_attn_grads = binned_call(
        functools.partial(enc_attention_kernel, images, parts),
        "enc_attention_grad",
        images,
        chain,
        meta,
        cut(enc_grad_mid, x, triple, enc_totals, enc_normed_t, enc_mixed_t)
        + both(enc_gains, enc_scales, reg_small, reg_attn_small, enc_small, reg_wide_sum, enc_wide_sum),
        (enc_output, enc_project),
        [((size, width), F32)],
        [((small_rows, width), F32)] + [((part + extra, width), BF16)] * 2 + [((part, width), BF16)] * 2,
        [
            vm(enc_output.shape),
            vm(enc_project.shape),
            pltpu.SemaphoreType.DMA((2,)),
            vm((size, size), F32),
            vm((size, width)),
            vm((size, 3 * width)),
            vm((part, 3 * width), F32),
            vm((part, width), F32),
        ],
    )

    enc_attn = reduction(
        "enc_attention",
        enc_attn_grads,
        (
            [(0, part, [(0, 0)]), (2, extra, [(0, 0)])],
            [(1, part, [(0, 0)])],
            [(1, part, [(0, width)])],
            [(1, part, [(0, 2 * width)])],
        ),
        (weight((part, width)), weight((part, 3 * width)), weight((extra, width))),
    )
    enc_ffn_sum.turn()
    reg_ffn.add()
    reg_attn.join()
    enc_attn.turn()
    enc_ffn_sum.join()
    reg_ffn.part()
    reg_attn.add()
    enc_attn.join()
    enc_ffn_sum.add()
    reg_ffn.widen()
    reg_attn.part()
    enc_attn.add()
    enc_ffn_sum.part()

    def own_places(places):
        mine = lax.dynamic_slice_in_dim(places, band * band_rows, band_rows, 1)
        return mine[:, :, None]

    by_image = pl.BlockSpec((None, band_rows, 1), lambda i, m: (i, 0, 0))
    bin_of_image = pl.BlockSpec((None, size, width), lambda i, m: (m[HEAD + i], 0, 0))
    image_out = pl.BlockSpec((None, band_rows, width), lambda i, m: (i, 0, 0))
    prediction, query_grad, patch_grad = pl.pallas_call(
        unpack_kernel,
        name="unpack",
        out_shape=[jax.ShapeDtypeStruct(patches.shape, F32)] * 3,
        grid_spec=pltpu.PrefetchScalarGridSpec(
            num_scalar_prefetch=1,
            grid=(images,),
            in_specs=[IN_HBM, by_image, by_image, bin_of_image, bin_of_image, bin_of_image],
            out_specs=[image_out] * 3,
        ),
        compiler_params=pltpu.CompilerParams(vmem_limit_bytes=VMEM_LIMIT),
        cost_estimate=LONG,
    )(meta, chain.last, own_places(keep_place), own_places(pick_place), final_rows, query_grad, patch_grad)

    chain.last = prediction
    reg_reduce_grad, reg_expand_grad = reg_ffn.finish()
    reg_attn.widen()
    enc_ffn_sum.widen()
    enc_attn.part()
    reg_query_grad, reg_output_grad, reg_keyval_grad = reg_attn.finish()
    enc_attn.widen()
    enc_reduce_grad, enc_expand_grad = enc_ffn_sum.finish()
    enc_output_grad, enc_project_grad, vectors = enc_attn.finish()
    reg_s, reg_a, enc_s, enc_a = jnp.split(vectors[: 4 * small_rows, :part], 4, 0)
    reg_wide_grad, enc_wide_grad = vectors[4 * small_rows], vectors[5 * small_rows]
    enc_gains_grad = jnp.stack([enc_a[3], enc_s[2]])
    enc_shifts_grad = jnp.stack([enc_a[4], enc_a[1], enc_a[2], enc_a[0], enc_s[3], enc_s[1]])
    enc_scales_grad = jnp.stack([enc_s[4], enc_s[0]])
    reg_gains_grad = jnp.stack([reg_a[3], reg_a[5], reg_s[2]])
    reg_shifts_grad = jnp.stack(
        [reg_a[4], reg_a[6], reg_a[1], reg_a[2], reg_a[0], reg_s[3], reg_s[1]]
    )
    reg_scales_grad = jnp.stack([reg_s[4], reg_s[0]])
    return (
        prediction,
        patch_grad,
        query_grad,
        enc_gains_grad,
        enc_shifts_grad,
        enc_wide_grad,
        enc_scales_grad,
        enc_project_grad,
        enc_output_grad,
        enc_expand_grad,
        enc_reduce_grad,
        reg_gains_grad,
        reg_shifts_grad,
        reg_wide_grad,
        reg_scales_grad,
        reg_query_grad,
        reg_keyval_grad,
        reg_output_grad,
        reg_expand_grad,
        reg_reduce_grad,
    )


def solution(mesh):
    token = P("batch", "band", None)
    in_specs = (token, token, token, P("batch"), P("batch", "band")) + (P(),) * 17
    by_row, by_col = P("band", None), P(None, "band")
    out_specs = (
        token,
        token,
        token,
        by_col,
        by_col,
        P("band"),
        by_col,
        by_row,
        by_row,
        by_row,
        by_row,
        by_col,
        by_col,
        P("band"),
        by_col,
        by_row,
        by_row,
        by_row,
        by_row,
        by_row,
    )
    return jax.shard_map(
        functools.partial(body, mesh.shape["batch"]),
        mesh=mesh,
        in_specs=in_specs,
        out_specs=out_specs,
        check_vma=False,
    )
```

```python
import functools

import jax
import jax.numpy as jnp
from jax import lax
from jax.experimental import pallas as pl
from jax.experimental.pallas import tpu as pltpu
from jax.sharding import PartitionSpec as P

HEADS = 12
HD = 64
EPS = 1e-06
ROOT_HALF = 0.7071067811865476
INV_ROOT_TAU = 0.3989422804014327
NEG_LARGE = -1e30
F32 = jnp.float32
BF16 = jnp.bfloat16
VMEM_LIMIT = 56 * 1024 * 1024
STEP_LIMIT = 16 * 1024 * 1024
LANES = 128
HEAD = 4


def dot(a, b):
    return lax.dot_general(a, b, (((1,), (0,)), ((), ())), preferred_element_type=F32)


def dot_nt(a, b):
    return lax.dot_general(a, b, (((1,), (1,)), ((), ())), preferred_element_type=F32)


def dot_tn(a, b):
    return lax.dot_general(a, b, (((0,), (0,)), ((), ())), preferred_element_type=F32)


def unit(values):
    row_mean = jnp.mean(values, -1, keepdims=True)
    centred = values - row_mean
    variance = jnp.mean(centred * centred, -1, keepdims=True)
    inv_std = lax.rsqrt(variance + EPS)
    return centred * inv_std, inv_std


def unit_back(grad_out, unit_rows, inv_std, gain):
    scaled = grad_out * gain
    first_term = jnp.mean(scaled, -1, keepdims=True)
    second_term = jnp.mean(scaled * unit_rows, -1, keepdims=True)
    return inv_std * (scaled - first_term - unit_rows * second_term)


def rows_sum(values):
    return jnp.sum(values, 0, keepdims=True)


def gate_and_slope(pre_act):
    bell = 0.5 * (1.0 + lax.erf(pre_act * ROOT_HALF))
    slope = bell + pre_act * INV_ROOT_TAU * jnp.exp(-0.5 * pre_act * pre_act)
    return (pre_act * bell).astype(BF16), slope.astype(BF16)


def relative_order(parts):
    order, offset = [0], parts // 2
    while offset:
        order, offset = order + [a ^ offset for a in order], offset // 2
    return order


class Meta:
    def __init__(self, ref, images):
        self.ref, self.images = ref, images

    def bins(self):
        return self.ref[0]

    def band(self):
        return self.ref[1]

    def bits(self):
        return self.ref[2], self.ref[3]

    def bin_of(self, image):
        return self.ref[HEAD + image]

    def keep_off(self, image):
        return self.ref[HEAD + self.images + image]

    def keep_count(self, image):
        return self.ref[HEAD + 2 * self.images + image]

    def pick_off(self, image):
        return self.ref[HEAD + 3 * self.images + image]

    def pick_count(self, image):
        return self.ref[HEAD + 4 * self.images + image]

    def count(self, image):
        return self.ref[HEAD + 5 * self.images + image]

    def segments(self, bin_now, kind, shape, dim, blank):
        rows = lax.broadcasted_iota(jnp.int32, shape, dim)
        owner = jnp.full(shape, blank, jnp.int32)
        for image in range(self.images):
            start = self.keep_off(image) if kind == "keep" else self.pick_off(image)
            count = self.keep_count(image) if kind == "keep" else self.pick_count(image)
            stop = start + jnp.where(self.bin_of(image) == bin_now, count, 0)
            owner = jnp.where((rows >= start) & (rows < stop), image, owner)
        return owner


def key_mask(meta, bin_now, query_kind, size, key_dim):
    along = ((size, 1), (1, size))
    query_owner = meta.segments(bin_now, query_kind, along[1 - key_dim], 1 - key_dim, -2)
    key_owner = meta.segments(bin_now, "keep", along[key_dim], key_dim, -1)
    return query_owner == key_owner


def quarter_rows(meta, width, parts):
    part = width // parts
    row = lax.broadcasted_iota(jnp.int32, (part, width), 0) + meta.band() * part
    return (row == lax.broadcasted_iota(jnp.int32, (part, width), 1)).astype(BF16)


def lower_half():
    return lax.broadcasted_iota(jnp.int32, (1, LANES), 1) < HD


def pair_cols(pair, first=0):
    at = first + pair * LANES
    return pl.ds(at if isinstance(at, int) else pl.multiple_of(at, LANES), LANES)


def each_pair(one_pair, together):
    steps = HEADS // 2 // together

    def step(index, _):
        for pair in range(together):
            one_pair(index * together + pair)
        return 0

    if steps == 1:
        step(0, 0)
    else:
        lax.fori_loop(0, steps, step, 0)


def attend_forward(query_of, key_of, value_of, mask_ref, mixed_ref, totals_ref):
    low = lower_half()
    sides = (low.astype(BF16), (~low).astype(BF16))
    lane = lax.broadcasted_iota(jnp.int32, totals_ref.shape, 1)
    totals_ref[...] = jnp.zeros_like(totals_ref)

    def one_pair(pair):
        query, key, value = query_of(pair), key_of(pair), value_of(pair)
        mixed = []
        for side in range(2):
            scores = dot_nt(query, key * sides[side]) * HD ** (-0.5)
            scores = jnp.where(mask_ref[...] > 0, scores, NEG_LARGE)
            top = jnp.max(scores, -1, keepdims=True)
            exp_scores = jnp.exp(scores - top)
            total = jnp.sum(exp_scores, -1, keepdims=True)
            weights = (exp_scores * (1.0 / total)).astype(BF16)
            totals_ref[...] = jnp.where(lane == 2 * pair + side, top + jnp.log(total), totals_ref[...])
            mixed.append(dot(weights, value))
        mixed_ref[:, pair_cols(pair)] = jnp.where(low, mixed[0], mixed[1]).astype(BF16)

    each_pair(one_pair, 6)


def attend_backward(query_of, key_of, value_of, grad_of, totals_ref, mask_ref, store):
    low = lower_half()
    sides = (low.astype(BF16), (~low).astype(BF16))

    def one_pair(pair):
        query, key, value, grad = query_of(pair), key_of(pair), value_of(pair), grad_of(pair)
        grad_query, grad_key, grad_value = [], [], []
        for side in range(2):
            scores = dot_nt(key * sides[side], query) * HD ** (-0.5)
            scores = jnp.where(mask_ref[...] > 0, scores, NEG_LARGE)
            probs = jnp.exp(scores - totals_ref[pl.ds(2 * pair + side, 1), :])
            grad_value.append(dot(probs.astype(BF16), grad))
            grad_probs = dot_nt(value * sides[side], grad)
            inner = jnp.sum(grad_probs * probs, 0, keepdims=True)
            grad_scores = (probs * (grad_probs - inner)).astype(BF16)
            grad_query.append(dot_tn(key, grad_scores)[side * HD : (side + 1) * HD, :])
            grad_key.append(dot(grad_scores, query))
        store(
            pair,
            jnp.concatenate(grad_query, 0).T * HD ** (-0.5),
            jnp.where(low, grad_key[0], grad_key[1]) * HD ** (-0.5),
            jnp.where(low, grad_value[0], grad_value[1]),
        )

    each_pair(one_pair, 6)


def pack_rows(meta, bin_now, place_ref, gathered, packed, size, by_block):
    packed[...] = jnp.zeros_like(packed)
    parts = len(gathered)
    slots = size // parts

    def add(image, blocks):
        taken = slice(blocks[0] * slots, (blocks[-1] + 1) * slots)
        shape = (size, len(blocks) * slots)
        row = lax.broadcasted_iota(jnp.int32, shape, 0)
        chosen = (row == place_ref[image : image + 1, taken]).astype(BF16)
        packed[...] += dot(chosen, jnp.concatenate([gathered[j][image] for j in blocks], 0))

    for image in range(meta.images):

        @pl.when(meta.bin_of(image) == bin_now)
        def _():
            if not by_block:
                add(image, range(parts))
                return
            for j, offset in enumerate(relative_order(parts)):
                pl.when(meta.count(image) > (meta.band() ^ offset) * slots)(functools.partial(add, image, [j]))


class Weights:
    def __init__(self, sources, targets, sems):
        self.copies = [
            pltpu.make_async_copy(source, target, sems.at[i])
            for i, (source, target) in enumerate(zip(sources, targets, strict=True))
        ]

    def start(self):
        @pl.when(pl.program_id(0) == 0)
        def _():
            for copy in self.copies:
                copy.start()

    def wait(self, index):
        @pl.when(pl.program_id(0) == 0)
        def _():
            self.copies[index].wait()


def add_row(small_ref, row, values):
    small_ref[row : row + 1, :] += values


def first_step(refs):
    @pl.when(pl.program_id(0) == 0)
    def _():
        for ref in refs:
            ref[...] = jnp.zeros_like(ref)


def split_rows(total):
    unit = 128
    return (total // 2 + unit - 1) // unit * unit


def cut_blocks(blocks, start, stop):
    at, cut = 0, []
    for rows, tag in blocks:
        low, high = max(at, start), min(at + rows, stop)
        if low < high:
            cut.append((tag, low - at, high - low, low - start))
        at += rows
    return cut


def quarters_of(blocks):
    total = sum(rows for rows, _ in blocks)
    first = split_rows(total)
    edges = (0, first // 2, first, first + (total - first) // 2, total)
    return [cut_blocks(blocks, a, b) for a, b in zip(edges, edges[1:], strict=False)]


def group_shapes(total, width):
    first = split_rows(total)
    return [((rows // 2, width), BF16) for rows in (first, first, total - first, total - first)]


def write_group(meta, blocks, width, outs):
    quarters = quarters_of(blocks)

    def write(cuts, out):
        for (ref, column), row, rows, at in cuts:
            values = ref[row : row + rows, column : column + width]
            out[at : at + rows, :] = values.astype(BF16)

    for bit, pair, (keep_out, send_out) in ((0, quarters[:2], outs[:2]), (1, quarters[2:], outs[2:])):
        for side in range(2):

            @pl.when(meta.bits()[bit] == side)
            def _():
                write(pair[side], keep_out)
                write(pair[1 - side], send_out)


def column_blocks(ref, width):
    return [(ref.shape[0], (ref, column)) for column in range(0, ref.shape[1], width)]


def last_step(meta, write):
    @pl.when(pl.program_id(0) == meta.bins() - 1)
    def _():
        write()


def choose_kernel(masked_ref, column_ref, patches_ref, queries_ref, tokens_out, flags_out):
    flags_out[...] = masked_ref[...].astype(F32)
    for image in range(tokens_out.shape[0]):
        tokens_out[image] = jnp.where(column_ref[image] == 0, patches_ref[image], queries_ref[image])


def hold_kernel(_, source, out):
    out[...] = source[...]


def plan_kernel(
    images,
    counts_ref,
    band_ref,
    keep_ref,
    pick_ref,
    meta_ref,
    keep_place_ref,
    pick_place_ref,
    words,
):
    size = keep_ref.shape[1]
    before = (
        lax.broadcasted_iota(jnp.int32, (size, size), 0)
        <= lax.broadcasted_iota(jnp.int32, (size, size), 1)
    ).astype(BF16)
    keep, pick = keep_ref[...], pick_ref[...]
    keep_rank = dot(keep.astype(BF16), before).astype(jnp.int32) - 1
    pick_rank = dot(pick.astype(BF16), before).astype(jnp.int32) - 1
    for image in range(images):
        meta_ref[HEAD + 5 * images + image] = counts_ref[image]
        words[0, image] = jnp.sum(keep[image : image + 1, :]).astype(jnp.int32)
        words[1, image] = jnp.sum(pick[image : image + 1, :]).astype(jnp.int32)
        for row in (2, 3, 4):
            words[row, image] = 0

    def place(_, bins):
        def largest(image, best):
            open_now = words[4, image] == 0
            better = open_now & ((best < 0) | (counts_ref[image] > counts_ref[jnp.maximum(best, 0)]))
            return jnp.where(better, image, best)

        image = lax.fori_loop(0, images, largest, jnp.int32(-1))
        keep_count, pick_count = words[0, image], words[1, image]

        def first_fit(step, best):
            bin_now = images - 1 - step
            fits = (words[2, bin_now] + keep_count <= size) & (words[3, bin_now] + pick_count <= size)
            return jnp.where(fits, bin_now, best)

        bin_now = lax.fori_loop(0, images, first_fit, jnp.int32(0))
        meta_ref[HEAD + image] = bin_now
        meta_ref[HEAD + images + image] = words[2, bin_now]
        meta_ref[HEAD + 2 * images + image] = keep_count
        meta_ref[HEAD + 3 * images + image] = words[3, bin_now]
        meta_ref[HEAD + 4 * images + image] = pick_count
        words[2, bin_now] = words[2, bin_now] + keep_count
        words[3, bin_now] = words[3, bin_now] + pick_count
        words[4, image] = 1
        return jnp.maximum(bins, bin_now + 1)

    meta_ref[0] = lax.fori_loop(0, images, place, jnp.int32(0))
    meta_ref[1] = band_ref[0]
    meta_ref[2] = band_ref[1]
    meta_ref[3] = band_ref[2]
    for image in range(images):
        row = slice(image, image + 1)
        keep_place_ref[row, :] = jnp.where(
            keep[row, :] > 0, keep_rank[row, :] + meta_ref[HEAD + images + image], -1
        )
        pick_place_ref[row, :] = jnp.where(
            pick[row, :] > 0, pick_rank[row, :] + meta_ref[HEAD + 3 * images + image], -1
        )


def ffn_forward(normed, expand, wide_bias, reduce_weight, act_ref, slope_ref, width):
    total = None
    for start in range(0, expand.shape[1], width):
        cols = slice(start, start + width)
        act, slope = gate_and_slope(dot(normed, expand[:, cols]) + wide_bias[:, cols])
        act_ref[:, cols] = act
        slope_ref[:, cols] = slope
        part = dot(act, reduce_weight[cols, :])
        total = part if total is None else total + part
    return total


def ffn_backward(grad_low, slope_ref, normed_part, expand, reduce_weight, expand_acc, wide_ref, width):
    total = None
    for start in range(0, expand.shape[1], width):
        cols = slice(start, start + width)
        grad_act = dot_nt(grad_low, reduce_weight[cols, :])
        grad_pre = grad_act * slope_ref[:, cols].astype(F32)
        grad_pre_low = grad_pre.astype(BF16)
        wide_ref[0:1, cols] += rows_sum(grad_pre_low.astype(F32))
        expand_acc[:, cols] += dot(normed_part, grad_pre_low)
        part = dot_nt(grad_pre_low, expand[:, cols])
        total = part if total is None else total + part
    return total


def enc_forward_kernel(
    images,
    parts,
    meta_ref,
    place_ref,
    *refs,
):
    row_refs = refs[:parts]
    enc_forward(images, parts, meta_ref, place_ref, row_refs, *refs[parts:])


def enc_forward(
    images,
    parts,
    meta_ref,
    place_ref,
    row_refs,
    gains,
    shifts,
    wide_bias,
    scales,
    reg_gains,
    reg_shifts,
    project_hbm,
    output_hbm,
    expand_hbm,
    reduce_hbm,
    keyval_hbm,
    x_out,
    triple_out,
    totals_out,
    normed_t_out,
    mixed_t_out,
    branch_out,
    act_out,
    slope_out,
    middle_t_out,
    ffn_out,
    pair_t_out,
    pair_out,
    project,
    output,
    expand,
    reduce_weight,
    keyval,
    sems,
    packed,
    mask_ref,
    act_all,
    mixed_ref,
):
    meta = Meta(meta_ref, images)
    bin_now = pl.program_id(0)
    weights = Weights(
        (project_hbm, output_hbm, expand_hbm, reduce_hbm, keyval_hbm),
        (project, output, expand, reduce_weight, keyval),
        sems,
    )
    weights.start()
    size, width = packed.shape
    pack_rows(meta, bin_now, place_ref, row_refs, packed, size, True)
    mask_ref[...] = key_mask(meta, bin_now, "keep", size, 1).astype(F32)
    part_of = quarter_rows(meta, width, parts)
    x = packed[...]
    x_out[...] = x.astype(BF16)
    unit_rows, _ = unit(x)
    normed = (unit_rows * gains[0:1, :] + shifts[0:1, :]).astype(BF16)
    normed_t_out[...] = dot_nt(part_of, normed).astype(BF16)
    weights.wait(0)
    triple_out[:, :width] = (dot(normed, project[:, :width]) + shifts[1:2, :]).astype(BF16)
    triple_out[:, width : 2 * width] = dot(normed, project[:, width : 2 * width]).astype(BF16)
    triple_out[:, 2 * width :] = (dot(normed, project[:, 2 * width :]) + shifts[2:3, :]).astype(BF16)

    attend_forward(
        lambda pair: triple_out[:, pair_cols(pair)],
        lambda pair: triple_out[:, pair_cols(pair, width)],
        lambda pair: triple_out[:, pair_cols(pair, 2 * width)],
        mask_ref,
        mixed_ref,
        totals_out,
    )
    mixed = mixed_ref[...]
    mixed_t_out[...] = dot_nt(part_of, mixed).astype(BF16)
    weights.wait(1)
    branch = (dot(mixed, output[...]) + shifts[3:4, :]).astype(BF16)
    branch_out[...] = branch
    middle = x + scales[0:1, :] * branch.astype(F32)
    unit_rows, _ = unit(middle)
    normed = (unit_rows * gains[1:2, :] + shifts[4:5, :]).astype(BF16)
    middle_t_out[...] = dot_nt(part_of, normed).astype(BF16)
    weights.wait(2)
    weights.wait(3)
    part_width = expand.shape[1] // parts
    ffn = ffn_forward(normed, expand, wide_bias, reduce_weight, act_all, slope_out, part_width) + shifts[5:6, :]
    act_out[...] = act_all[:, pl.ds(pl.multiple_of(meta.band() * part_width, part_width), part_width)]
    ffn_out[...] = ffn
    encoded = middle + scales[1:2, :] * ffn
    unit_rows, _ = unit(encoded)
    pair_normed = (unit_rows * reg_gains[1:2, :] + reg_shifts[1:2, :]).astype(BF16)
    pair_t_out[...] = dot_nt(part_of, pair_normed).astype(BF16)
    weights.wait(4)
    pair_out[:, :width] = dot(pair_normed, keyval[:, :width]).astype(BF16)
    pair_out[:, width:] = (dot(pair_normed, keyval[:, width:]) + reg_shifts[3:4, :]).astype(BF16)


def reg_forward_kernel(
    images,
    parts,
    meta_ref,
    place_ref,
    *refs,
):
    row_refs, refs = refs[:parts], refs[parts:]
    reg_forward(images, parts, meta_ref, place_ref, row_refs, *refs)


def reg_forward(
    images,
    parts,
    meta_ref,
    place_ref,
    row_refs,
    pair_ref,
    gains,
    shifts,
    wide_bias,
    scales,
    query_hbm,
    output_hbm,
    expand_hbm,
    reduce_hbm,
    grad_hbm,
    x_out,
    query_out,
    totals_out,
    normed_t_out,
    mixed_t_out,
    final_out,
    grad_mid_out,
    small_out,
    wide_out,
    out_0,
    out_1,
    out_2,
    out_3,
    query_weight,
    output,
    expand,
    reduce_weight,
    sems,
    packed,
    packed_grad,
    mask_ref,
    act_all,
    slope_all,
    mixed_ref,
    expand_acc,
    reduce_acc,
    grad_rows,
):
    meta = Meta(meta_ref, images)
    bin_now = pl.program_id(0)
    relative = relative_order(parts)
    weights = Weights(
        (query_hbm, output_hbm, expand_hbm, reduce_hbm) + tuple(grad_hbm.at[meta.band() ^ i] for i in relative),
        (query_weight, output, expand, reduce_weight) + tuple(grad_rows.at[i] for i in range(parts)),
        sems,
    )
    weights.start()
    first_step((small_out, wide_out, expand_acc, reduce_acc))
    size, width = packed.shape
    pack_rows(meta, bin_now, place_ref, row_refs, packed, size, False)
    mask_ref[...] = key_mask(meta, bin_now, "pick", size, 1).astype(F32)
    part_of = quarter_rows(meta, width, parts)
    z = packed[...]
    x_out[...] = z.astype(BF16)
    unit_rows, _ = unit(z)
    normed = (unit_rows * gains[0:1, :] + shifts[0:1, :]).astype(BF16)
    normed_t_out[...] = dot_nt(part_of, normed).astype(BF16)
    weights.wait(0)
    query_out[...] = (dot(normed, query_weight[...]) + shifts[2:3, :]).astype(BF16)

    attend_forward(
        lambda pair: query_out[:, pair_cols(pair)],
        lambda pair: pair_ref[:, pair_cols(pair)],
        lambda pair: pair_ref[:, pair_cols(pair, width)],
        mask_ref,
        mixed_ref,
        totals_out,
    )
    mixed = mixed_ref[...]
    mixed_t_out[...] = dot_nt(part_of, mixed).astype(BF16)
    weights.wait(1)
    branch = (dot(mixed, output[...]) + shifts[4:5, :]).astype(BF16).astype(F32)
    middle = z + scales[0:1, :] * branch
    unit_rows, inv_std = unit(middle)
    normed = (unit_rows * gains[2:3, :] + shifts[5:6, :]).astype(BF16)
    normed_part = dot_nt(part_of, normed).astype(BF16)
    weights.wait(2)
    weights.wait(3)
    part_width = expand.shape[1] // parts
    ffn = ffn_forward(normed, expand, wide_bias, reduce_weight, act_all, slope_all, part_width) + shifts[6:7, :]
    final_out[...] = middle + scales[1:2, :] * ffn
    for i in range(parts):
        weights.wait(4 + i)
    pack_rows(
        meta, bin_now, place_ref, [grad_rows.at[i] for i in range(parts)], packed_grad, size, False
    )
    grad_final = packed_grad[...]
    add_row(small_out, 0, rows_sum(grad_final * ffn))
    grad_low = (scales[1:2, :] * grad_final).astype(BF16)
    add_row(small_out, 1, rows_sum(grad_low.astype(F32)))
    act_part = act_all[:, pl.ds(pl.multiple_of(meta.band() * part_width, part_width), part_width)]
    reduce_acc[...] += dot_tn(act_part, grad_low)
    grad_normed = ffn_backward(
        grad_low, slope_all, normed_part, expand, reduce_weight, expand_acc, wide_out, part_width
    )
    add_row(small_out, 2, rows_sum(grad_normed * unit_rows))
    add_row(small_out, 3, rows_sum(grad_normed))
    grad_mid = grad_final + unit_back(grad_normed, unit_rows, inv_std, gains[2:3, :])
    grad_mid_out[...] = grad_mid
    add_row(small_out, 4, rows_sum(grad_mid * branch))

    blocks = column_blocks(reduce_acc, width) + column_blocks(expand_acc, width)
    last_step(meta, lambda: write_group(meta, blocks, width, (out_0, out_1, out_2, out_3)))


def reg_attention_kernel(
    images,
    parts,
    meta_ref,
    z_ref,
    query_ref,
    totals_ref,
    normed_t_ref,
    mixed_t_ref,
    grad_mid_ref,
    pair_ref,
    pair_t_ref,
    x_ref,
    enc_branch_ref,
    enc_ffn_ref,
    gains,
    scales,
    enc_scales,
    query_hbm,
    keyval_hbm,
    output_hbm,
    query_grad_out,
    encoded_grad_out,
    small_out,
    out_0,
    out_1,
    out_2,
    out_3,
    query_weight,
    keyval,
    output,
    sems,
    mask_ref,
    mixed_grad_ref,
    query_back,
    pair_back,
    query_acc,
    pair_acc,
    output_acc,
    totals_rows,
):
    meta = Meta(meta_ref, images)
    bin_now = pl.program_id(0)
    weights = Weights((output_hbm, query_hbm, keyval_hbm), (output, query_weight, keyval), sems)
    weights.start()
    first_step((small_out, query_acc, pair_acc, output_acc))
    size, width = mixed_grad_ref.shape
    mask_ref[...] = key_mask(meta, bin_now, "pick", size, 0).astype(F32)
    grad_mid = grad_mid_ref[...]
    branch_grad = (scales[0:1, :] * grad_mid).astype(BF16)
    output_acc[...] += dot(mixed_t_ref[...], branch_grad)
    add_row(small_out, 0, rows_sum(branch_grad.astype(F32)))
    weights.wait(0)
    mixed_grad_ref[...] = dot_nt(branch_grad, output[...]).astype(BF16)

    def store(pair, grad_query, grad_key, grad_value):
        query_back[:, pair_cols(pair)] = grad_query.astype(BF16)
        pair_back[:, pair_cols(pair)] = grad_key.astype(BF16)
        pair_back[:, pair_cols(pair, width)] = grad_value.astype(BF16)

    totals_rows[...] = totals_ref[...].T
    attend_backward(
        lambda pair: query_ref[:, pair_cols(pair)],
        lambda pair: pair_ref[:, pair_cols(pair)],
        lambda pair: pair_ref[:, pair_cols(pair, width)],
        lambda pair: mixed_grad_ref[:, pair_cols(pair)],
        totals_rows,
        mask_ref,
        store,
    )
    grad_query, grad_pair = query_back[...], pair_back[...]
    query_acc[...] += dot(normed_t_ref[...], grad_query)
    pair_acc[...] += dot(pair_t_ref[...], grad_pair)
    add_row(small_out, 1, rows_sum(grad_query.astype(F32)))
    add_row(small_out, 2, rows_sum(grad_pair[:, width:].astype(F32)))
    weights.wait(1)
    query_side = dot_nt(grad_query, query_weight[...]).astype(BF16).astype(F32)
    weights.wait(2)
    pair_side = dot_nt(grad_pair, keyval[...]).astype(BF16).astype(F32)
    unit_rows, inv_std = unit(z_ref[...].astype(F32))
    add_row(small_out, 3, rows_sum(query_side * unit_rows))
    add_row(small_out, 4, rows_sum(query_side))
    query_grad_out[...] = grad_mid + unit_back(query_side, unit_rows, inv_std, gains[0:1, :])
    encoded = (
        x_ref[...].astype(F32)
        + enc_scales[0:1, :] * enc_branch_ref[...].astype(F32)
        + enc_scales[1:2, :] * enc_ffn_ref[...]
    )
    unit_rows, inv_std = unit(encoded)
    add_row(small_out, 5, rows_sum(pair_side * unit_rows))
    add_row(small_out, 6, rows_sum(pair_side))
    encoded_grad_out[...] = unit_back(pair_side, unit_rows, inv_std, gains[1:2, :])

    blocks = [block for ref in (query_acc, output_acc, pair_acc) for block in column_blocks(ref, width)]
    last_step(meta, lambda: write_group(meta, blocks, width, (out_0, out_1, out_2, out_3)))


def enc_ffn_kernel(
    images,
    parts,
    meta_ref,
    encoded_grad_ref,
    x_ref,
    branch_ref,
    ffn_ref,
    act_ref,
    slope_ref,
    middle_t_ref,
    gains,
    scales,
    expand_hbm,
    reduce_hbm,
    grad_mid_out,
    small_out,
    wide_out,
    out_0,
    out_1,
    out_2,
    out_3,
    expand,
    reduce_weight,
    sems,
    expand_acc,
    reduce_acc,
):
    meta = Meta(meta_ref, images)
    weights = Weights((reduce_hbm, expand_hbm), (reduce_weight, expand), sems)
    weights.start()
    first_step((small_out, wide_out, expand_acc, reduce_acc))
    width = x_ref.shape[1]
    encoded_grad = encoded_grad_ref[...]
    add_row(small_out, 0, rows_sum(encoded_grad * ffn_ref[...]))
    grad_low = (scales[1:2, :] * encoded_grad).astype(BF16)
    add_row(small_out, 1, rows_sum(grad_low.astype(F32)))
    reduce_acc[...] += dot_tn(act_ref[...], grad_low)
    weights.wait(0)
    weights.wait(1)
    part_width = expand.shape[1] // parts
    grad_normed = ffn_backward(
        grad_low, slope_ref, middle_t_ref[...], expand, reduce_weight, expand_acc, wide_out, part_width
    )
    branch = branch_ref[...].astype(F32)
    unit_rows, inv_std = unit(x_ref[...].astype(F32) + scales[0:1, :] * branch)
    add_row(small_out, 2, rows_sum(grad_normed * unit_rows))
    add_row(small_out, 3, rows_sum(grad_normed))
    grad_mid = encoded_grad + unit_back(grad_normed, unit_rows, inv_std, gains[1:2, :])
    grad_mid_out[...] = grad_mid
    add_row(small_out, 4, rows_sum(grad_mid * branch))

    blocks = column_blocks(reduce_acc, width) + column_blocks(expand_acc, width)
    last_step(meta, lambda: write_group(meta, blocks, width, (out_0, out_1, out_2, out_3)))


def enc_attention_kernel(
    images,
    parts,
    meta_ref,
    grad_mid_ref,
    x_ref,
    triple_ref,
    totals_ref,
    normed_t_ref,
    mixed_t_ref,
    gains,
    scales,
    reg_small,
    reg_attn_small,
    enc_small,
    reg_wide,
    enc_wide,
    output_hbm,
    project_hbm,
    patch_grad_out,
    small_out,
    out_0,
    out_1,
    out_2,
    out_3,
    output,
    project,
    sems,
    mask_ref,
    mixed_grad_ref,
    triple_back,
    project_acc,
    output_acc,
    totals_rows,
    vectors,
):
    meta = Meta(meta_ref, images)
    bin_now = pl.program_id(0)
    weights = Weights((output_hbm, project_hbm), (output, project), sems)
    weights.start()
    first_step((small_out, project_acc, output_acc))
    size, width = mixed_grad_ref.shape
    mask_ref[...] = key_mask(meta, bin_now, "keep", size, 0).astype(F32)
    grad_mid = grad_mid_ref[...]
    branch_grad = (scales[0:1, :] * grad_mid).astype(BF16)
    output_acc[...] += dot(mixed_t_ref[...], branch_grad)
    add_row(small_out, 0, rows_sum(branch_grad.astype(F32)))
    weights.wait(0)
    mixed_grad_ref[...] = dot_nt(branch_grad, output[...]).astype(BF16)

    def store(pair, grad_query, grad_key, grad_value):
        triple_back[:, pair_cols(pair)] = grad_query.astype(BF16)
        triple_back[:, pair_cols(pair, width)] = grad_key.astype(BF16)
        triple_back[:, pair_cols(pair, 2 * width)] = grad_value.astype(BF16)

    totals_rows[...] = totals_ref[...].T
    attend_backward(
        lambda pair: triple_ref[:, pair_cols(pair)],
        lambda pair: triple_ref[:, pair_cols(pair, width)],
        lambda pair: triple_ref[:, pair_cols(pair, 2 * width)],
        lambda pair: mixed_grad_ref[:, pair_cols(pair)],
        totals_rows,
        mask_ref,
        store,
    )
    back = triple_back[...]
    project_acc[...] += dot(normed_t_ref[...], back)
    add_row(small_out, 1, rows_sum(back[:, :width].astype(F32)))
    add_row(small_out, 2, rows_sum(back[:, 2 * width :].astype(F32)))
    weights.wait(1)
    rows_grad = dot_nt(back, project[...]).astype(BF16).astype(F32)
    unit_rows, inv_std = unit(x_ref[...].astype(F32))
    add_row(small_out, 3, rows_sum(rows_grad * unit_rows))
    add_row(small_out, 4, rows_sum(rows_grad))
    patch_grad_out[...] = grad_mid + unit_back(rows_grad, unit_rows, inv_std, gains[0:1, :])

    def write():
        part_of = quarter_rows(meta, width, parts)
        part = part_of.shape[0]
        vectors[...] = jnp.zeros_like(vectors)
        at = 0
        for small in (reg_small, reg_attn_small, enc_small, small_out):
            rows = small.shape[0]
            vectors[at : at + rows, :part] = dot_nt(small[...].astype(BF16), part_of)
            at += rows
        mine = pl.ds(pl.multiple_of(meta.band() * width, width), width)
        vectors[at : at + 8, :] = reg_wide[:, mine]
        vectors[at + 8 : at + 16, :] = enc_wide[:, mine]
        blocks = [block for ref in (vectors, output_acc, project_acc) for block in column_blocks(ref, width)]
        write_group(meta, blocks, width, (out_0, out_1, out_2, out_3))

    last_step(meta, write)


def unpack_kernel(meta_ref, _, keep_place, pick_place, final_ref, query_grad_ref, patch_grad_ref, final_out, query_grad_out, patch_grad_out):
    rows = keep_place.shape[0]
    size = final_ref.shape[0]
    lane = lax.broadcasted_iota(jnp.int32, (rows, size), 1)
    kept = (keep_place[...] == lane).astype(BF16)
    picked = (pick_place[...] == lane).astype(BF16)
    for chosen, source, target in (
        (picked, final_ref, final_out),
        (picked, query_grad_ref, query_grad_out),
        (kept, patch_grad_ref, patch_grad_out),
    ):
        values = source[...]
        high = values.astype(BF16)
        rest = (values - high.astype(F32)).astype(BF16)
        target[...] = dot(chosen, high) + dot(chosen, rest)


def whole(array):
    return pl.BlockSpec(array.shape, lambda *_: (0,) * array.ndim)


def by_bin(shape):
    return pl.BlockSpec((None,) + tuple(shape), lambda b, meta: (jnp.minimum(b, meta[0] - 1), 0, 0))


def for_used_bins(kernel):
    def guarded(meta_ref, _, *refs):
        @pl.when(pl.program_id(0) < meta_ref[0])
        def _():
            kernel(meta_ref, *refs)

    return guarded


IN_HBM = pl.BlockSpec(memory_space=pl.ANY)
SHORT = pl.CostEstimate(flops=2_000_000_000, bytes_accessed=1_000_000, transcendentals=0)
LONG = pl.CostEstimate(flops=20_000_000_000, bytes_accessed=10_000_000, transcendentals=0)


def binned_call(kernel, name, images, chain, meta, binned, hbm, binned_outs, full_outs, scratch):
    operands = [meta, chain.last] + [a for _, a in binned] + list(hbm)
    in_specs = [IN_HBM] + [whole(a) if kind == "full" else by_bin(a.shape[1:]) for kind, a in binned]
    in_specs += [IN_HBM] * len(hbm)
    out_shape = [jax.ShapeDtypeStruct((images,) + s, t) for s, t in binned_outs]
    out_shape += [jax.ShapeDtypeStruct(s, t) for s, t in full_outs]
    out_specs = [by_bin(s) for s, _ in binned_outs]
    out_specs += [pl.BlockSpec(s, lambda *_: (0, 0)) for s, _ in full_outs]
    outs = pl.pallas_call(
        for_used_bins(kernel),
        name=name,
        out_shape=out_shape,
        grid_spec=pltpu.PrefetchScalarGridSpec(
            num_scalar_prefetch=1,
            grid=(images,),
            in_specs=in_specs,
            out_specs=out_specs,
            scratch_shapes=scratch,
        ),
        compiler_params=pltpu.CompilerParams(
            vmem_limit_bytes=VMEM_LIMIT, dimension_semantics=("arbitrary",)
        ),
        cost_estimate=LONG,
    )(*operands)
    chain.last = outs[-1]
    return outs


def summed(mine, got, at):
    return (mine[at, :].astype(F32) + got[at, :].astype(F32)).astype(BF16)


def rows_at(index, rows):
    return pl.ds(pl.multiple_of(index * rows, rows), rows)


def turn_kernel(place, mine, got, other_mine, other_got, own, send, other_own, other_send):
    for bit, a, b, keep, out in ((1, mine, got, own, send), (0, other_mine, other_got, other_own, other_send)):
        rows = keep.shape[0]
        keep[...] = summed(a, b, rows_at(place[bit], rows))
        out[...] = summed(a, b, rows_at(1 - place[bit], rows))


def join_kernel(place, mine, got, other_mine, other_got, own, send):
    at = 0
    for a, b in ((mine, got), (other_mine, other_got)):
        rows = a.shape[0] // 2
        own[at : at + rows, :] = summed(a, b, rows_at(place[2], rows))
        send[at : at + rows, :] = summed(a, b, rows_at(1 - place[2], rows))
        at += rows


def add_kernel(place, mine, got, out):
    out[...] = summed(mine, got, slice(None))


def part_kernel(place, mine, got, out, other_out):
    at = 0
    for target in (out, other_out):
        rows = target.shape[0] // 2
        target[rows_at(place[2], rows), :] = mine[at : at + rows, :]
        target[rows_at(1 - place[2], rows), :] = got[at : at + rows, :]
        at += rows


def widen_kernel(place, mine, got, other_mine, other_got, out, other_out):
    for bit, a, b, target in ((1, mine, got, out), (0, other_mine, other_got, other_out)):
        rows = a.shape[0]
        target[rows_at(place[bit], rows), :] = a[...]
        target[rows_at(1 - place[bit], rows), :] = b[...]


def finish_kernel(quarters, vectors, place, mine, got, other_mine, other_got, *outs):
    def write(cuts, source):
        for tag, row, rows, at in cuts:
            values = source[at : at + rows, :].astype(F32)
            if tag != "vectors":
                index, column = tag
                outs[index][row : row + rows, column : column + source.shape[1]] = values
                continue
            for index, taken, columns in vectors:
                for to, one in enumerate(taken):
                    outs[index][to : to + 1, :] = values[one : one + 1, :columns]

    for bit, a, b, pair in ((0, mine, got, quarters[:2]), (1, other_mine, other_got, quarters[2:])):
        for side in range(2):

            @pl.when(place[bit] == side)
            def _():
                write(pair[0], (a, b)[side])
                write(pair[1], (b, a)[side])


class Chain:
    def __init__(self, first):
        self.last = first


class Reduction:
    def __init__(self, batch_size, chain, place, name, halves, blocks, outs, vectors=()):
        self.batch_size, self.chain, self.place, self.name = batch_size, chain, place, name
        self.quarters, self.outs, self.vectors = quarters_of(blocks), outs, vectors
        self.mine, send, self.other, other_send = halves
        self.by_hand = batch_size == 8
        self.got, self.other_got = self.exchange(send, 1), self.exchange(other_send, 2)

    def exchange(self, array, offset):
        return lax.ppermute(array, "batch", [(i, i ^ offset) for i in range(self.batch_size)])

    def call(self, kernel, step, out_shape, *arrays):
        count = len(arrays)

        def copied_in(place, _, *refs):
            sources, outs = refs[:count], refs[count : -count - 1]
            copies, sems = refs[-count - 1 : -1], refs[-1]
            moves = [
                pltpu.make_async_copy(source, copy, sems.at[i])
                for i, (source, copy) in enumerate(zip(sources, copies, strict=True))
            ]
            for move in moves:
                move.start()
            for move in moves:
                move.wait()
            kernel(place, *copies, *outs)

        in_vmem = pl.BlockSpec(memory_space=pltpu.VMEM)
        out = pl.pallas_call(
            copied_in,
            name=self.name + "_" + step,
            out_shape=out_shape,
            in_specs=[pl.BlockSpec(memory_space=pltpu.SMEM)] + [IN_HBM] * (count + 1),
            out_specs=jax.tree.map(lambda _: in_vmem, out_shape),
            scratch_shapes=[pltpu.VMEM(a.shape, a.dtype) for a in arrays]
            + [pltpu.SemaphoreType.DMA((count,))],
            compiler_params=pltpu.CompilerParams(vmem_limit_bytes=STEP_LIMIT),
            cost_estimate=SHORT,
        )(self.place, self.chain.last, *arrays)
        self.chain.last = out[0] if isinstance(out, (list, tuple)) else out
        return out

    def both(self):
        return self.mine, self.got, self.other, self.other_got

    def turn(self):
        if not self.by_hand:
            size = self.batch_size
            low = [[i for i in range(size) if i % 2 == side] for side in range(2)]
            high = [[i for i in range(size) if i // 2 % 2 == side] for side in range(2)]
            self.mine = lax.psum(self.mine + self.got, "batch", axis_index_groups=low)
            self.other = lax.psum(self.other + self.other_got, "batch", axis_index_groups=high)
            return
        shapes = [half_of(a) for a in (self.mine, self.mine, self.other, self.other)]
        self.mine, send, self.other, other_send = self.call(turn_kernel, "turn", shapes, *self.both())
        self.got, self.other_got = self.exchange(send, 2), self.exchange(other_send, 1)

    def join(self):
        if self.by_hand:
            rows = (self.mine.shape[0] + self.other.shape[0]) // 2
            shape = jax.ShapeDtypeStruct((rows, self.mine.shape[1]), BF16)
            self.counts = self.mine.shape[0], self.other.shape[0]
            self.joined, send = self.call(join_kernel, "join", [shape] * 2, *self.both())
            self.joined_got = self.exchange(send, 4)

    def add(self):
        if self.by_hand:
            shape = jax.ShapeDtypeStruct(self.joined.shape, BF16)
            self.joined = self.call(add_kernel, "add", shape, self.joined, self.joined_got)
            self.joined_got = self.exchange(self.joined, 4)

    def part(self):
        if self.by_hand:
            shapes = [jax.ShapeDtypeStruct((rows, self.joined.shape[1]), BF16) for rows in self.counts]
            self.mine, self.other = self.call(part_kernel, "part", shapes, self.joined, self.joined_got)
            self.got, self.other_got = self.exchange(self.mine, 2), self.exchange(self.other, 1)

    def widen(self):
        if self.by_hand:
            shapes = [jax.ShapeDtypeStruct((2 * a.shape[0], a.shape[1]), BF16) for a in (self.mine, self.other)]
            self.mine, self.other = self.call(widen_kernel, "widen", shapes, *self.both())
        self.got, self.other_got = self.exchange(self.mine, 1), self.exchange(self.other, 2)

    def finish(self):
        return self.call(
            functools.partial(finish_kernel, self.quarters, self.vectors), "finish", list(self.outs), *self.both()
        )


def half_of(array):
    return jax.ShapeDtypeStruct((array.shape[0] // 2, array.shape[1]), BF16)


def body(
    batch_size,
    band_size,
    patches,
    queries,
    cotangent,
    counts,
    masked,
    enc_gains,
    enc_shifts,
    enc_widebias,
    enc_scales,
    enc_project,
    enc_output,
    enc_expand,
    enc_reduce,
    reg_gains,
    reg_shifts,
    reg_widebias,
    reg_scales,
    reg_query,
    reg_keyval,
    reg_output,
    reg_expand,
    reg_reduce,
):
    images, band_rows, width = patches.shape
    hidden = enc_expand.shape[1]
    band = lax.axis_index("band")
    batch = lax.axis_index("batch")
    place = jnp.stack([lax.rem(batch // bit, 2) for bit in (1, 2, 4)])
    parts = band_size
    size = parts * band_rows
    part, part_hidden = width // parts, hidden // parts

    def exchange(array, offset):
        return lax.ppermute(array, "band", [(i, i ^ offset) for i in range(parts)])

    def gather(array):
        rows = [array]
        offset = parts // 2
        while offset:
            rows = rows + [exchange(a, offset) for a in rows]
            offset //= 2
        return rows

    order = relative_order(parts)
    in_smem = pl.BlockSpec(memory_space=pltpu.SMEM)
    in_vmem = pl.BlockSpec(memory_space=pltpu.VMEM)
    tokens, flags = pl.pallas_call(
        choose_kernel,
        name="choose",
        out_shape=[
            jax.ShapeDtypeStruct(patches.shape, patches.dtype),
            jax.ShapeDtypeStruct(masked.shape, F32),
        ],
        in_specs=[in_vmem] * 4,
        out_specs=[in_vmem] * 2,
        cost_estimate=SHORT,
    )(masked, masked[:, :, None], patches, queries)
    token_rows = gather(tokens)
    bands = band ^ jnp.array(order, jnp.int32)
    masked_all = jnp.concatenate([flags] + [exchange(flags, a) for a in order[1:]], 1)
    slots = (bands[:, None] * band_rows + jnp.arange(band_rows, dtype=jnp.int32)[None, :]).reshape(1, size)

    real = slots < counts[:, None]
    keep = jnp.where(real & (masked_all == 0), 1.0, 0.0).astype(F32)
    pick = jnp.where(real & (masked_all == 1), 1.0, 0.0).astype(F32)
    meta, keep_place, pick_place = pl.pallas_call(
        functools.partial(plan_kernel, images),
        name="plan",
        cost_estimate=LONG,
        out_shape=[
            jax.ShapeDtypeStruct((HEAD + 6 * images,), jnp.int32),
            jax.ShapeDtypeStruct((images, size), jnp.int32),
            jax.ShapeDtypeStruct((images, size), jnp.int32),
        ],
        in_specs=[in_smem, in_smem, in_vmem, in_vmem],
        out_specs=[in_smem, in_vmem, in_vmem],
        scratch_shapes=[pltpu.SMEM((5, images), jnp.int32)],
    )(counts, jnp.stack([band, place[0], place[1]]), keep, pick)
    cotangent = pl.pallas_call(
        hold_kernel,
        name="hold",
        out_shape=jax.ShapeDtypeStruct(cotangent.shape, cotangent.dtype),
        in_specs=[IN_HBM, in_vmem],
        out_specs=in_vmem,
        cost_estimate=SHORT,
    )(token_rows[1], cotangent)
    grad_rows = lax.all_gather(cotangent, "band", axis=0)

    chain = Chain(keep_place)
    small_rows, extra = 8, 128
    weight = functools.partial(jax.ShapeDtypeStruct, dtype=F32)

    def reduction(name, halves, outs, vectors=()):
        blocks = [(extra, "vectors")] if vectors else []
        count = len(outs) - len(vectors)
        for index in range(count):
            rows, columns = outs[index].shape
            blocks += [(rows, (index, column)) for column in range(0, columns, width)]
        return Reduction(batch_size, chain, place, name, halves, blocks, outs, vectors)

    ffn_outs = (weight((part_hidden, width)), weight((part, hidden)))

    def both(*arrays):
        return [("full", a) for a in arrays]

    def cut(*arrays):
        return [("bin", a) for a in arrays]

    def vm(shape, dtype=BF16):
        return pltpu.VMEM(shape, dtype)

    enc_wide = enc_widebias.reshape(1, hidden)
    reg_wide = reg_widebias.reshape(1, hidden)
    (
        x,
        triple,
        enc_totals,
        enc_normed_t,
        enc_mixed_t,
        enc_branch,
        enc_act,
        enc_slope,
        enc_middle_t,
        enc_ffn,
        pair_t,
        pair,
    ) = binned_call(
        functools.partial(enc_forward_kernel, images, parts),
        "enc_forward",
        images,
        chain,
        meta,
        both(keep_place, *token_rows, enc_gains, enc_shifts, enc_wide, enc_scales, reg_gains, reg_shifts),
        (enc_project, enc_output, enc_expand, enc_reduce, reg_keyval),
        [
            ((size, width), BF16),
            ((size, 3 * width), BF16),
            ((size, LANES), F32),
            ((part, size), BF16),
            ((part, size), BF16),
            ((size, width), BF16),
            ((size, part_hidden), BF16),
            ((size, hidden), BF16),
            ((part, size), BF16),
            ((size, width), F32),
            ((part, size), BF16),
            ((size, 2 * width), BF16),
        ],
        [],
        [
            vm(enc_project.shape),
            vm(enc_output.shape),
            vm(enc_expand.shape),
            vm(enc_reduce.shape),
            vm(reg_keyval.shape),
            pltpu.SemaphoreType.DMA((5,)),
            vm((size, width), F32),
            vm((size, size), F32),
            vm((size, hidden)),
            vm((size, width)),
        ],
    )
    (
        z,
        reg_query_low,
        reg_totals,
        reg_normed_t,
        reg_mixed_t,
        final_rows,
        reg_grad_mid,
        reg_small,
        reg_wide_sum,
        *reg_ffn_grads,
    ) = binned_call(
        functools.partial(reg_forward_kernel, images, parts),
        "reg_forward",
        images,
        chain,
        meta,
        both(pick_place, *token_rows)
        + cut(pair)
        + both(reg_gains, reg_shifts, reg_wide, reg_scales),
        (reg_query, reg_output, reg_expand, reg_reduce, grad_rows),
        [
            ((size, width), BF16),
            ((size, width), BF16),
            ((size, LANES), F32),
            ((part, size), BF16),
            ((part, size), BF16),
            ((size, width), F32),
            ((size, width), F32),
        ],
        [
            ((small_rows, width), F32),
            ((small_rows, hidden), F32),
        ]
        + group_shapes(part_hidden + parts * part, width),
        [
            vm(reg_query.shape),
            vm(reg_output.shape),
            vm(reg_expand.shape),
            vm(reg_reduce.shape),
            pltpu.SemaphoreType.DMA((4 + parts,)),
            vm((size, width), F32),
            vm((size, width), F32),
            vm((size, size), F32),
            vm((size, hidden)),
            vm((size, hidden)),
            vm((size, width)),
            vm((part, hidden), F32),
            vm((part_hidden, width), F32),
            vm((parts, images, band_rows, width)),
        ],
    )
    reg_ffn = reduction("reg_ffn", reg_ffn_grads, ffn_outs)
    query_grad, encoded_grad, reg_attn_small, *reg_attn_grads = binned_call(
        functools.partial(reg_attention_kernel, images, parts),
        "reg_attention_grad",
        images,
        chain,
        meta,
        cut(z, reg_query_low, reg_totals, reg_normed_t, reg_mixed_t, reg_grad_mid, pair, pair_t, x, enc_branch, enc_ffn)
        + both(reg_gains, reg_scales, enc_scales),
        (reg_query, reg_keyval, reg_output),
        [((size, width), F32), ((size, width), F32)],
        [((small_rows, width), F32)] + group_shapes(4 * part, width),
        [
            vm(reg_query.shape),
            vm(reg_keyval.shape),
            vm(reg_output.shape),
            pltpu.SemaphoreType.DMA((3,)),
            vm((size, size), F32),
            vm((size, width)),
            vm((size, width)),
            vm((size, 2 * width)),
            vm((part, width), F32),
            vm((part, 2 * width), F32),
            vm((part, width), F32),
            vm((LANES, size), F32),
        ],
    )
    reg_attn = reduction(
        "reg_attention",
        reg_attn_grads,
        (weight((part, width)), weight((part, width)), weight((part, 2 * width))),
    )
    reg_ffn.turn()
    enc_grad_mid, enc_small, enc_wide_sum, *enc_ffn_grads = binned_call(
        functools.partial(enc_ffn_kernel, images, parts),
        "enc_ffn_grad",
        images,
        chain,
        meta,
        cut(encoded_grad, x, enc_branch, enc_ffn, enc_act, enc_slope, enc_middle_t)
        + both(enc_gains, enc_scales),
        (enc_expand, enc_reduce),
        [((size, width), F32)],
        [
            ((small_rows, width), F32),
            ((small_rows, hidden), F32),
        ]
        + group_shapes(part_hidden + parts * part, width),
        [
            vm(enc_expand.shape),
            vm(enc_reduce.shape),
            pltpu.SemaphoreType.DMA((2,)),
            vm((part, hidden), F32),
            vm((part_hidden, width), F32),
        ],
    )
    enc_ffn_sum = reduction("enc_ffn", enc_ffn_grads, ffn_outs)
    reg_ffn.join()
    reg_attn.turn()
    patch_grad, _, *enc_attn_grads = binned_call(
        functools.partial(enc_attention_kernel, images, parts),
        "enc_attention_grad",
        images,
        chain,
        meta,
        cut(enc_grad_mid, x, triple, enc_totals, enc_normed_t, enc_mixed_t)
        + both(enc_gains, enc_scales, reg_small, reg_attn_small, enc_small, reg_wide_sum, enc_wide_sum),
        (enc_output, enc_project),
        [((size, width), F32)],
        [((small_rows, width), F32)] + group_shapes(4 * part + extra, width),
        [
            vm(enc_output.shape),
            vm(enc_project.shape),
            pltpu.SemaphoreType.DMA((2,)),
            vm((size, size), F32),
            vm((size, width)),
            vm((size, 3 * width)),
            vm((part, 3 * width), F32),
            vm((part, width), F32),
            vm((LANES, size), F32),
            vm((extra, width), F32),
        ],
    )

    reg_s, reg_a, enc_s, enc_a = (small_rows * i for i in range(4))
    vectors = (
        (enc_a + 3, enc_s + 2),
        (enc_a + 4, enc_a + 1, enc_a + 2, enc_a, enc_s + 3, enc_s + 1),
        (enc_s + 4, enc_s),
        (reg_a + 3, reg_a + 5, reg_s + 2),
        (reg_a + 4, reg_a + 6, reg_a + 1, reg_a + 2, reg_a, reg_s + 3, reg_s + 1),
        (reg_s + 4, reg_s),
    )
    vector_rows = [(2 + i, rows, part) for i, rows in enumerate(vectors)]
    vector_rows += [(2 + len(vectors) + i, (enc_a + small_rows * (1 + i),), width) for i in range(2)]
    enc_attn = reduction(
        "enc_attention",
        enc_attn_grads,
        [weight((part, width)), weight((part, 3 * width))]
        + [weight((len(rows), part)) for rows in vectors]
        + [weight((1, width))] * 2,
        vector_rows,
    )
    enc_ffn_sum.turn()
    reg_ffn.add()
    reg_attn.join()
    enc_attn.turn()
    enc_ffn_sum.join()
    reg_ffn.part()
    reg_attn.add()
    enc_attn.join()
    enc_ffn_sum.add()
    reg_ffn.widen()
    reg_attn.part()
    enc_attn.add()
    enc_ffn_sum.part()
    reg_reduce_grad, reg_expand_grad = reg_ffn.finish()
    reg_attn.widen()
    enc_ffn_sum.widen()
    enc_attn.part()

    def own_places(places):
        return places[:, :band_rows, None]

    by_image = pl.BlockSpec((None, band_rows, 1), lambda i, m: (i, 0, 0))
    bin_of_image = pl.BlockSpec((None, size, width), lambda i, m: (m[HEAD + i], 0, 0))
    image_out = pl.BlockSpec((None, band_rows, width), lambda i, m: (i, 0, 0))
    prediction, query_grad, patch_grad = pl.pallas_call(
        unpack_kernel,
        name="unpack",
        out_shape=[jax.ShapeDtypeStruct(patches.shape, F32)] * 3,
        grid_spec=pltpu.PrefetchScalarGridSpec(
            num_scalar_prefetch=1,
            grid=(images,),
            in_specs=[IN_HBM, by_image, by_image, bin_of_image, bin_of_image, bin_of_image],
            out_specs=[image_out] * 3,
        ),
        compiler_params=pltpu.CompilerParams(vmem_limit_bytes=VMEM_LIMIT),
        cost_estimate=LONG,
    )(meta, chain.last, own_places(keep_place), own_places(pick_place), final_rows, query_grad, patch_grad)

    chain.last = prediction
    enc_attn.widen()
    reg_query_grad, reg_output_grad, reg_keyval_grad = reg_attn.finish()
    enc_reduce_grad, enc_expand_grad = enc_ffn_sum.finish()
    (
        enc_output_grad,
        enc_project_grad,
        enc_gains_grad,
        enc_shifts_grad,
        enc_scales_grad,
        reg_gains_grad,
        reg_shifts_grad,
        reg_scales_grad,
        reg_wide_grad,
        enc_wide_grad,
    ) = enc_attn.finish()
    return (
        prediction,
        patch_grad,
        query_grad,
        enc_gains_grad,
        enc_shifts_grad,
        enc_wide_grad.reshape(-1),
        enc_scales_grad,
        enc_project_grad,
        enc_output_grad,
        enc_expand_grad,
        enc_reduce_grad,
        reg_gains_grad,
        reg_shifts_grad,
        reg_wide_grad.reshape(-1),
        reg_scales_grad,
        reg_query_grad,
        reg_keyval_grad,
        reg_output_grad,
        reg_expand_grad,
        reg_reduce_grad,
    )


def solution(mesh):
    token = P("batch", "band", None)
    in_specs = (token, token, token, P("batch"), P("batch", "band")) + (P(),) * 17
    by_row, by_col = P("band", None), P(None, "band")
    out_specs = (
        token,
        token,
        token,
        by_col,
        by_col,
        P("band"),
        by_col,
        by_row,
        by_row,
        by_row,
        by_row,
        by_col,
        by_col,
        P("band"),
        by_col,
        by_row,
        by_row,
        by_row,
        by_row,
        by_row,
    )
    return jax.shard_map(
        functools.partial(body, mesh.shape["batch"], mesh.shape["band"]),
        mesh=mesh,
        in_specs=in_specs,
        out_specs=out_specs,
        check_vma=False,
    )
```

```python
import functools

import jax
import jax.numpy as jnp
from jax import lax
from jax.experimental import pallas as pl
from jax.experimental.pallas import tpu as pltpu
from jax.sharding import PartitionSpec as P

HEADS = 12
HD = 64
EPS = 1e-06
ROOT_HALF = 0.7071067811865476
INV_ROOT_TAU = 0.3989422804014327
NEG_LARGE = -1e30
F32 = jnp.float32
BF16 = jnp.bfloat16
VMEM_LIMIT = 56 * 1024 * 1024
STEP_LIMIT = 16 * 1024 * 1024
LANES = 128
HEAD = 4


def dot(a, b):
    return lax.dot_general(a, b, (((1,), (0,)), ((), ())), preferred_element_type=F32)


def dot_nt(a, b):
    return lax.dot_general(a, b, (((1,), (1,)), ((), ())), preferred_element_type=F32)


def dot_tn(a, b):
    return lax.dot_general(a, b, (((0,), (0,)), ((), ())), preferred_element_type=F32)


def unit(values):
    row_mean = jnp.mean(values, -1, keepdims=True)
    centred = values - row_mean
    variance = jnp.mean(centred * centred, -1, keepdims=True)
    inv_std = lax.rsqrt(variance + EPS)
    return centred * inv_std, inv_std


def unit_back(grad_out, unit_rows, inv_std, gain):
    scaled = grad_out * gain
    first_term = jnp.mean(scaled, -1, keepdims=True)
    second_term = jnp.mean(scaled * unit_rows, -1, keepdims=True)
    return inv_std * (scaled - first_term - unit_rows * second_term)


def rows_sum(values):
    return jnp.sum(values, 0, keepdims=True)


def gate_and_slope(pre_act):
    bell = 0.5 * (1.0 + lax.erf(pre_act * ROOT_HALF))
    slope = bell + pre_act * INV_ROOT_TAU * jnp.exp(-0.5 * pre_act * pre_act)
    return (pre_act * bell).astype(BF16), slope.astype(BF16)


def relative_order(parts):
    order, offset = [0], parts // 2
    while offset:
        order, offset = order + [a ^ offset for a in order], offset // 2
    return order


class Meta:
    def __init__(self, ref, images):
        self.ref, self.images = ref, images

    def bins(self):
        return self.ref[0]

    def band(self):
        return self.ref[1]

    def bits(self):
        return self.ref[2], self.ref[3]

    def bin_of(self, image):
        return self.ref[HEAD + image]

    def keep_off(self, image):
        return self.ref[HEAD + self.images + image]

    def keep_count(self, image):
        return self.ref[HEAD + 2 * self.images + image]

    def pick_off(self, image):
        return self.ref[HEAD + 3 * self.images + image]

    def pick_count(self, image):
        return self.ref[HEAD + 4 * self.images + image]

    def count(self, image):
        return self.ref[HEAD + 5 * self.images + image]

    def segments(self, bin_now, kind, shape, dim, blank):
        rows = lax.broadcasted_iota(jnp.int32, shape, dim)
        owner = jnp.full(shape, blank, jnp.int32)
        for image in range(self.images):
            start = self.keep_off(image) if kind == "keep" else self.pick_off(image)
            count = self.keep_count(image) if kind == "keep" else self.pick_count(image)
            stop = start + jnp.where(self.bin_of(image) == bin_now, count, 0)
            owner = jnp.where((rows >= start) & (rows < stop), image, owner)
        return owner


def key_mask(meta, bin_now, query_kind, size, key_dim):
    along = ((size, 1), (1, size))
    query_owner = meta.segments(bin_now, query_kind, along[1 - key_dim], 1 - key_dim, -2)
    key_owner = meta.segments(bin_now, "keep", along[key_dim], key_dim, -1)
    return query_owner == key_owner


def quarter_rows(meta, width, parts):
    part = width // parts
    row = lax.broadcasted_iota(jnp.int32, (part, width), 0) + meta.band() * part
    return (row == lax.broadcasted_iota(jnp.int32, (part, width), 1)).astype(BF16)


def lower_half():
    return lax.broadcasted_iota(jnp.int32, (1, LANES), 1) < HD


def pair_cols(pair, first=0):
    at = first + pair * LANES
    return pl.ds(at if isinstance(at, int) else pl.multiple_of(at, LANES), LANES)


def each_pair(one_pair, together):
    steps = HEADS // 2 // together

    def step(index, _):
        for pair in range(together):
            one_pair(index * together + pair)
        return 0

    if steps == 1:
        step(0, 0)
    else:
        lax.fori_loop(0, steps, step, 0)


def attend_forward(query_of, key_of, value_of, mask_ref, mixed_ref, totals_ref):
    low = lower_half()
    sides = (low.astype(BF16), (~low).astype(BF16))
    lane = lax.broadcasted_iota(jnp.int32, totals_ref.shape, 1)
    totals_ref[...] = jnp.zeros_like(totals_ref)

    def one_pair(pair):
        query, key, value = query_of(pair), key_of(pair), value_of(pair)
        mixed = []
        for side in range(2):
            scores = dot_nt(query, key * sides[side]) * HD ** (-0.5)
            scores = jnp.where(mask_ref[...] > 0, scores, NEG_LARGE)
            top = jnp.max(scores, -1, keepdims=True)
            exp_scores = jnp.exp(scores - top)
            total = jnp.sum(exp_scores, -1, keepdims=True)
            weights = (exp_scores * (1.0 / total)).astype(BF16)
            totals_ref[...] = jnp.where(lane == 2 * pair + side, top + jnp.log(total), totals_ref[...])
            mixed.append(dot(weights, value))
        mixed_ref[:, pair_cols(pair)] = jnp.where(low, mixed[0], mixed[1]).astype(BF16)

    each_pair(one_pair, 6)


def attend_backward(query_of, key_of, value_of, grad_of, totals_ref, mask_ref, store):
    low = lower_half()
    sides = (low.astype(BF16), (~low).astype(BF16))

    def one_pair(pair):
        query, key, value, grad = query_of(pair), key_of(pair), value_of(pair), grad_of(pair)
        grad_query, grad_key, grad_value = [], [], []
        for side in range(2):
            scores = dot_nt(key * sides[side], query) * HD ** (-0.5)
            scores = jnp.where(mask_ref[...] > 0, scores, NEG_LARGE)
            probs = jnp.exp(scores - totals_ref[pl.ds(2 * pair + side, 1), :])
            grad_value.append(dot(probs.astype(BF16), grad))
            grad_probs = dot_nt(value * sides[side], grad)
            inner = jnp.sum(grad_probs * probs, 0, keepdims=True)
            grad_scores = (probs * (grad_probs - inner)).astype(BF16)
            grad_query.append(dot_tn(key, grad_scores)[side * HD : (side + 1) * HD, :])
            grad_key.append(dot(grad_scores, query))
        store(
            pair,
            jnp.concatenate(grad_query, 0).T * HD ** (-0.5),
            jnp.where(low, grad_key[0], grad_key[1]) * HD ** (-0.5),
            jnp.where(low, grad_value[0], grad_value[1]),
        )

    each_pair(one_pair, 6)


def pack_rows(meta, bin_now, place_ref, gathered, packed, size, by_block):
    packed[...] = jnp.zeros_like(packed)
    parts = len(gathered)
    slots = size // parts

    def add(image, blocks):
        taken = slice(blocks[0] * slots, (blocks[-1] + 1) * slots)
        shape = (size, len(blocks) * slots)
        row = lax.broadcasted_iota(jnp.int32, shape, 0)
        chosen = (row == place_ref[image : image + 1, taken]).astype(BF16)
        packed[...] += dot(chosen, jnp.concatenate([gathered[j][image] for j in blocks], 0))

    for image in range(meta.images):

        @pl.when(meta.bin_of(image) == bin_now)
        def _():
            if not by_block:
                add(image, range(parts))
                return
            for j, offset in enumerate(relative_order(parts)):
                pl.when(meta.count(image) > (meta.band() ^ offset) * slots)(functools.partial(add, image, [j]))


class Weights:
    def __init__(self, sources, targets, sems):
        self.copies = [
            pltpu.make_async_copy(source, target, sems.at[i])
            for i, (source, target) in enumerate(zip(sources, targets, strict=True))
        ]

    def start(self):
        @pl.when(pl.program_id(0) == 0)
        def _():
            for copy in self.copies:
                copy.start()

    def wait(self, index):
        @pl.when(pl.program_id(0) == 0)
        def _():
            self.copies[index].wait()


def add_row(small_ref, row, values):
    small_ref[row : row + 1, :] += values


def first_step(refs):
    @pl.when(pl.program_id(0) == 0)
    def _():
        for ref in refs:
            ref[...] = jnp.zeros_like(ref)


def split_rows(total):
    unit = 128
    return (total // 2 + unit - 1) // unit * unit


def cut_blocks(blocks, start, stop):
    at, cut = 0, []
    for rows, tag in blocks:
        low, high = max(at, start), min(at + rows, stop)
        if low < high:
            cut.append((tag, low - at, high - low, low - start))
        at += rows
    return cut


def quarters_of(blocks):
    total = sum(rows for rows, _ in blocks)
    first = split_rows(total)
    edges = (0, first // 2, first, first + (total - first) // 2, total)
    return [cut_blocks(blocks, a, b) for a, b in zip(edges, edges[1:], strict=False)]


def group_shapes(total, width):
    first = split_rows(total)
    return [((rows // 2, width), BF16) for rows in (first, first, total - first, total - first)]


def write_group(meta, blocks, width, outs):
    quarters = quarters_of(blocks)

    def write(cuts, out):
        for (ref, column), row, rows, at in cuts:
            values = ref[row : row + rows, column : column + width]
            out[at : at + rows, :] = values.astype(BF16)

    for bit, pair, (keep_out, send_out) in ((0, quarters[:2], outs[:2]), (1, quarters[2:], outs[2:])):
        for side in range(2):

            @pl.when(meta.bits()[bit] == side)
            def _():
                write(pair[side], keep_out)
                write(pair[1 - side], send_out)


def column_blocks(ref, width):
    return [(ref.shape[0], (ref, column)) for column in range(0, ref.shape[1], width)]


def last_step(meta, write):
    @pl.when(pl.program_id(0) == meta.bins() - 1)
    def _():
        write()


def choose_kernel(masked_ref, patches_ref, queries_ref, tokens_out, flags_out):
    flags = masked_ref[...].astype(F32)
    flags_out[...] = flags
    columns = flags.T
    for image in range(tokens_out.shape[0]):
        tokens_out[image] = jnp.where(columns[:, image : image + 1] == 0, patches_ref[image], queries_ref[image])


def hold_kernel(_, __, source, out):
    out[...] = source[...]


def plan_kernel(
    images,
    counts_ref,
    band_ref,
    keep_ref,
    pick_ref,
    meta_ref,
    keep_place_ref,
    pick_place_ref,
    words,
):
    size = keep_ref.shape[1]
    before = (
        lax.broadcasted_iota(jnp.int32, (size, size), 0)
        <= lax.broadcasted_iota(jnp.int32, (size, size), 1)
    ).astype(BF16)
    keep, pick = keep_ref[...], pick_ref[...]
    keep_rank = dot(keep.astype(BF16), before).astype(jnp.int32) - 1
    pick_rank = dot(pick.astype(BF16), before).astype(jnp.int32) - 1
    for image in range(images):
        meta_ref[HEAD + 5 * images + image] = counts_ref[image]
        words[0, image] = jnp.sum(keep[image : image + 1, :]).astype(jnp.int32)
        words[1, image] = jnp.sum(pick[image : image + 1, :]).astype(jnp.int32)
        for row in (2, 3, 4):
            words[row, image] = 0

    def place(_, bins):
        def largest(image, best):
            open_now = words[4, image] == 0
            better = open_now & ((best < 0) | (counts_ref[image] > counts_ref[jnp.maximum(best, 0)]))
            return jnp.where(better, image, best)

        image = lax.fori_loop(0, images, largest, jnp.int32(-1))
        keep_count, pick_count = words[0, image], words[1, image]

        def first_fit(step, best):
            bin_now = images - 1 - step
            fits = (words[2, bin_now] + keep_count <= size) & (words[3, bin_now] + pick_count <= size)
            return jnp.where(fits, bin_now, best)

        bin_now = lax.fori_loop(0, images, first_fit, jnp.int32(0))
        meta_ref[HEAD + image] = bin_now
        meta_ref[HEAD + images + image] = words[2, bin_now]
        meta_ref[HEAD + 2 * images + image] = keep_count
        meta_ref[HEAD + 3 * images + image] = words[3, bin_now]
        meta_ref[HEAD + 4 * images + image] = pick_count
        words[2, bin_now] = words[2, bin_now] + keep_count
        words[3, bin_now] = words[3, bin_now] + pick_count
        words[4, image] = 1
        return jnp.maximum(bins, bin_now + 1)

    meta_ref[0] = lax.fori_loop(0, images, place, jnp.int32(0))
    meta_ref[1] = band_ref[0]
    meta_ref[2] = band_ref[1]
    meta_ref[3] = band_ref[2]
    for image in range(images):
        row = slice(image, image + 1)
        keep_place_ref[row, :] = jnp.where(
            keep[row, :] > 0, keep_rank[row, :] + meta_ref[HEAD + images + image], -1
        )
        pick_place_ref[row, :] = jnp.where(
            pick[row, :] > 0, pick_rank[row, :] + meta_ref[HEAD + 3 * images + image], -1
        )


def ffn_forward(normed, expand, wide_bias, reduce_weight, act_ref, slope_ref, width):
    total = None
    for start in range(0, expand.shape[1], width):
        cols = slice(start, start + width)
        act, slope = gate_and_slope(dot(normed, expand[:, cols]) + wide_bias[:, cols])
        act_ref[:, cols] = act
        slope_ref[:, cols] = slope
        part = dot(act, reduce_weight[cols, :])
        total = part if total is None else total + part
    return total


def ffn_backward(grad_low, slope_ref, normed_part, expand, reduce_weight, expand_acc, wide_ref, width):
    total = None
    for start in range(0, expand.shape[1], width):
        cols = slice(start, start + width)
        grad_act = dot_nt(grad_low, reduce_weight[cols, :])
        grad_pre = grad_act * slope_ref[:, cols].astype(F32)
        grad_pre_low = grad_pre.astype(BF16)
        wide_ref[0:1, cols] += rows_sum(grad_pre_low.astype(F32))
        expand_acc[:, cols] += dot(normed_part, grad_pre_low)
        part = dot_nt(grad_pre_low, expand[:, cols])
        total = part if total is None else total + part
    return total


def enc_forward_kernel(images, parts, meta_ref, place_ref, pick_ref, *refs):
    enc_forward(images, parts, meta_ref, place_ref, pick_ref, refs[:parts], *refs[parts:])


def enc_forward(
    images,
    parts,
    meta_ref,
    place_ref,
    pick_ref,
    row_refs,
    gains,
    shifts,
    wide_bias,
    scales,
    reg_gains,
    reg_shifts,
    project_hbm,
    output_hbm,
    expand_hbm,
    reduce_hbm,
    keyval_hbm,
    x_out,
    triple_out,
    totals_out,
    normed_t_out,
    mixed_t_out,
    branch_out,
    act_out,
    slope_out,
    middle_t_out,
    ffn_out,
    pair_t_out,
    pair_out,
    z_out,
    project,
    output,
    expand,
    reduce_weight,
    keyval,
    sems,
    packed,
    mask_ref,
    act_all,
    mixed_ref,
):
    meta = Meta(meta_ref, images)
    bin_now = pl.program_id(0)
    weights = Weights(
        (project_hbm, output_hbm, expand_hbm, reduce_hbm, keyval_hbm),
        (project, output, expand, reduce_weight, keyval),
        sems,
    )
    weights.start()
    size, width = packed.shape
    pack_rows(meta, bin_now, pick_ref, row_refs, packed, size, False)
    z_out[...] = packed[...].astype(BF16)
    pack_rows(meta, bin_now, place_ref, row_refs, packed, size, True)
    mask_ref[...] = key_mask(meta, bin_now, "keep", size, 1).astype(F32)
    part_of = quarter_rows(meta, width, parts)
    x = packed[...]
    x_out[...] = x.astype(BF16)
    unit_rows, _ = unit(x)
    normed = (unit_rows * gains[0:1, :] + shifts[0:1, :]).astype(BF16)
    normed_t_out[...] = dot_nt(part_of, normed).astype(BF16)
    weights.wait(0)
    triple_out[:, :width] = (dot(normed, project[:, :width]) + shifts[1:2, :]).astype(BF16)
    triple_out[:, width : 2 * width] = dot(normed, project[:, width : 2 * width]).astype(BF16)
    triple_out[:, 2 * width :] = (dot(normed, project[:, 2 * width :]) + shifts[2:3, :]).astype(BF16)

    attend_forward(
        lambda pair: triple_out[:, pair_cols(pair)],
        lambda pair: triple_out[:, pair_cols(pair, width)],
        lambda pair: triple_out[:, pair_cols(pair, 2 * width)],
        mask_ref,
        mixed_ref,
        totals_out,
    )
    mixed = mixed_ref[...]
    mixed_t_out[...] = dot_nt(part_of, mixed).astype(BF16)
    weights.wait(1)
    branch = (dot(mixed, output[...]) + shifts[3:4, :]).astype(BF16)
    branch_out[...] = branch
    middle = x + scales[0:1, :] * branch.astype(F32)
    unit_rows, _ = unit(middle)
    normed = (unit_rows * gains[1:2, :] + shifts[4:5, :]).astype(BF16)
    middle_t_out[...] = dot_nt(part_of, normed).astype(BF16)
    weights.wait(2)
    weights.wait(3)
    part_width = expand.shape[1] // parts
    ffn = ffn_forward(normed, expand, wide_bias, reduce_weight, act_all, slope_out, part_width) + shifts[5:6, :]
    act_out[...] = act_all[:, pl.ds(pl.multiple_of(meta.band() * part_width, part_width), part_width)]
    ffn_out[...] = ffn
    encoded = middle + scales[1:2, :] * ffn
    unit_rows, _ = unit(encoded)
    pair_normed = (unit_rows * reg_gains[1:2, :] + reg_shifts[1:2, :]).astype(BF16)
    pair_t_out[...] = dot_nt(part_of, pair_normed).astype(BF16)
    weights.wait(4)
    pair_out[:, :width] = dot(pair_normed, keyval[:, :width]).astype(BF16)
    pair_out[:, width:] = (dot(pair_normed, keyval[:, width:]) + reg_shifts[3:4, :]).astype(BF16)


def reg_forward_kernel(
    images,
    parts,
    meta_ref,
    place_ref,
    z_ref,
    pair_ref,
    gains,
    shifts,
    wide_bias,
    scales,
    query_hbm,
    output_hbm,
    expand_hbm,
    reduce_hbm,
    grad_hbm,
    query_out,
    totals_out,
    normed_t_out,
    mixed_t_out,
    final_out,
    grad_mid_out,
    small_out,
    wide_out,
    out_0,
    out_1,
    out_2,
    out_3,
    query_weight,
    output,
    expand,
    reduce_weight,
    sems,
    packed_grad,
    mask_ref,
    act_all,
    slope_all,
    mixed_ref,
    expand_acc,
    reduce_acc,
    grad_rows,
):
    meta = Meta(meta_ref, images)
    bin_now = pl.program_id(0)
    relative = relative_order(parts)
    weights = Weights(
        (query_hbm, output_hbm, expand_hbm, reduce_hbm) + tuple(grad_hbm.at[meta.band() ^ i] for i in relative),
        (query_weight, output, expand, reduce_weight) + tuple(grad_rows.at[i] for i in range(parts)),
        sems,
    )
    weights.start()
    first_step((small_out, wide_out, expand_acc, reduce_acc))
    size, width = packed_grad.shape
    mask_ref[...] = key_mask(meta, bin_now, "pick", size, 1).astype(F32)
    part_of = quarter_rows(meta, width, parts)
    z = z_ref[...].astype(F32)
    unit_rows, _ = unit(z)
    normed = (unit_rows * gains[0:1, :] + shifts[0:1, :]).astype(BF16)
    normed_t_out[...] = dot_nt(part_of, normed).astype(BF16)
    weights.wait(0)
    query_out[...] = (dot(normed, query_weight[...]) + shifts[2:3, :]).astype(BF16)

    attend_forward(
        lambda pair: query_out[:, pair_cols(pair)],
        lambda pair: pair_ref[:, pair_cols(pair)],
        lambda pair: pair_ref[:, pair_cols(pair, width)],
        mask_ref,
        mixed_ref,
        totals_out,
    )
    mixed = mixed_ref[...]
    mixed_t_out[...] = dot_nt(part_of, mixed).astype(BF16)
    weights.wait(1)
    branch = (dot(mixed, output[...]) + shifts[4:5, :]).astype(BF16).astype(F32)
    middle = z + scales[0:1, :] * branch
    unit_rows, inv_std = unit(middle)
    normed = (unit_rows * gains[2:3, :] + shifts[5:6, :]).astype(BF16)
    normed_part = dot_nt(part_of, normed).astype(BF16)
    weights.wait(2)
    weights.wait(3)
    part_width = expand.shape[1] // parts
    ffn = ffn_forward(normed, expand, wide_bias, reduce_weight, act_all, slope_all, part_width) + shifts[6:7, :]
    final_out[...] = middle + scales[1:2, :] * ffn
    for i in range(parts):
        weights.wait(4 + i)
    pack_rows(
        meta, bin_now, place_ref, [grad_rows.at[i] for i in range(parts)], packed_grad, size, False
    )
    grad_final = packed_grad[...]
    add_row(small_out, 0, rows_sum(grad_final * ffn))
    grad_low = (scales[1:2, :] * grad_final).astype(BF16)
    add_row(small_out, 1, rows_sum(grad_low.astype(F32)))
    act_part = act_all[:, pl.ds(pl.multiple_of(meta.band() * part_width, part_width), part_width)]
    reduce_acc[...] += dot_tn(act_part, grad_low)
    grad_normed = ffn_backward(
        grad_low, slope_all, normed_part, expand, reduce_weight, expand_acc, wide_out, part_width
    )
    add_row(small_out, 2, rows_sum(grad_normed * unit_rows))
    add_row(small_out, 3, rows_sum(grad_normed))
    grad_mid = grad_final + unit_back(grad_normed, unit_rows, inv_std, gains[2:3, :])
    grad_mid_out[...] = grad_mid
    add_row(small_out, 4, rows_sum(grad_mid * branch))

    blocks = column_blocks(reduce_acc, width) + column_blocks(expand_acc, width)
    last_step(meta, lambda: write_group(meta, blocks, width, (out_0, out_1, out_2, out_3)))


def reg_attention_kernel(
    images,
    parts,
    meta_ref,
    z_ref,
    query_ref,
    totals_ref,
    normed_t_ref,
    mixed_t_ref,
    grad_mid_ref,
    pair_ref,
    pair_t_ref,
    x_ref,
    enc_branch_ref,
    enc_ffn_ref,
    gains,
    scales,
    enc_scales,
    query_hbm,
    keyval_hbm,
    output_hbm,
    query_grad_out,
    encoded_grad_out,
    small_out,
    out_0,
    out_1,
    out_2,
    out_3,
    query_weight,
    keyval,
    output,
    sems,
    mask_ref,
    mixed_grad_ref,
    query_back,
    pair_back,
    query_acc,
    pair_acc,
    output_acc,
    totals_rows,
):
    meta = Meta(meta_ref, images)
    bin_now = pl.program_id(0)
    weights = Weights((output_hbm, query_hbm, keyval_hbm), (output, query_weight, keyval), sems)
    weights.start()
    first_step((small_out, query_acc, pair_acc, output_acc))
    size, width = mixed_grad_ref.shape
    mask_ref[...] = key_mask(meta, bin_now, "pick", size, 0).astype(F32)
    grad_mid = grad_mid_ref[...]
    branch_grad = (scales[0:1, :] * grad_mid).astype(BF16)
    output_acc[...] += dot(mixed_t_ref[...], branch_grad)
    add_row(small_out, 0, rows_sum(branch_grad.astype(F32)))
    weights.wait(0)
    mixed_grad_ref[...] = dot_nt(branch_grad, output[...]).astype(BF16)

    def store(pair, grad_query, grad_key, grad_value):
        query_back[:, pair_cols(pair)] = grad_query.astype(BF16)
        pair_back[:, pair_cols(pair)] = grad_key.astype(BF16)
        pair_back[:, pair_cols(pair, width)] = grad_value.astype(BF16)

    totals_rows[...] = totals_ref[...].T
    attend_backward(
        lambda pair: query_ref[:, pair_cols(pair)],
        lambda pair: pair_ref[:, pair_cols(pair)],
        lambda pair: pair_ref[:, pair_cols(pair, width)],
        lambda pair: mixed_grad_ref[:, pair_cols(pair)],
        totals_rows,
        mask_ref,
        store,
    )
    grad_query, grad_pair = query_back[...], pair_back[...]
    query_acc[...] += dot(normed_t_ref[...], grad_query)
    pair_acc[...] += dot(pair_t_ref[...], grad_pair)
    add_row(small_out, 1, rows_sum(grad_query.astype(F32)))
    add_row(small_out, 2, rows_sum(grad_pair[:, width:].astype(F32)))
    weights.wait(1)
    query_side = dot_nt(grad_query, query_weight[...]).astype(BF16).astype(F32)
    weights.wait(2)
    pair_side = dot_nt(grad_pair, keyval[...]).astype(BF16).astype(F32)
    unit_rows, inv_std = unit(z_ref[...].astype(F32))
    add_row(small_out, 3, rows_sum(query_side * unit_rows))
    add_row(small_out, 4, rows_sum(query_side))
    query_grad_out[...] = grad_mid + unit_back(query_side, unit_rows, inv_std, gains[0:1, :])
    encoded = (
        x_ref[...].astype(F32)
        + enc_scales[0:1, :] * enc_branch_ref[...].astype(F32)
        + enc_scales[1:2, :] * enc_ffn_ref[...]
    )
    unit_rows, inv_std = unit(encoded)
    add_row(small_out, 5, rows_sum(pair_side * unit_rows))
    add_row(small_out, 6, rows_sum(pair_side))
    encoded_grad_out[...] = unit_back(pair_side, unit_rows, inv_std, gains[1:2, :])

    blocks = [block for ref in (query_acc, output_acc, pair_acc) for block in column_blocks(ref, width)]
    last_step(meta, lambda: write_group(meta, blocks, width, (out_0, out_1, out_2, out_3)))


def enc_ffn_kernel(
    images,
    parts,
    meta_ref,
    encoded_grad_ref,
    x_ref,
    branch_ref,
    ffn_ref,
    act_ref,
    slope_ref,
    middle_t_ref,
    gains,
    scales,
    expand_hbm,
    reduce_hbm,
    grad_mid_out,
    small_out,
    wide_out,
    out_0,
    out_1,
    out_2,
    out_3,
    expand,
    reduce_weight,
    sems,
    expand_acc,
    reduce_acc,
):
    meta = Meta(meta_ref, images)
    weights = Weights((reduce_hbm, expand_hbm), (reduce_weight, expand), sems)
    weights.start()
    first_step((small_out, wide_out, expand_acc, reduce_acc))
    width = x_ref.shape[1]
    encoded_grad = encoded_grad_ref[...]
    add_row(small_out, 0, rows_sum(encoded_grad * ffn_ref[...]))
    grad_low = (scales[1:2, :] * encoded_grad).astype(BF16)
    add_row(small_out, 1, rows_sum(grad_low.astype(F32)))
    reduce_acc[...] += dot_tn(act_ref[...], grad_low)
    weights.wait(0)
    weights.wait(1)
    part_width = expand.shape[1] // parts
    grad_normed = ffn_backward(
        grad_low, slope_ref, middle_t_ref[...], expand, reduce_weight, expand_acc, wide_out, part_width
    )
    branch = branch_ref[...].astype(F32)
    unit_rows, inv_std = unit(x_ref[...].astype(F32) + scales[0:1, :] * branch)
    add_row(small_out, 2, rows_sum(grad_normed * unit_rows))
    add_row(small_out, 3, rows_sum(grad_normed))
    grad_mid = encoded_grad + unit_back(grad_normed, unit_rows, inv_std, gains[1:2, :])
    grad_mid_out[...] = grad_mid
    add_row(small_out, 4, rows_sum(grad_mid * branch))

    blocks = column_blocks(reduce_acc, width) + column_blocks(expand_acc, width)
    last_step(meta, lambda: write_group(meta, blocks, width, (out_0, out_1, out_2, out_3)))


def enc_attention_kernel(
    images,
    parts,
    meta_ref,
    grad_mid_ref,
    x_ref,
    triple_ref,
    totals_ref,
    normed_t_ref,
    mixed_t_ref,
    gains,
    scales,
    reg_small,
    reg_attn_small,
    enc_small,
    reg_wide,
    enc_wide,
    output_hbm,
    project_hbm,
    patch_grad_out,
    small_out,
    out_0,
    out_1,
    out_2,
    out_3,
    output,
    project,
    sems,
    mask_ref,
    mixed_grad_ref,
    triple_back,
    project_acc,
    output_acc,
    totals_rows,
    vectors,
):
    meta = Meta(meta_ref, images)
    bin_now = pl.program_id(0)
    weights = Weights((output_hbm, project_hbm), (output, project), sems)
    weights.start()
    first_step((small_out, project_acc, output_acc))
    size, width = mixed_grad_ref.shape
    mask_ref[...] = key_mask(meta, bin_now, "keep", size, 0).astype(F32)
    grad_mid = grad_mid_ref[...]
    branch_grad = (scales[0:1, :] * grad_mid).astype(BF16)
    output_acc[...] += dot(mixed_t_ref[...], branch_grad)
    add_row(small_out, 0, rows_sum(branch_grad.astype(F32)))
    weights.wait(0)
    mixed_grad_ref[...] = dot_nt(branch_grad, output[...]).astype(BF16)

    def store(pair, grad_query, grad_key, grad_value):
        triple_back[:, pair_cols(pair)] = grad_query.astype(BF16)
        triple_back[:, pair_cols(pair, width)] = grad_key.astype(BF16)
        triple_back[:, pair_cols(pair, 2 * width)] = grad_value.astype(BF16)

    totals_rows[...] = totals_ref[...].T
    attend_backward(
        lambda pair: triple_ref[:, pair_cols(pair)],
        lambda pair: triple_ref[:, pair_cols(pair, width)],
        lambda pair: triple_ref[:, pair_cols(pair, 2 * width)],
        lambda pair: mixed_grad_ref[:, pair_cols(pair)],
        totals_rows,
        mask_ref,
        store,
    )
    back = triple_back[...]
    project_acc[...] += dot(normed_t_ref[...], back)
    add_row(small_out, 1, rows_sum(back[:, :width].astype(F32)))
    add_row(small_out, 2, rows_sum(back[:, 2 * width :].astype(F32)))
    weights.wait(1)
    rows_grad = dot_nt(back, project[...]).astype(BF16).astype(F32)
    unit_rows, inv_std = unit(x_ref[...].astype(F32))
    add_row(small_out, 3, rows_sum(rows_grad * unit_rows))
    add_row(small_out, 4, rows_sum(rows_grad))
    patch_grad_out[...] = grad_mid + unit_back(rows_grad, unit_rows, inv_std, gains[0:1, :])

    def write():
        part_of = quarter_rows(meta, width, parts)
        part = part_of.shape[0]
        vectors[...] = jnp.zeros_like(vectors)
        at = 0
        for small in (reg_small, reg_attn_small, enc_small, small_out):
            rows = small.shape[0]
            vectors[at : at + rows, :part] = dot_nt(small[...].astype(BF16), part_of)
            at += rows
        mine = pl.ds(pl.multiple_of(meta.band() * width, width), width)
        vectors[at : at + 8, :] = reg_wide[:, mine]
        vectors[at + 8 : at + 16, :] = enc_wide[:, mine]
        blocks = [block for ref in (vectors, output_acc, project_acc) for block in column_blocks(ref, width)]
        write_group(meta, blocks, width, (out_0, out_1, out_2, out_3))

    last_step(meta, write)


def unpack_kernel(
    meta_ref, _, keep_place, pick_place, final_ref, query_grad_ref, patch_grad_ref, final_out, query_grad_out, patch_grad_out
):
    image = pl.program_id(0)
    rows, size = final_out.shape[0], final_ref.shape[0]
    row = lax.broadcasted_iota(jnp.int32, (size, rows), 0)
    kept = (row == keep_place[pl.ds(image, 1), :][:, :rows]).astype(BF16)
    picked = (row == pick_place[pl.ds(image, 1), :][:, :rows]).astype(BF16)
    for chosen, source, target in (
        (picked, final_ref, final_out),
        (picked, query_grad_ref, query_grad_out),
        (kept, patch_grad_ref, patch_grad_out),
    ):
        values = source[...]
        high = values.astype(BF16)
        rest = (values - high.astype(F32)).astype(BF16)
        target[...] = dot_tn(chosen, high) + dot_tn(chosen, rest)


def whole(array):
    return pl.BlockSpec(array.shape, lambda *_: (0,) * array.ndim)


def by_bin(shape):
    return pl.BlockSpec((None,) + tuple(shape), lambda b, meta: (jnp.minimum(b, meta[0] - 1), 0, 0))


def for_used_bins(kernel):
    def guarded(meta_ref, _, *refs):
        @pl.when(pl.program_id(0) < meta_ref[0])
        def _():
            kernel(meta_ref, *refs)

    return guarded


IN_HBM = pl.BlockSpec(memory_space=pl.ANY)
SHORT = pl.CostEstimate(flops=2_000_000_000, bytes_accessed=1_000_000, transcendentals=0)
LONG = pl.CostEstimate(flops=20_000_000_000, bytes_accessed=10_000_000, transcendentals=0)


def binned_call(kernel, name, images, chain, meta, binned, hbm, binned_outs, full_outs, scratch):
    operands = [meta, chain.last] + [a for _, a in binned] + list(hbm)
    in_specs = [IN_HBM] + [whole(a) if kind == "full" else by_bin(a.shape[1:]) for kind, a in binned]
    in_specs += [IN_HBM] * len(hbm)
    out_shape = [jax.ShapeDtypeStruct((images,) + s, t) for s, t in binned_outs]
    out_shape += [jax.ShapeDtypeStruct(s, t) for s, t in full_outs]
    out_specs = [by_bin(s) for s, _ in binned_outs]
    out_specs += [pl.BlockSpec(s, lambda *_: (0, 0)) for s, _ in full_outs]
    outs = pl.pallas_call(
        for_used_bins(kernel),
        name=name,
        out_shape=out_shape,
        grid_spec=pltpu.PrefetchScalarGridSpec(
            num_scalar_prefetch=1,
            grid=(images,),
            in_specs=in_specs,
            out_specs=out_specs,
            scratch_shapes=scratch,
        ),
        compiler_params=pltpu.CompilerParams(
            vmem_limit_bytes=VMEM_LIMIT, dimension_semantics=("arbitrary",)
        ),
        cost_estimate=LONG,
    )(*operands)
    chain.last = outs[-1]
    return outs


def summed(mine, got, at):
    return (mine[at, :].astype(F32) + got[at, :].astype(F32)).astype(BF16)


def rows_at(index, rows):
    return pl.ds(pl.multiple_of(index * rows, rows), rows)


def turn_kernel(place, mine, got, other_mine, other_got, own, send, other_own, other_send):
    for bit, a, b, keep, out in ((1, mine, got, own, send), (0, other_mine, other_got, other_own, other_send)):
        rows = keep.shape[0]
        keep[...] = summed(a, b, rows_at(place[bit], rows))
        out[...] = summed(a, b, rows_at(1 - place[bit], rows))


def join_kernel(place, mine, got, other_mine, other_got, own, send):
    at = 0
    for a, b in ((mine, got), (other_mine, other_got)):
        rows = a.shape[0] // 2
        own[at : at + rows, :] = summed(a, b, rows_at(place[2], rows))
        send[at : at + rows, :] = summed(a, b, rows_at(1 - place[2], rows))
        at += rows


def add_kernel(place, mine, got, out):
    out[...] = summed(mine, got, slice(None))


def part_kernel(place, mine, got, out, other_out):
    at = 0
    for target in (out, other_out):
        rows = target.shape[0] // 2
        target[rows_at(place[2], rows), :] = mine[at : at + rows, :]
        target[rows_at(1 - place[2], rows), :] = got[at : at + rows, :]
        at += rows


def widen_kernel(place, mine, got, other_mine, other_got, out, other_out):
    for bit, a, b, target in ((1, mine, got, out), (0, other_mine, other_got, other_out)):
        rows = a.shape[0]
        target[rows_at(place[bit], rows), :] = a[...]
        target[rows_at(1 - place[bit], rows), :] = b[...]


def finish_kernel(quarters, vectors, place, mine, got, other_mine, other_got, *outs):
    def write(cuts, source):
        for tag, row, rows, at in cuts:
            values = source[at : at + rows, :].astype(F32)
            if tag != "vectors":
                index, column = tag
                outs[index][row : row + rows, column : column + source.shape[1]] = values
                continue
            for index, taken, columns in vectors:
                for to, one in enumerate(taken):
                    outs[index][to : to + 1, :] = values[one : one + 1, :columns]

    for bit, a, b, pair in ((0, mine, got, quarters[:2]), (1, other_mine, other_got, quarters[2:])):
        for side in range(2):

            @pl.when(place[bit] == side)
            def _():
                write(pair[0], (a, b)[side])
                write(pair[1], (b, a)[side])


class Chain:
    def __init__(self, first):
        self.last = first


class Reduction:
    def __init__(self, batch_size, chain, place, name, halves, blocks, outs, vectors=()):
        self.batch_size, self.chain, self.place, self.name = batch_size, chain, place, name
        self.quarters, self.outs, self.vectors = quarters_of(blocks), outs, vectors
        self.mine, send, self.other, other_send = halves
        self.by_hand = batch_size == 8
        self.got, self.other_got = self.exchange(send, 1), self.exchange(other_send, 2)

    def exchange(self, array, offset):
        return lax.ppermute(array, "batch", [(i, i ^ offset) for i in range(self.batch_size)])

    def call(self, kernel, step, out_shape, *arrays):
        def without_chain(place, _, *refs):
            kernel(place, *refs)

        in_vmem = pl.BlockSpec(memory_space=pltpu.VMEM)
        out = pl.pallas_call(
            without_chain,
            name=self.name + "_" + step,
            out_shape=out_shape,
            in_specs=[pl.BlockSpec(memory_space=pltpu.SMEM), IN_HBM] + [in_vmem] * len(arrays),
            out_specs=jax.tree.map(lambda _: in_vmem, out_shape),
            compiler_params=pltpu.CompilerParams(vmem_limit_bytes=STEP_LIMIT),
            cost_estimate=SHORT,
        )(self.place, self.chain.last, *[pltpu.with_memory_space_constraint(a, pltpu.VMEM) for a in arrays])
        self.chain.last = out[0] if isinstance(out, (list, tuple)) else out
        return out

    def both(self):
        return self.mine, self.got, self.other, self.other_got

    def turn(self):
        if not self.by_hand:
            size = self.batch_size
            low = [[i for i in range(size) if i % 2 == side] for side in range(2)]
            high = [[i for i in range(size) if i // 2 % 2 == side] for side in range(2)]
            self.mine = lax.psum(self.mine + self.got, "batch", axis_index_groups=low)
            self.other = lax.psum(self.other + self.other_got, "batch", axis_index_groups=high)
            return
        shapes = [half_of(a) for a in (self.mine, self.mine, self.other, self.other)]
        self.mine, send, self.other, other_send = self.call(turn_kernel, "turn", shapes, *self.both())
        self.got, self.other_got = self.exchange(send, 2), self.exchange(other_send, 1)

    def join(self):
        if self.by_hand:
            rows = (self.mine.shape[0] + self.other.shape[0]) // 2
            shape = jax.ShapeDtypeStruct((rows, self.mine.shape[1]), BF16)
            self.counts = self.mine.shape[0], self.other.shape[0]
            self.joined, send = self.call(join_kernel, "join", [shape] * 2, *self.both())
            self.joined_got = self.exchange(send, 4)

    def add(self):
        if self.by_hand:
            shape = jax.ShapeDtypeStruct(self.joined.shape, BF16)
            self.joined = self.call(add_kernel, "add", shape, self.joined, self.joined_got)
            self.joined_got = self.exchange(self.joined, 4)

    def part(self):
        if self.by_hand:
            shapes = [jax.ShapeDtypeStruct((rows, self.joined.shape[1]), BF16) for rows in self.counts]
            self.mine, self.other = self.call(part_kernel, "part", shapes, self.joined, self.joined_got)
            self.got, self.other_got = self.exchange(self.mine, 2), self.exchange(self.other, 1)

    def widen(self):
        if self.by_hand:
            shapes = [jax.ShapeDtypeStruct((2 * a.shape[0], a.shape[1]), BF16) for a in (self.mine, self.other)]
            self.mine, self.other = self.call(widen_kernel, "widen", shapes, *self.both())
        self.got, self.other_got = self.exchange(self.mine, 1), self.exchange(self.other, 2)

    def finish(self):
        return self.call(
            functools.partial(finish_kernel, self.quarters, self.vectors), "finish", list(self.outs), *self.both()
        )


def half_of(array):
    return jax.ShapeDtypeStruct((array.shape[0] // 2, array.shape[1]), BF16)


def body(
    batch_size,
    band_size,
    patches,
    queries,
    cotangent,
    counts,
    masked,
    enc_gains,
    enc_shifts,
    enc_widebias,
    enc_scales,
    enc_project,
    enc_output,
    enc_expand,
    enc_reduce,
    reg_gains,
    reg_shifts,
    reg_widebias,
    reg_scales,
    reg_query,
    reg_keyval,
    reg_output,
    reg_expand,
    reg_reduce,
):
    images, band_rows, width = patches.shape
    hidden = enc_expand.shape[1]
    band = lax.axis_index("band")
    batch = lax.axis_index("batch")
    place = jnp.stack([lax.rem(batch // bit, 2) for bit in (1, 2, 4)])
    parts = band_size
    size = parts * band_rows
    part, part_hidden = width // parts, hidden // parts

    def exchange(array, offset):
        return lax.ppermute(array, "band", [(i, i ^ offset) for i in range(parts)])

    def gather(array):
        rows = [array]
        offset = parts // 2
        while offset:
            rows = rows + [exchange(a, offset) for a in rows]
            offset //= 2
        return rows

    order = relative_order(parts)
    in_smem = pl.BlockSpec(memory_space=pltpu.SMEM)
    in_vmem = pl.BlockSpec(memory_space=pltpu.VMEM)
    tokens, flags = pl.pallas_call(
        choose_kernel,
        name="choose",
        out_shape=[
            jax.ShapeDtypeStruct(patches.shape, patches.dtype),
            jax.ShapeDtypeStruct(masked.shape, F32),
        ],
        in_specs=[in_vmem] * 3,
        out_specs=[in_vmem] * 2,
        cost_estimate=SHORT,
    )(masked, patches, queries)
    token_rows = gather(tokens)
    bands = band ^ jnp.array(order, jnp.int32)
    masked_all = jnp.concatenate([flags] + [exchange(flags, a) for a in order[1:]], 1)
    slots = (bands[:, None] * band_rows + jnp.arange(band_rows, dtype=jnp.int32)[None, :]).reshape(1, size)

    real = slots < counts[:, None]
    keep = jnp.where(real & (masked_all == 0), 1.0, 0.0).astype(F32)
    pick = jnp.where(real & (masked_all == 1), 1.0, 0.0).astype(F32)
    meta, keep_place, pick_place = pl.pallas_call(
        functools.partial(plan_kernel, images),
        name="plan",
        cost_estimate=LONG,
        out_shape=[
            jax.ShapeDtypeStruct((HEAD + 6 * images,), jnp.int32),
            jax.ShapeDtypeStruct((images, size), jnp.int32),
            jax.ShapeDtypeStruct((images, size), jnp.int32),
        ],
        in_specs=[in_smem, in_smem, in_vmem, in_vmem],
        out_specs=[in_smem, in_vmem, in_vmem],
        scratch_shapes=[pltpu.SMEM((5, images), jnp.int32)],
    )(counts, jnp.stack([band, place[0], place[1]]), keep, pick)
    cotangent = pl.pallas_call(
        hold_kernel,
        name="hold",
        out_shape=jax.ShapeDtypeStruct(cotangent.shape, cotangent.dtype),
        in_specs=[IN_HBM, IN_HBM, in_vmem],
        out_specs=in_vmem,
        cost_estimate=SHORT,
    )(token_rows[1], keep_place, cotangent)
    grad_rows = lax.all_gather(cotangent, "band", axis=0)

    chain = Chain(keep_place)
    small_rows, extra = 8, 128
    weight = functools.partial(jax.ShapeDtypeStruct, dtype=F32)

    def reduction(name, halves, outs, vectors=()):
        blocks = [(extra, "vectors")] if vectors else []
        count = len(outs) - len(vectors)
        for index in range(count):
            rows, columns = outs[index].shape
            blocks += [(rows, (index, column)) for column in range(0, columns, width)]
        return Reduction(batch_size, chain, place, name, halves, blocks, outs, vectors)

    ffn_outs = (weight((part_hidden, width)), weight((part, hidden)))

    def both(*arrays):
        return [("full", a) for a in arrays]

    def cut(*arrays):
        return [("bin", a) for a in arrays]

    def vm(shape, dtype=BF16):
        return pltpu.VMEM(shape, dtype)

    enc_wide = enc_widebias.reshape(1, hidden)
    reg_wide = reg_widebias.reshape(1, hidden)
    (
        x,
        triple,
        enc_totals,
        enc_normed_t,
        enc_mixed_t,
        enc_branch,
        enc_act,
        enc_slope,
        enc_middle_t,
        enc_ffn,
        pair_t,
        pair,
        z,
    ) = binned_call(
        functools.partial(enc_forward_kernel, images, parts),
        "enc_forward",
        images,
        chain,
        meta,
        both(keep_place, pick_place, *token_rows, enc_gains, enc_shifts, enc_wide, enc_scales, reg_gains, reg_shifts),
        (enc_project, enc_output, enc_expand, enc_reduce, reg_keyval),
        [
            ((size, width), BF16),
            ((size, 3 * width), BF16),
            ((size, LANES), F32),
            ((part, size), BF16),
            ((part, size), BF16),
            ((size, width), BF16),
            ((size, part_hidden), BF16),
            ((size, hidden), BF16),
            ((part, size), BF16),
            ((size, width), F32),
            ((part, size), BF16),
            ((size, 2 * width), BF16),
            ((size, width), BF16),
        ],
        [],
        [
            vm(enc_project.shape),
            vm(enc_output.shape),
            vm(enc_expand.shape),
            vm(enc_reduce.shape),
            vm(reg_keyval.shape),
            pltpu.SemaphoreType.DMA((5,)),
            vm((size, width), F32),
            vm((size, size), F32),
            vm((size, hidden)),
            vm((size, width)),
        ],
    )
    (
        reg_query_low,
        reg_totals,
        reg_normed_t,
        reg_mixed_t,
        final_rows,
        reg_grad_mid,
        reg_small,
        reg_wide_sum,
        *reg_ffn_grads,
    ) = binned_call(
        functools.partial(reg_forward_kernel, images, parts),
        "reg_forward",
        images,
        chain,
        meta,
        both(pick_place)
        + cut(z, pair)
        + both(reg_gains, reg_shifts, reg_wide, reg_scales),
        (reg_query, reg_output, reg_expand, reg_reduce, grad_rows),
        [
            ((size, width), BF16),
            ((size, LANES), F32),
            ((part, size), BF16),
            ((part, size), BF16),
            ((size, width), F32),
            ((size, width), F32),
        ],
        [
            ((small_rows, width), F32),
            ((small_rows, hidden), F32),
        ]
        + group_shapes(part_hidden + parts * part, width),
        [
            vm(reg_query.shape),
            vm(reg_output.shape),
            vm(reg_expand.shape),
            vm(reg_reduce.shape),
            pltpu.SemaphoreType.DMA((4 + parts,)),
            vm((size, width), F32),
            vm((size, size), F32),
            vm((size, hidden)),
            vm((size, hidden)),
            vm((size, width)),
            vm((part, hidden), F32),
            vm((part_hidden, width), F32),
            vm((parts, images, band_rows, width)),
        ],
    )
    reg_ffn = reduction("reg_ffn", reg_ffn_grads, ffn_outs)
    query_grad, encoded_grad, reg_attn_small, *reg_attn_grads = binned_call(
        functools.partial(reg_attention_kernel, images, parts),
        "reg_attention_grad",
        images,
        chain,
        meta,
        cut(z, reg_query_low, reg_totals, reg_normed_t, reg_mixed_t, reg_grad_mid, pair, pair_t, x, enc_branch, enc_ffn)
        + both(reg_gains, reg_scales, enc_scales),
        (reg_query, reg_keyval, reg_output),
        [((size, width), F32), ((size, width), F32)],
        [((small_rows, width), F32)] + group_shapes(4 * part, width),
        [
            vm(reg_query.shape),
            vm(reg_keyval.shape),
            vm(reg_output.shape),
            pltpu.SemaphoreType.DMA((3,)),
            vm((size, size), F32),
            vm((size, width)),
            vm((size, width)),
            vm((size, 2 * width)),
            vm((part, width), F32),
            vm((part, 2 * width), F32),
            vm((part, width), F32),
            vm((LANES, size), F32),
        ],
    )
    reg_attn = reduction(
        "reg_attention",
        reg_attn_grads,
        (weight((part, width)), weight((part, width)), weight((part, 2 * width))),
    )
    reg_ffn.turn()
    enc_grad_mid, enc_small, enc_wide_sum, *enc_ffn_grads = binned_call(
        functools.partial(enc_ffn_kernel, images, parts),
        "enc_ffn_grad",
        images,
        chain,
        meta,
        cut(encoded_grad, x, enc_branch, enc_ffn, enc_act, enc_slope, enc_middle_t)
        + both(enc_gains, enc_scales),
        (enc_expand, enc_reduce),
        [((size, width), F32)],
        [
            ((small_rows, width), F32),
            ((small_rows, hidden), F32),
        ]
        + group_shapes(part_hidden + parts * part, width),
        [
            vm(enc_expand.shape),
            vm(enc_reduce.shape),
            pltpu.SemaphoreType.DMA((2,)),
            vm((part, hidden), F32),
            vm((part_hidden, width), F32),
        ],
    )
    enc_ffn_sum = reduction("enc_ffn", enc_ffn_grads, ffn_outs)
    reg_ffn.join()
    reg_attn.turn()
    patch_grad, _, *enc_attn_grads = binned_call(
        functools.partial(enc_attention_kernel, images, parts),
        "enc_attention_grad",
        images,
        chain,
        meta,
        cut(enc_grad_mid, x, triple, enc_totals, enc_normed_t, enc_mixed_t)
        + both(enc_gains, enc_scales, reg_small, reg_attn_small, enc_small, reg_wide_sum, enc_wide_sum),
        (enc_output, enc_project),
        [((size, width), F32)],
        [((small_rows, width), F32)] + group_shapes(4 * part + extra, width),
        [
            vm(enc_output.shape),
            vm(enc_project.shape),
            pltpu.SemaphoreType.DMA((2,)),
            vm((size, size), F32),
            vm((size, width)),
            vm((size, 3 * width)),
            vm((part, 3 * width), F32),
            vm((part, width), F32),
            vm((LANES, size), F32),
            vm((extra, width), F32),
        ],
    )

    reg_s, reg_a, enc_s, enc_a = (small_rows * i for i in range(4))
    vectors = (
        (enc_a + 3, enc_s + 2),
        (enc_a + 4, enc_a + 1, enc_a + 2, enc_a, enc_s + 3, enc_s + 1),
        (enc_s + 4, enc_s),
        (reg_a + 3, reg_a + 5, reg_s + 2),
        (reg_a + 4, reg_a + 6, reg_a + 1, reg_a + 2, reg_a, reg_s + 3, reg_s + 1),
        (reg_s + 4, reg_s),
    )
    vector_rows = [(2 + i, rows, part) for i, rows in enumerate(vectors)]
    vector_rows += [(2 + len(vectors) + i, (enc_a + small_rows * (1 + i),), width) for i in range(2)]
    enc_attn = reduction(
        "enc_attention",
        enc_attn_grads,
        [weight((part, width)), weight((part, 3 * width))]
        + [weight((len(rows), part)) for rows in vectors]
        + [weight((1, width))] * 2,
        vector_rows,
    )
    enc_ffn_sum.turn()
    reg_ffn.add()
    reg_attn.join()
    bin_of_image = pl.BlockSpec((None, size, width), lambda i, m: (m[HEAD + i], 0, 0))
    image_out = pl.BlockSpec((None, band_rows, width), lambda i, m: (i, 0, 0))
    prediction, query_grad, patch_grad = pl.pallas_call(
        unpack_kernel,
        name="unpack",
        out_shape=[jax.ShapeDtypeStruct(patches.shape, F32)] * 3,
        grid_spec=pltpu.PrefetchScalarGridSpec(
            num_scalar_prefetch=1,
            grid=(images,),
            in_specs=[IN_HBM, whole(keep_place), whole(pick_place), bin_of_image, bin_of_image, bin_of_image],
            out_specs=[image_out] * 3,
        ),
        compiler_params=pltpu.CompilerParams(vmem_limit_bytes=VMEM_LIMIT),
        cost_estimate=LONG,
    )(meta, chain.last, keep_place, pick_place, final_rows, query_grad, patch_grad)

    chain.last = prediction
    enc_attn.turn()
    enc_ffn_sum.join()
    reg_ffn.part()
    reg_attn.add()
    enc_attn.join()
    enc_ffn_sum.add()
    reg_ffn.widen()
    reg_attn.part()
    enc_attn.add()
    enc_ffn_sum.part()
    reg_reduce_grad, reg_expand_grad = reg_ffn.finish()
    reg_attn.widen()
    enc_ffn_sum.widen()
    enc_attn.part()

    enc_attn.widen()
    reg_query_grad, reg_output_grad, reg_keyval_grad = reg_attn.finish()
    enc_reduce_grad, enc_expand_grad = enc_ffn_sum.finish()
    (
        enc_output_grad,
        enc_project_grad,
        enc_gains_grad,
        enc_shifts_grad,
        enc_scales_grad,
        reg_gains_grad,
        reg_shifts_grad,
        reg_scales_grad,
        reg_wide_grad,
        enc_wide_grad,
    ) = enc_attn.finish()
    return (
        prediction,
        patch_grad,
        query_grad,
        enc_gains_grad,
        enc_shifts_grad,
        enc_wide_grad.reshape(-1),
        enc_scales_grad,
        enc_project_grad,
        enc_output_grad,
        enc_expand_grad,
        enc_reduce_grad,
        reg_gains_grad,
        reg_shifts_grad,
        reg_wide_grad.reshape(-1),
        reg_scales_grad,
        reg_query_grad,
        reg_keyval_grad,
        reg_output_grad,
        reg_expand_grad,
        reg_reduce_grad,
    )


def solution(mesh):
    token = P("batch", "band", None)
    in_specs = (token, token, token, P("batch"), P("batch", "band")) + (P(),) * 17
    by_row, by_col = P("band", None), P(None, "band")
    out_specs = (
        token,
        token,
        token,
        by_col,
        by_col,
        P("band"),
        by_col,
        by_row,
        by_row,
        by_row,
        by_row,
        by_col,
        by_col,
        P("band"),
        by_col,
        by_row,
        by_row,
        by_row,
        by_row,
        by_row,
    )
    return jax.shard_map(
        functools.partial(body, mesh.shape["batch"], mesh.shape["band"]),
        mesh=mesh,
        in_specs=in_specs,
        out_specs=out_specs,
        check_vma=False,
    )
```

```python
import functools

import jax
import jax.numpy as jnp
from jax import lax
from jax.experimental import pallas as pl
from jax.experimental.pallas import tpu as pltpu
from jax.sharding import PartitionSpec as P

HEADS = 12
HD = 64
EPS = 1e-06
ROOT_HALF = 0.7071067811865476
INV_ROOT_TAU = 0.3989422804014327
NEG_LARGE = -1e30
F32 = jnp.float32
BF16 = jnp.bfloat16
VMEM_LIMIT = 56 * 1024 * 1024
STEP_LIMIT = 16 * 1024 * 1024
LANES = 128
HEAD = 4


def dot(a, b):
    return lax.dot_general(a, b, (((1,), (0,)), ((), ())), preferred_element_type=F32)


def dot_nt(a, b):
    return lax.dot_general(a, b, (((1,), (1,)), ((), ())), preferred_element_type=F32)


def dot_tn(a, b):
    return lax.dot_general(a, b, (((0,), (0,)), ((), ())), preferred_element_type=F32)


def unit(values):
    row_mean = jnp.mean(values, -1, keepdims=True)
    centred = values - row_mean
    variance = jnp.mean(centred * centred, -1, keepdims=True)
    inv_std = lax.rsqrt(variance + EPS)
    return centred * inv_std, inv_std


def unit_back(grad_out, unit_rows, inv_std, gain):
    scaled = grad_out * gain
    first_term = jnp.mean(scaled, -1, keepdims=True)
    second_term = jnp.mean(scaled * unit_rows, -1, keepdims=True)
    return inv_std * (scaled - first_term - unit_rows * second_term)


def rows_sum(values):
    return jnp.sum(values, 0, keepdims=True)


def gate_and_slope(pre_act):
    bell = 0.5 * (1.0 + lax.erf(pre_act * ROOT_HALF))
    slope = bell + pre_act * INV_ROOT_TAU * jnp.exp(-0.5 * pre_act * pre_act)
    return (pre_act * bell).astype(BF16), slope.astype(BF16)


def relative_order(parts):
    order, offset = [0], parts // 2
    while offset:
        order, offset = order + [a ^ offset for a in order], offset // 2
    return order


class Meta:
    def __init__(self, ref, images):
        self.ref, self.images = ref, images

    def bins(self):
        return self.ref[0]

    def band(self):
        return self.ref[1]

    def bits(self):
        return self.ref[2], self.ref[3]

    def bin_of(self, image):
        return self.ref[HEAD + image]

    def keep_off(self, image):
        return self.ref[HEAD + self.images + image]

    def keep_count(self, image):
        return self.ref[HEAD + 2 * self.images + image]

    def pick_off(self, image):
        return self.ref[HEAD + 3 * self.images + image]

    def pick_count(self, image):
        return self.ref[HEAD + 4 * self.images + image]

    def count(self, image):
        return self.ref[HEAD + 5 * self.images + image]

    def segments(self, bin_now, kind, shape, dim, blank):
        rows = lax.broadcasted_iota(jnp.int32, shape, dim)
        owner = jnp.full(shape, blank, jnp.int32)
        for image in range(self.images):
            start = self.keep_off(image) if kind == "keep" else self.pick_off(image)
            count = self.keep_count(image) if kind == "keep" else self.pick_count(image)
            stop = start + jnp.where(self.bin_of(image) == bin_now, count, 0)
            owner = jnp.where((rows >= start) & (rows < stop), image, owner)
        return owner


def key_bias(meta, bin_now, query_kind, size, key_dim):
    along = ((size, 1), (1, size))
    query_owner = meta.segments(bin_now, query_kind, along[1 - key_dim], 1 - key_dim, -2)
    key_owner = meta.segments(bin_now, "keep", along[key_dim], key_dim, -1)
    return jnp.where(query_owner == key_owner, 0.0, NEG_LARGE)


def quarter_rows(meta, width, parts):
    part = width // parts
    row = lax.broadcasted_iota(jnp.int32, (part, width), 0) + meta.band() * part
    return (row == lax.broadcasted_iota(jnp.int32, (part, width), 1)).astype(BF16)


def lower_half():
    return lax.broadcasted_iota(jnp.int32, (1, LANES), 1) < HD


def pair_cols(pair, first=0):
    at = first + pair * LANES
    return pl.ds(at if isinstance(at, int) else pl.multiple_of(at, LANES), LANES)


def each_pair(one_pair, together):
    steps = HEADS // 2 // together

    def step(index, _):
        for pair in range(together):
            one_pair(index * together + pair)
        return 0

    if steps == 1:
        step(0, 0)
    else:
        lax.fori_loop(0, steps, step, 0)


def attend_forward(query_of, key_of, value_of, bias_ref, mixed_ref, totals_ref):
    low = lower_half()
    sides = (low.astype(BF16), (~low).astype(BF16))
    key_sides = [side * HD ** (-0.5) for side in sides]
    lane = lax.broadcasted_iota(jnp.int32, totals_ref.shape, 1)
    totals_ref[...] = jnp.zeros_like(totals_ref)

    def one_pair(pair):
        query, key, value = query_of(pair), key_of(pair), value_of(pair)
        mixed = []
        for side in range(2):
            scores = dot_nt(query, key * key_sides[side]) + bias_ref[...]
            top = jnp.max(scores, -1, keepdims=True)
            exp_scores = jnp.exp(scores - top)
            total = jnp.sum(exp_scores, -1, keepdims=True)
            weights = (exp_scores * (1.0 / total)).astype(BF16)
            totals_ref[...] = jnp.where(lane == 2 * pair + side, top + jnp.log(total), totals_ref[...])
            mixed.append(dot(weights, value))
        mixed_ref[:, pair_cols(pair)] = jnp.where(low, mixed[0], mixed[1]).astype(BF16)

    each_pair(one_pair, 6)


def attend_backward(query_of, key_of, value_of, grad_of, totals_ref, bias_ref, store):
    low = lower_half()
    sides = (low.astype(BF16), (~low).astype(BF16))
    key_sides = [side * HD ** (-0.5) for side in sides]

    def one_pair(pair):
        query, key, value, grad = query_of(pair), key_of(pair), value_of(pair), grad_of(pair)
        grad_query, grad_key, grad_value = [], [], []
        for side in range(2):
            scores = dot_nt(key * key_sides[side], query) + bias_ref[...]
            probs = jnp.exp(scores - totals_ref[pl.ds(2 * pair + side, 1), :])
            grad_value.append(dot(probs.astype(BF16), grad))
            grad_probs = dot_nt(value * sides[side], grad)
            inner = jnp.sum(grad_probs * probs, 0, keepdims=True)
            grad_scores = (probs * (grad_probs - inner)).astype(BF16)
            grad_query.append(dot_tn(key, grad_scores)[side * HD : (side + 1) * HD, :])
            grad_key.append(dot(grad_scores, query))
        store(
            pair,
            jnp.concatenate(grad_query, 0).T * HD ** (-0.5),
            jnp.where(low, grad_key[0], grad_key[1]) * HD ** (-0.5),
            jnp.where(low, grad_value[0], grad_value[1]),
        )

    each_pair(one_pair, 6)


def pack_rows(meta, bin_now, place_ref, gathered, packed, size, by_block):
    packed[...] = jnp.zeros_like(packed)
    parts = len(gathered)
    slots = size // parts

    def add(image, blocks):
        taken = slice(blocks[0] * slots, (blocks[-1] + 1) * slots)
        shape = (size, len(blocks) * slots)
        row = lax.broadcasted_iota(jnp.int32, shape, 0)
        chosen = (row == place_ref[image : image + 1, taken]).astype(BF16)
        packed[...] += dot(chosen, jnp.concatenate([gathered[j][image] for j in blocks], 0))

    for image in range(meta.images):

        @pl.when(meta.bin_of(image) == bin_now)
        def _():
            if not by_block:
                add(image, range(parts))
                return
            for j, offset in enumerate(relative_order(parts)):
                pl.when(meta.count(image) > (meta.band() ^ offset) * slots)(functools.partial(add, image, [j]))


class Weights:
    def __init__(self, sources, targets, sems):
        self.copies = [
            pltpu.make_async_copy(source, target, sems.at[i])
            for i, (source, target) in enumerate(zip(sources, targets, strict=True))
        ]

    def start(self):
        @pl.when(pl.program_id(0) == 0)
        def _():
            for copy in self.copies:
                copy.start()

    def wait(self, index):
        @pl.when(pl.program_id(0) == 0)
        def _():
            self.copies[index].wait()


def add_row(small_ref, row, values):
    small_ref[row : row + 1, :] += values


def first_step(refs):
    @pl.when(pl.program_id(0) == 0)
    def _():
        for ref in refs:
            ref[...] = jnp.zeros_like(ref)


def split_rows(total):
    unit = 128
    return (total // 2 + unit - 1) // unit * unit


def cut_blocks(blocks, start, stop):
    at, cut = 0, []
    for rows, tag in blocks:
        low, high = max(at, start), min(at + rows, stop)
        if low < high:
            cut.append((tag, low - at, high - low, low - start))
        at += rows
    return cut


def quarters_of(blocks):
    total = sum(rows for rows, _ in blocks)
    first = split_rows(total)
    edges = (0, first // 2, first, first + (total - first) // 2, total)
    return [cut_blocks(blocks, a, b) for a, b in zip(edges, edges[1:], strict=False)]


def group_shapes(total, width):
    first = split_rows(total)
    return [((rows // 2, width), BF16) for rows in (first, first, total - first, total - first)]


def write_group(meta, blocks, width, outs):
    quarters = quarters_of(blocks)

    def write(cuts, out):
        for (ref, column), row, rows, at in cuts:
            values = ref[row : row + rows, column : column + width]
            out[at : at + rows, :] = values.astype(BF16)

    for bit, pair, (keep_out, send_out) in ((0, quarters[:2], outs[:2]), (1, quarters[2:], outs[2:])):
        for side in range(2):

            @pl.when(meta.bits()[bit] == side)
            def _():
                write(pair[side], keep_out)
                write(pair[1 - side], send_out)


def column_blocks(ref, width):
    return [(ref.shape[0], (ref, column)) for column in range(0, ref.shape[1], width)]


def last_step(meta, write):
    @pl.when(pl.program_id(0) == meta.bins() - 1)
    def _():
        write()


def choose_kernel(masked_ref, patches_ref, queries_ref, tokens_out, flags_out):
    flags = masked_ref[...].astype(F32)
    flags_out[...] = flags
    columns = flags.T
    for image in range(tokens_out.shape[0]):
        tokens_out[image] = jnp.where(columns[:, image : image + 1] == 0, patches_ref[image], queries_ref[image])


def hold_kernel(_, __, source, out):
    out[...] = source[...]


def plan_kernel(
    images,
    counts_ref,
    band_ref,
    keep_ref,
    pick_ref,
    _,
    meta_ref,
    keep_place_ref,
    pick_place_ref,
    words,
):
    size = keep_ref.shape[1]
    before = (
        lax.broadcasted_iota(jnp.int32, (size, size), 0)
        <= lax.broadcasted_iota(jnp.int32, (size, size), 1)
    ).astype(BF16)
    keep, pick = keep_ref[...], pick_ref[...]
    keep_rank = dot(keep.astype(BF16), before).astype(jnp.int32) - 1
    pick_rank = dot(pick.astype(BF16), before).astype(jnp.int32) - 1
    for image in range(images):
        meta_ref[HEAD + 5 * images + image] = counts_ref[image]
        words[0, image] = jnp.sum(keep[image : image + 1, :]).astype(jnp.int32)
        words[1, image] = jnp.sum(pick[image : image + 1, :]).astype(jnp.int32)
        for row in (2, 3, 4):
            words[row, image] = 0

    def place(_, bins):
        def largest(image, best):
            open_now = words[4, image] == 0
            better = open_now & ((best < 0) | (counts_ref[image] > counts_ref[jnp.maximum(best, 0)]))
            return jnp.where(better, image, best)

        image = lax.fori_loop(0, images, largest, jnp.int32(-1))
        keep_count, pick_count = words[0, image], words[1, image]

        def first_fit(step, best):
            bin_now = images - 1 - step
            fits = (words[2, bin_now] + keep_count <= size) & (words[3, bin_now] + pick_count <= size)
            return jnp.where(fits, bin_now, best)

        bin_now = lax.fori_loop(0, images, first_fit, jnp.int32(0))
        meta_ref[HEAD + image] = bin_now
        meta_ref[HEAD + images + image] = words[2, bin_now]
        meta_ref[HEAD + 2 * images + image] = keep_count
        meta_ref[HEAD + 3 * images + image] = words[3, bin_now]
        meta_ref[HEAD + 4 * images + image] = pick_count
        words[2, bin_now] = words[2, bin_now] + keep_count
        words[3, bin_now] = words[3, bin_now] + pick_count
        words[4, image] = 1
        return jnp.maximum(bins, bin_now + 1)

    meta_ref[0] = lax.fori_loop(0, images, place, jnp.int32(0))
    meta_ref[1] = band_ref[0]
    meta_ref[2] = band_ref[1]
    meta_ref[3] = band_ref[2]
    for image in range(images):
        row = slice(image, image + 1)
        keep_place_ref[row, :] = jnp.where(
            keep[row, :] > 0, keep_rank[row, :] + meta_ref[HEAD + images + image], -1
        )
        pick_place_ref[row, :] = jnp.where(
            pick[row, :] > 0, pick_rank[row, :] + meta_ref[HEAD + 3 * images + image], -1
        )


def ffn_forward(normed, expand, wide_bias, reduce_weight, act_ref, slope_ref, width):
    total = None
    for start in range(0, expand.shape[1], width):
        cols = slice(start, start + width)
        act, slope = gate_and_slope(dot(normed, expand[:, cols]) + wide_bias[:, cols])
        act_ref[:, cols] = act
        slope_ref[:, cols] = slope
        part = dot(act, reduce_weight[cols, :])
        total = part if total is None else total + part
    return total


def ffn_backward(grad_low, slope_ref, normed_part, expand, reduce_weight, expand_acc, wide_ref, width):
    total = None
    for start in range(0, expand.shape[1], width):
        cols = slice(start, start + width)
        grad_act = dot_nt(grad_low, reduce_weight[cols, :])
        grad_pre = grad_act * slope_ref[:, cols].astype(F32)
        grad_pre_low = grad_pre.astype(BF16)
        wide_ref[0:1, cols] += rows_sum(grad_pre_low.astype(F32))
        expand_acc[:, cols] += dot(normed_part, grad_pre_low)
        part = dot_nt(grad_pre_low, expand[:, cols])
        total = part if total is None else total + part
    return total


def enc_forward_kernel(images, parts, meta_ref, place_ref, pick_ref, *refs):
    enc_forward(images, parts, meta_ref, place_ref, pick_ref, refs[:parts], *refs[parts:])


def enc_forward(
    images,
    parts,
    meta_ref,
    place_ref,
    pick_ref,
    row_refs,
    gains,
    shifts,
    wide_bias,
    scales,
    reg_gains,
    reg_shifts,
    project_hbm,
    output_hbm,
    expand_hbm,
    reduce_hbm,
    keyval_hbm,
    x_out,
    triple_out,
    totals_out,
    normed_t_out,
    mixed_t_out,
    branch_out,
    act_out,
    slope_out,
    middle_t_out,
    ffn_out,
    pair_t_out,
    pair_out,
    z_out,
    project,
    output,
    expand,
    reduce_weight,
    keyval,
    sems,
    packed,
    bias_ref,
    act_all,
    mixed_ref,
):
    meta = Meta(meta_ref, images)
    bin_now = pl.program_id(0)
    weights = Weights(
        (project_hbm, output_hbm, expand_hbm, reduce_hbm, keyval_hbm),
        (project, output, expand, reduce_weight, keyval),
        sems,
    )
    weights.start()
    size, width = packed.shape
    pack_rows(meta, bin_now, pick_ref, row_refs, packed, size, False)
    z_out[...] = packed[...].astype(BF16)
    pack_rows(meta, bin_now, place_ref, row_refs, packed, size, True)
    bias_ref[...] = key_bias(meta, bin_now, "keep", size, 1)
    part_of = quarter_rows(meta, width, parts)
    x = packed[...]
    x_out[...] = x.astype(BF16)
    unit_rows, _ = unit(x)
    normed = (unit_rows * gains[0:1, :] + shifts[0:1, :]).astype(BF16)
    normed_t_out[...] = dot_nt(part_of, normed).astype(BF16)
    weights.wait(0)
    triple_out[:, :width] = (dot(normed, project[:, :width]) + shifts[1:2, :]).astype(BF16)
    triple_out[:, width : 2 * width] = dot(normed, project[:, width : 2 * width]).astype(BF16)
    triple_out[:, 2 * width :] = (dot(normed, project[:, 2 * width :]) + shifts[2:3, :]).astype(BF16)

    attend_forward(
        lambda pair: triple_out[:, pair_cols(pair)],
        lambda pair: triple_out[:, pair_cols(pair, width)],
        lambda pair: triple_out[:, pair_cols(pair, 2 * width)],
        bias_ref,
        mixed_ref,
        totals_out,
    )
    mixed = mixed_ref[...]
    mixed_t_out[...] = dot_nt(part_of, mixed).astype(BF16)
    weights.wait(1)
    branch = (dot(mixed, output[...]) + shifts[3:4, :]).astype(BF16)
    branch_out[...] = branch
    middle = x + scales[0:1, :] * branch.astype(F32)
    unit_rows, _ = unit(middle)
    normed = (unit_rows * gains[1:2, :] + shifts[4:5, :]).astype(BF16)
    middle_t_out[...] = dot_nt(part_of, normed).astype(BF16)
    weights.wait(2)
    weights.wait(3)
    part_width = expand.shape[1] // parts
    ffn = ffn_forward(normed, expand, wide_bias, reduce_weight, act_all, slope_out, part_width) + shifts[5:6, :]
    act_out[...] = act_all[:, pl.ds(pl.multiple_of(meta.band() * part_width, part_width), part_width)]
    ffn_out[...] = ffn
    encoded = middle + scales[1:2, :] * ffn
    unit_rows, _ = unit(encoded)
    pair_normed = (unit_rows * reg_gains[1:2, :] + reg_shifts[1:2, :]).astype(BF16)
    pair_t_out[...] = dot_nt(part_of, pair_normed).astype(BF16)
    weights.wait(4)
    pair_out[:, :width] = dot(pair_normed, keyval[:, :width]).astype(BF16)
    pair_out[:, width:] = (dot(pair_normed, keyval[:, width:]) + reg_shifts[3:4, :]).astype(BF16)


def reg_forward_kernel(
    images,
    parts,
    meta_ref,
    place_ref,
    z_ref,
    pair_ref,
    gains,
    shifts,
    wide_bias,
    scales,
    query_hbm,
    output_hbm,
    expand_hbm,
    reduce_hbm,
    grad_hbm,
    query_out,
    totals_out,
    normed_t_out,
    mixed_t_out,
    final_out,
    grad_mid_out,
    small_out,
    wide_out,
    out_0,
    out_1,
    out_2,
    out_3,
    query_weight,
    output,
    expand,
    reduce_weight,
    sems,
    packed_grad,
    bias_ref,
    act_all,
    slope_all,
    mixed_ref,
    expand_acc,
    reduce_acc,
    grad_rows,
):
    meta = Meta(meta_ref, images)
    bin_now = pl.program_id(0)
    relative = relative_order(parts)
    weights = Weights(
        (query_hbm, output_hbm, expand_hbm, reduce_hbm) + tuple(grad_hbm.at[meta.band() ^ i] for i in relative),
        (query_weight, output, expand, reduce_weight) + tuple(grad_rows.at[i] for i in range(parts)),
        sems,
    )
    weights.start()
    first_step((small_out, wide_out, expand_acc, reduce_acc))
    size, width = packed_grad.shape
    bias_ref[...] = key_bias(meta, bin_now, "pick", size, 1)
    part_of = quarter_rows(meta, width, parts)
    z = z_ref[...].astype(F32)
    unit_rows, _ = unit(z)
    normed = (unit_rows * gains[0:1, :] + shifts[0:1, :]).astype(BF16)
    normed_t_out[...] = dot_nt(part_of, normed).astype(BF16)
    weights.wait(0)
    query_out[...] = (dot(normed, query_weight[...]) + shifts[2:3, :]).astype(BF16)

    attend_forward(
        lambda pair: query_out[:, pair_cols(pair)],
        lambda pair: pair_ref[:, pair_cols(pair)],
        lambda pair: pair_ref[:, pair_cols(pair, width)],
        bias_ref,
        mixed_ref,
        totals_out,
    )
    mixed = mixed_ref[...]
    mixed_t_out[...] = dot_nt(part_of, mixed).astype(BF16)
    weights.wait(1)
    branch = (dot(mixed, output[...]) + shifts[4:5, :]).astype(BF16).astype(F32)
    middle = z + scales[0:1, :] * branch
    unit_rows, inv_std = unit(middle)
    normed = (unit_rows * gains[2:3, :] + shifts[5:6, :]).astype(BF16)
    normed_part = dot_nt(part_of, normed).astype(BF16)
    weights.wait(2)
    weights.wait(3)
    part_width = expand.shape[1] // parts
    ffn = ffn_forward(normed, expand, wide_bias, reduce_weight, act_all, slope_all, part_width) + shifts[6:7, :]
    final_out[...] = middle + scales[1:2, :] * ffn
    for i in range(parts):
        weights.wait(4 + i)
    pack_rows(
        meta, bin_now, place_ref, [grad_rows.at[i] for i in range(parts)], packed_grad, size, False
    )
    grad_final = packed_grad[...]
    add_row(small_out, 0, rows_sum(grad_final * ffn))
    grad_low = (scales[1:2, :] * grad_final).astype(BF16)
    add_row(small_out, 1, rows_sum(grad_low.astype(F32)))
    act_part = act_all[:, pl.ds(pl.multiple_of(meta.band() * part_width, part_width), part_width)]
    reduce_acc[...] += dot_tn(act_part, grad_low)
    grad_normed = ffn_backward(
        grad_low, slope_all, normed_part, expand, reduce_weight, expand_acc, wide_out, part_width
    )
    add_row(small_out, 2, rows_sum(grad_normed * unit_rows))
    add_row(small_out, 3, rows_sum(grad_normed))
    grad_mid = grad_final + unit_back(grad_normed, unit_rows, inv_std, gains[2:3, :])
    grad_mid_out[...] = grad_mid
    add_row(small_out, 4, rows_sum(grad_mid * branch))

    blocks = column_blocks(reduce_acc, width) + column_blocks(expand_acc, width)
    last_step(meta, lambda: write_group(meta, blocks, width, (out_0, out_1, out_2, out_3)))


def reg_attention_kernel(
    images,
    parts,
    meta_ref,
    z_ref,
    query_ref,
    totals_ref,
    normed_t_ref,
    mixed_t_ref,
    grad_mid_ref,
    pair_ref,
    pair_t_ref,
    x_ref,
    enc_branch_ref,
    enc_ffn_ref,
    gains,
    scales,
    enc_scales,
    query_hbm,
    keyval_hbm,
    output_hbm,
    query_grad_out,
    encoded_grad_out,
    small_out,
    out_0,
    out_1,
    out_2,
    out_3,
    query_weight,
    keyval,
    output,
    sems,
    bias_ref,
    mixed_grad_ref,
    query_back,
    pair_back,
    query_acc,
    pair_acc,
    output_acc,
    totals_rows,
):
    meta = Meta(meta_ref, images)
    bin_now = pl.program_id(0)
    weights = Weights((output_hbm, query_hbm, keyval_hbm), (output, query_weight, keyval), sems)
    weights.start()
    first_step((small_out, query_acc, pair_acc, output_acc))
    size, width = mixed_grad_ref.shape
    bias_ref[...] = key_bias(meta, bin_now, "pick", size, 0)
    grad_mid = grad_mid_ref[...]
    branch_grad = (scales[0:1, :] * grad_mid).astype(BF16)
    output_acc[...] += dot(mixed_t_ref[...], branch_grad)
    add_row(small_out, 0, rows_sum(branch_grad.astype(F32)))
    weights.wait(0)
    mixed_grad_ref[...] = dot_nt(branch_grad, output[...]).astype(BF16)

    def store(pair, grad_query, grad_key, grad_value):
        query_back[:, pair_cols(pair)] = grad_query.astype(BF16)
        pair_back[:, pair_cols(pair)] = grad_key.astype(BF16)
        pair_back[:, pair_cols(pair, width)] = grad_value.astype(BF16)

    totals_rows[...] = totals_ref[...].T
    attend_backward(
        lambda pair: query_ref[:, pair_cols(pair)],
        lambda pair: pair_ref[:, pair_cols(pair)],
        lambda pair: pair_ref[:, pair_cols(pair, width)],
        lambda pair: mixed_grad_ref[:, pair_cols(pair)],
        totals_rows,
        bias_ref,
        store,
    )
    grad_query, grad_pair = query_back[...], pair_back[...]
    query_acc[...] += dot(normed_t_ref[...], grad_query)
    pair_acc[...] += dot(pair_t_ref[...], grad_pair)
    add_row(small_out, 1, rows_sum(grad_query.astype(F32)))
    add_row(small_out, 2, rows_sum(grad_pair[:, width:].astype(F32)))
    weights.wait(1)
    query_side = dot_nt(grad_query, query_weight[...]).astype(BF16).astype(F32)
    weights.wait(2)
    pair_side = dot_nt(grad_pair, keyval[...]).astype(BF16).astype(F32)
    unit_rows, inv_std = unit(z_ref[...].astype(F32))
    add_row(small_out, 3, rows_sum(query_side * unit_rows))
    add_row(small_out, 4, rows_sum(query_side))
    query_grad_out[...] = grad_mid + unit_back(query_side, unit_rows, inv_std, gains[0:1, :])
    encoded = (
        x_ref[...].astype(F32)
        + enc_scales[0:1, :] * enc_branch_ref[...].astype(F32)
        + enc_scales[1:2, :] * enc_ffn_ref[...]
    )
    unit_rows, inv_std = unit(encoded)
    add_row(small_out, 5, rows_sum(pair_side * unit_rows))
    add_row(small_out, 6, rows_sum(pair_side))
    encoded_grad_out[...] = unit_back(pair_side, unit_rows, inv_std, gains[1:2, :])

    blocks = [block for ref in (query_acc, output_acc, pair_acc) for block in column_blocks(ref, width)]
    last_step(meta, lambda: write_group(meta, blocks, width, (out_0, out_1, out_2, out_3)))


def enc_ffn_kernel(
    images,
    parts,
    meta_ref,
    encoded_grad_ref,
    x_ref,
    branch_ref,
    ffn_ref,
    act_ref,
    slope_ref,
    middle_t_ref,
    gains,
    scales,
    expand_hbm,
    reduce_hbm,
    grad_mid_out,
    small_out,
    wide_out,
    out_0,
    out_1,
    out_2,
    out_3,
    expand,
    reduce_weight,
    sems,
    expand_acc,
    reduce_acc,
):
    meta = Meta(meta_ref, images)
    weights = Weights((reduce_hbm, expand_hbm), (reduce_weight, expand), sems)
    weights.start()
    first_step((small_out, wide_out, expand_acc, reduce_acc))
    width = x_ref.shape[1]
    encoded_grad = encoded_grad_ref[...]
    add_row(small_out, 0, rows_sum(encoded_grad * ffn_ref[...]))
    grad_low = (scales[1:2, :] * encoded_grad).astype(BF16)
    add_row(small_out, 1, rows_sum(grad_low.astype(F32)))
    reduce_acc[...] += dot_tn(act_ref[...], grad_low)
    weights.wait(0)
    weights.wait(1)
    part_width = expand.shape[1] // parts
    grad_normed = ffn_backward(
        grad_low, slope_ref, middle_t_ref[...], expand, reduce_weight, expand_acc, wide_out, part_width
    )
    branch = branch_ref[...].astype(F32)
    unit_rows, inv_std = unit(x_ref[...].astype(F32) + scales[0:1, :] * branch)
    add_row(small_out, 2, rows_sum(grad_normed * unit_rows))
    add_row(small_out, 3, rows_sum(grad_normed))
    grad_mid = encoded_grad + unit_back(grad_normed, unit_rows, inv_std, gains[1:2, :])
    grad_mid_out[...] = grad_mid
    add_row(small_out, 4, rows_sum(grad_mid * branch))

    blocks = column_blocks(reduce_acc, width) + column_blocks(expand_acc, width)
    last_step(meta, lambda: write_group(meta, blocks, width, (out_0, out_1, out_2, out_3)))


def enc_attention_kernel(
    images,
    parts,
    meta_ref,
    grad_mid_ref,
    x_ref,
    triple_ref,
    totals_ref,
    normed_t_ref,
    mixed_t_ref,
    gains,
    scales,
    reg_small,
    reg_attn_small,
    enc_small,
    reg_wide,
    enc_wide,
    output_hbm,
    project_hbm,
    patch_grad_out,
    small_out,
    out_0,
    out_1,
    out_2,
    out_3,
    output,
    project,
    sems,
    bias_ref,
    mixed_grad_ref,
    triple_back,
    project_acc,
    output_acc,
    totals_rows,
    vectors,
):
    meta = Meta(meta_ref, images)
    bin_now = pl.program_id(0)
    weights = Weights((output_hbm, project_hbm), (output, project), sems)
    weights.start()
    first_step((small_out, project_acc, output_acc))
    size, width = mixed_grad_ref.shape
    bias_ref[...] = key_bias(meta, bin_now, "keep", size, 0)
    grad_mid = grad_mid_ref[...]
    branch_grad = (scales[0:1, :] * grad_mid).astype(BF16)
    output_acc[...] += dot(mixed_t_ref[...], branch_grad)
    add_row(small_out, 0, rows_sum(branch_grad.astype(F32)))
    weights.wait(0)
    mixed_grad_ref[...] = dot_nt(branch_grad, output[...]).astype(BF16)

    def store(pair, grad_query, grad_key, grad_value):
        triple_back[:, pair_cols(pair)] = grad_query.astype(BF16)
        triple_back[:, pair_cols(pair, width)] = grad_key.astype(BF16)
        triple_back[:, pair_cols(pair, 2 * width)] = grad_value.astype(BF16)

    totals_rows[...] = totals_ref[...].T
    attend_backward(
        lambda pair: triple_ref[:, pair_cols(pair)],
        lambda pair: triple_ref[:, pair_cols(pair, width)],
        lambda pair: triple_ref[:, pair_cols(pair, 2 * width)],
        lambda pair: mixed_grad_ref[:, pair_cols(pair)],
        totals_rows,
        bias_ref,
        store,
    )
    back = triple_back[...]
    project_acc[...] += dot(normed_t_ref[...], back)
    add_row(small_out, 1, rows_sum(back[:, :width].astype(F32)))
    add_row(small_out, 2, rows_sum(back[:, 2 * width :].astype(F32)))
    weights.wait(1)
    rows_grad = dot_nt(back, project[...]).astype(BF16).astype(F32)
    unit_rows, inv_std = unit(x_ref[...].astype(F32))
    add_row(small_out, 3, rows_sum(rows_grad * unit_rows))
    add_row(small_out, 4, rows_sum(rows_grad))
    patch_grad_out[...] = grad_mid + unit_back(rows_grad, unit_rows, inv_std, gains[0:1, :])

    def write():
        part_of = quarter_rows(meta, width, parts)
        part = part_of.shape[0]
        vectors[...] = jnp.zeros_like(vectors)
        at = 0
        for small in (reg_small, reg_attn_small, enc_small, small_out):
            rows = small.shape[0]
            vectors[at : at + rows, :part] = dot_nt(small[...].astype(BF16), part_of)
            at += rows
        mine = pl.ds(pl.multiple_of(meta.band() * width, width), width)
        vectors[at : at + 8, :] = reg_wide[:, mine]
        vectors[at + 8 : at + 16, :] = enc_wide[:, mine]
        blocks = [block for ref in (vectors, output_acc, project_acc) for block in column_blocks(ref, width)]
        write_group(meta, blocks, width, (out_0, out_1, out_2, out_3))

    last_step(meta, write)


def unpack_kernel(
    meta_ref, _, keep_place, pick_place, final_ref, query_grad_ref, patch_grad_ref, final_out, query_grad_out, patch_grad_out
):
    image = pl.program_id(0)
    rows, size = final_out.shape[0], final_ref.shape[0]
    row = lax.broadcasted_iota(jnp.int32, (size, rows), 0)
    kept = (row == keep_place[pl.ds(image, 1), :][:, :rows]).astype(BF16)
    picked = (row == pick_place[pl.ds(image, 1), :][:, :rows]).astype(BF16)
    for chosen, source, target in (
        (picked, final_ref, final_out),
        (picked, query_grad_ref, query_grad_out),
        (kept, patch_grad_ref, patch_grad_out),
    ):
        values = source[...]
        high = values.astype(BF16)
        rest = (values - high.astype(F32)).astype(BF16)
        target[...] = dot_tn(chosen, high) + dot_tn(chosen, rest)


def whole(array):
    return pl.BlockSpec(array.shape, lambda *_: (0,) * array.ndim)


def by_bin(shape):
    return pl.BlockSpec((None,) + tuple(shape), lambda b, meta: (jnp.minimum(b, meta[0] - 1), 0, 0))


def for_used_bins(kernel):
    def guarded(meta_ref, _, *refs):
        @pl.when(pl.program_id(0) < meta_ref[0])
        def _():
            kernel(meta_ref, *refs)

    return guarded


IN_HBM = pl.BlockSpec(memory_space=pl.ANY)
SHORT = pl.CostEstimate(flops=2_000_000_000, bytes_accessed=1_000_000, transcendentals=0)
LONG = pl.CostEstimate(flops=20_000_000_000, bytes_accessed=10_000_000, transcendentals=0)


def binned_call(kernel, name, images, chain, meta, binned, hbm, binned_outs, full_outs, scratch):
    operands = [meta, chain.last] + [a for _, a in binned] + list(hbm)
    in_specs = [IN_HBM] + [whole(a) if kind == "full" else by_bin(a.shape[1:]) for kind, a in binned]
    in_specs += [IN_HBM] * len(hbm)
    out_shape = [jax.ShapeDtypeStruct((images,) + s, t) for s, t in binned_outs]
    out_shape += [jax.ShapeDtypeStruct(s, t) for s, t in full_outs]
    out_specs = [by_bin(s) for s, _ in binned_outs]
    out_specs += [pl.BlockSpec(s, lambda *_: (0, 0)) for s, _ in full_outs]
    outs = pl.pallas_call(
        for_used_bins(kernel),
        name=name,
        out_shape=out_shape,
        grid_spec=pltpu.PrefetchScalarGridSpec(
            num_scalar_prefetch=1,
            grid=(images,),
            in_specs=in_specs,
            out_specs=out_specs,
            scratch_shapes=scratch,
        ),
        compiler_params=pltpu.CompilerParams(
            vmem_limit_bytes=VMEM_LIMIT, dimension_semantics=("arbitrary",)
        ),
        cost_estimate=LONG,
    )(*operands)
    chain.last = outs[-1]
    return outs


def summed(mine, got, at):
    return (mine[at, :].astype(F32) + got[at, :].astype(F32)).astype(BF16)


def rows_at(index, rows):
    return pl.ds(pl.multiple_of(index * rows, rows), rows)


def turn_kernel(place, mine, got, other_mine, other_got, own, send, other_own, other_send):
    for bit, a, b, keep, out in ((1, mine, got, own, send), (0, other_mine, other_got, other_own, other_send)):
        rows = keep.shape[0]
        keep[...] = summed(a, b, rows_at(place[bit], rows))
        out[...] = summed(a, b, rows_at(1 - place[bit], rows))


def join_kernel(place, mine, got, other_mine, other_got, own, send):
    at = 0
    for a, b in ((mine, got), (other_mine, other_got)):
        rows = a.shape[0] // 2
        own[at : at + rows, :] = summed(a, b, rows_at(place[2], rows))
        send[at : at + rows, :] = summed(a, b, rows_at(1 - place[2], rows))
        at += rows


def add_kernel(place, mine, got, out):
    out[...] = summed(mine, got, slice(None))


def part_kernel(place, mine, got, out, other_out):
    at = 0
    for target in (out, other_out):
        rows = target.shape[0] // 2
        target[rows_at(place[2], rows), :] = mine[at : at + rows, :]
        target[rows_at(1 - place[2], rows), :] = got[at : at + rows, :]
        at += rows


def widen_kernel(place, mine, got, other_mine, other_got, out, other_out):
    for bit, a, b, target in ((1, mine, got, out), (0, other_mine, other_got, other_out)):
        rows = a.shape[0]
        target[rows_at(place[bit], rows), :] = a[...]
        target[rows_at(1 - place[bit], rows), :] = b[...]


def finish_kernel(quarters, vectors, place, mine, got, other_mine, other_got, *outs):
    def write(cuts, source):
        for tag, row, rows, at in cuts:
            values = source[at : at + rows, :].astype(F32)
            if tag != "vectors":
                index, column = tag
                outs[index][row : row + rows, column : column + source.shape[1]] = values
                continue
            for index, taken, columns in vectors:
                for to, one in enumerate(taken):
                    if len(outs[index].shape) == 1:
                        outs[index][...] = values[one, :columns]
                    else:
                        outs[index][to : to + 1, :] = values[one : one + 1, :columns]

    for bit, a, b, pair in ((0, mine, got, quarters[:2]), (1, other_mine, other_got, quarters[2:])):
        for side in range(2):

            @pl.when(place[bit] == side)
            def _():
                write(pair[0], (a, b)[side])
                write(pair[1], (b, a)[side])


class Chain:
    def __init__(self, first):
        self.last = first


class Reduction:
    def __init__(self, batch_size, chain, place, name, halves, blocks, outs, vectors=()):
        self.batch_size, self.chain, self.place, self.name = batch_size, chain, place, name
        self.quarters, self.outs, self.vectors = quarters_of(blocks), outs, vectors
        self.mine, send, self.other, other_send = halves
        self.by_hand = batch_size == 8
        self.got, self.other_got = self.exchange(send, 1), self.exchange(other_send, 2)

    def exchange(self, array, offset):
        return lax.ppermute(array, "batch", [(i, i ^ offset) for i in range(self.batch_size)])

    def call(self, kernel, step, out_shape, *arrays):
        def without_chain(place, _, *refs):
            kernel(place, *refs)

        in_vmem = pl.BlockSpec(memory_space=pltpu.VMEM)
        out = pl.pallas_call(
            without_chain,
            name=self.name + "_" + step,
            out_shape=out_shape,
            in_specs=[pl.BlockSpec(memory_space=pltpu.SMEM), IN_HBM] + [in_vmem] * len(arrays),
            out_specs=jax.tree.map(lambda _: in_vmem, out_shape),
            compiler_params=pltpu.CompilerParams(vmem_limit_bytes=STEP_LIMIT),
            cost_estimate=SHORT,
        )(self.place, self.chain.last, *[pltpu.with_memory_space_constraint(a, pltpu.VMEM) for a in arrays])
        self.chain.last = out[0] if isinstance(out, (list, tuple)) else out
        return out

    def both(self):
        return self.mine, self.got, self.other, self.other_got

    def turn(self):
        if not self.by_hand:
            size = self.batch_size
            low = [[i for i in range(size) if i % 2 == side] for side in range(2)]
            high = [[i for i in range(size) if i // 2 % 2 == side] for side in range(2)]
            self.mine = lax.psum(self.mine + self.got, "batch", axis_index_groups=low)
            self.other = lax.psum(self.other + self.other_got, "batch", axis_index_groups=high)
            return
        shapes = [half_of(a) for a in (self.mine, self.mine, self.other, self.other)]
        self.mine, send, self.other, other_send = self.call(turn_kernel, "turn", shapes, *self.both())
        self.got, self.other_got = self.exchange(send, 2), self.exchange(other_send, 1)

    def join(self):
        if self.by_hand:
            rows = (self.mine.shape[0] + self.other.shape[0]) // 2
            shape = jax.ShapeDtypeStruct((rows, self.mine.shape[1]), BF16)
            self.counts = self.mine.shape[0], self.other.shape[0]
            self.joined, send = self.call(join_kernel, "join", [shape] * 2, *self.both())
            self.joined_got = self.exchange(send, 4)

    def add(self):
        if self.by_hand:
            shape = jax.ShapeDtypeStruct(self.joined.shape, BF16)
            self.joined = self.call(add_kernel, "add", shape, self.joined, self.joined_got)
            self.joined_got = self.exchange(self.joined, 4)

    def part(self):
        if self.by_hand:
            shapes = [jax.ShapeDtypeStruct((rows, self.joined.shape[1]), BF16) for rows in self.counts]
            self.mine, self.other = self.call(part_kernel, "part", shapes, self.joined, self.joined_got)
            self.got, self.other_got = self.exchange(self.mine, 2), self.exchange(self.other, 1)

    def widen(self):
        if self.by_hand:
            shapes = [jax.ShapeDtypeStruct((2 * a.shape[0], a.shape[1]), BF16) for a in (self.mine, self.other)]
            self.mine, self.other = self.call(widen_kernel, "widen", shapes, *self.both())
        self.got, self.other_got = self.exchange(self.mine, 1), self.exchange(self.other, 2)

    def finish(self):
        return self.call(
            functools.partial(finish_kernel, self.quarters, self.vectors), "finish", list(self.outs), *self.both()
        )


def half_of(array):
    return jax.ShapeDtypeStruct((array.shape[0] // 2, array.shape[1]), BF16)


def body(
    batch_size,
    band_size,
    patches,
    queries,
    cotangent,
    counts,
    masked,
    enc_gains,
    enc_shifts,
    enc_widebias,
    enc_scales,
    enc_project,
    enc_output,
    enc_expand,
    enc_reduce,
    reg_gains,
    reg_shifts,
    reg_widebias,
    reg_scales,
    reg_query,
    reg_keyval,
    reg_output,
    reg_expand,
    reg_reduce,
):
    images, band_rows, width = patches.shape
    hidden = enc_expand.shape[1]
    band = lax.axis_index("band")
    batch = lax.axis_index("batch")
    place = jnp.stack([lax.rem(batch // bit, 2) for bit in (1, 2, 4)])
    parts = band_size
    size = parts * band_rows
    part, part_hidden = width // parts, hidden // parts

    def exchange(array, offset):
        return lax.ppermute(array, "band", [(i, i ^ offset) for i in range(parts)])

    def gather(array):
        rows = [array]
        offset = parts // 2
        while offset:
            rows = rows + [exchange(a, offset) for a in rows]
            offset //= 2
        return rows

    order = relative_order(parts)
    in_smem = pl.BlockSpec(memory_space=pltpu.SMEM)
    in_vmem = pl.BlockSpec(memory_space=pltpu.VMEM)
    tokens, flags = pl.pallas_call(
        choose_kernel,
        name="choose",
        out_shape=[
            jax.ShapeDtypeStruct(patches.shape, patches.dtype),
            jax.ShapeDtypeStruct(masked.shape, F32),
        ],
        in_specs=[in_vmem] * 3,
        out_specs=[in_vmem] * 2,
        cost_estimate=SHORT,
    )(masked, patches, queries)
    token_rows = gather(tokens)
    bands = band ^ jnp.array(order, jnp.int32)
    masked_all = jnp.concatenate([flags] + [exchange(flags, a) for a in order[1:]], 1)
    slots = (bands[:, None] * band_rows + jnp.arange(band_rows, dtype=jnp.int32)[None, :]).reshape(1, size)

    real = slots < counts[:, None]
    keep = jnp.where(real & (masked_all == 0), 1.0, 0.0).astype(F32)
    pick = jnp.where(real & (masked_all == 1), 1.0, 0.0).astype(F32)
    meta, keep_place, pick_place = pl.pallas_call(
        functools.partial(plan_kernel, images),
        name="plan",
        cost_estimate=LONG,
        out_shape=[
            jax.ShapeDtypeStruct((HEAD + 6 * images,), jnp.int32),
            jax.ShapeDtypeStruct((images, size), jnp.int32),
            jax.ShapeDtypeStruct((images, size), jnp.int32),
        ],
        in_specs=[in_smem, in_smem, in_vmem, in_vmem, IN_HBM],
        out_specs=[in_smem, in_vmem, in_vmem],
        scratch_shapes=[pltpu.SMEM((5, images), jnp.int32)],
    )(counts, jnp.stack([band, place[0], place[1]]), keep, pick, token_rows[2])
    cotangent = pl.pallas_call(
        hold_kernel,
        name="hold",
        out_shape=jax.ShapeDtypeStruct(cotangent.shape, cotangent.dtype),
        in_specs=[IN_HBM, IN_HBM, in_vmem],
        out_specs=in_vmem,
        cost_estimate=SHORT,
    )(token_rows[1], keep_place, cotangent)
    grad_rows = lax.all_gather(cotangent, "band", axis=0)

    chain = Chain(keep_place)
    small_rows, extra = 8, 128
    weight = functools.partial(jax.ShapeDtypeStruct, dtype=F32)

    def reduction(name, halves, outs, vectors=()):
        blocks = [(extra, "vectors")] if vectors else []
        count = len(outs) - len(vectors)
        for index in range(count):
            rows, columns = outs[index].shape
            blocks += [(rows, (index, column)) for column in range(0, columns, width)]
        return Reduction(batch_size, chain, place, name, halves, blocks, outs, vectors)

    ffn_outs = (weight((part_hidden, width)), weight((part, hidden)))

    def both(*arrays):
        return [("full", a) for a in arrays]

    def cut(*arrays):
        return [("bin", a) for a in arrays]

    def vm(shape, dtype=BF16):
        return pltpu.VMEM(shape, dtype)

    enc_wide = enc_widebias.reshape(1, hidden)
    reg_wide = reg_widebias.reshape(1, hidden)
    (
        x,
        triple,
        enc_totals,
        enc_normed_t,
        enc_mixed_t,
        enc_branch,
        enc_act,
        enc_slope,
        enc_middle_t,
        enc_ffn,
        pair_t,
        pair,
        z,
    ) = binned_call(
        functools.partial(enc_forward_kernel, images, parts),
        "enc_forward",
        images,
        chain,
        meta,
        both(keep_place, pick_place, *token_rows, enc_gains, enc_shifts, enc_wide, enc_scales, reg_gains, reg_shifts),
        (enc_project, enc_output, enc_expand, enc_reduce, reg_keyval),
        [
            ((size, width), BF16),
            ((size, 3 * width), BF16),
            ((size, LANES), F32),
            ((part, size), BF16),
            ((part, size), BF16),
            ((size, width), BF16),
            ((size, part_hidden), BF16),
            ((size, hidden), BF16),
            ((part, size), BF16),
            ((size, width), F32),
            ((part, size), BF16),
            ((size, 2 * width), BF16),
            ((size, width), BF16),
        ],
        [],
        [
            vm(enc_project.shape),
            vm(enc_output.shape),
            vm(enc_expand.shape),
            vm(enc_reduce.shape),
            vm(reg_keyval.shape),
            pltpu.SemaphoreType.DMA((5,)),
            vm((size, width), F32),
            vm((size, size), F32),
            vm((size, hidden)),
            vm((size, width)),
        ],
    )
    (
        reg_query_low,
        reg_totals,
        reg_normed_t,
        reg_mixed_t,
        final_rows,
        reg_grad_mid,
        reg_small,
        reg_wide_sum,
        *reg_ffn_grads,
    ) = binned_call(
        functools.partial(reg_forward_kernel, images, parts),
        "reg_forward",
        images,
        chain,
        meta,
        both(pick_place)
        + cut(z, pair)
        + both(reg_gains, reg_shifts, reg_wide, reg_scales),
        (reg_query, reg_output, reg_expand, reg_reduce, grad_rows),
        [
            ((size, width), BF16),
            ((size, LANES), F32),
            ((part, size), BF16),
            ((part, size), BF16),
            ((size, width), F32),
            ((size, width), F32),
        ],
        [
            ((small_rows, width), F32),
            ((small_rows, hidden), F32),
        ]
        + group_shapes(part_hidden + parts * part, width),
        [
            vm(reg_query.shape),
            vm(reg_output.shape),
            vm(reg_expand.shape),
            vm(reg_reduce.shape),
            pltpu.SemaphoreType.DMA((4 + parts,)),
            vm((size, width), F32),
            vm((size, size), F32),
            vm((size, hidden)),
            vm((size, hidden)),
            vm((size, width)),
            vm((part, hidden), F32),
            vm((part_hidden, width), F32),
            vm((parts, images, band_rows, width)),
        ],
    )
    reg_ffn = reduction("reg_ffn", reg_ffn_grads, ffn_outs)
    query_grad, encoded_grad, reg_attn_small, *reg_attn_grads = binned_call(
        functools.partial(reg_attention_kernel, images, parts),
        "reg_attention_grad",
        images,
        chain,
        meta,
        cut(z, reg_query_low, reg_totals, reg_normed_t, reg_mixed_t, reg_grad_mid, pair, pair_t, x, enc_branch, enc_ffn)
        + both(reg_gains, reg_scales, enc_scales),
        (reg_query, reg_keyval, reg_output),
        [((size, width), F32), ((size, width), F32)],
        [((small_rows, width), F32)] + group_shapes(4 * part, width),
        [
            vm(reg_query.shape),
            vm(reg_keyval.shape),
            vm(reg_output.shape),
            pltpu.SemaphoreType.DMA((3,)),
            vm((size, size), F32),
            vm((size, width)),
            vm((size, width)),
            vm((size, 2 * width)),
            vm((part, width), F32),
            vm((part, 2 * width), F32),
            vm((part, width), F32),
            vm((LANES, size), F32),
        ],
    )
    reg_attn = reduction(
        "reg_attention",
        reg_attn_grads,
        (weight((part, width)), weight((part, width)), weight((part, 2 * width))),
    )
    reg_ffn.turn()
    enc_grad_mid, enc_small, enc_wide_sum, *enc_ffn_grads = binned_call(
        functools.partial(enc_ffn_kernel, images, parts),
        "enc_ffn_grad",
        images,
        chain,
        meta,
        cut(encoded_grad, x, enc_branch, enc_ffn, enc_act, enc_slope, enc_middle_t)
        + both(enc_gains, enc_scales),
        (enc_expand, enc_reduce),
        [((size, width), F32)],
        [
            ((small_rows, width), F32),
            ((small_rows, hidden), F32),
        ]
        + group_shapes(part_hidden + parts * part, width),
        [
            vm(enc_expand.shape),
            vm(enc_reduce.shape),
            pltpu.SemaphoreType.DMA((2,)),
            vm((part, hidden), F32),
            vm((part_hidden, width), F32),
        ],
    )
    enc_ffn_sum = reduction("enc_ffn", enc_ffn_grads, ffn_outs)
    reg_ffn.join()
    reg_attn.turn()
    patch_grad, _, *enc_attn_grads = binned_call(
        functools.partial(enc_attention_kernel, images, parts),
        "enc_attention_grad",
        images,
        chain,
        meta,
        cut(enc_grad_mid, x, triple, enc_totals, enc_normed_t, enc_mixed_t)
        + both(enc_gains, enc_scales, reg_small, reg_attn_small, enc_small, reg_wide_sum, enc_wide_sum),
        (enc_output, enc_project),
        [((size, width), F32)],
        [((small_rows, width), F32)] + group_shapes(4 * part + extra, width),
        [
            vm(enc_output.shape),
            vm(enc_project.shape),
            pltpu.SemaphoreType.DMA((2,)),
            vm((size, size), F32),
            vm((size, width)),
            vm((size, 3 * width)),
            vm((part, 3 * width), F32),
            vm((part, width), F32),
            vm((LANES, size), F32),
            vm((extra, width), F32),
        ],
    )

    reg_s, reg_a, enc_s, enc_a = (small_rows * i for i in range(4))
    vectors = (
        (enc_a + 3, enc_s + 2),
        (enc_a + 4, enc_a + 1, enc_a + 2, enc_a, enc_s + 3, enc_s + 1),
        (enc_s + 4, enc_s),
        (reg_a + 3, reg_a + 5, reg_s + 2),
        (reg_a + 4, reg_a + 6, reg_a + 1, reg_a + 2, reg_a, reg_s + 3, reg_s + 1),
        (reg_s + 4, reg_s),
    )
    vector_rows = [(2 + i, rows, part) for i, rows in enumerate(vectors)]
    vector_rows += [(2 + len(vectors) + i, (enc_a + small_rows * (1 + i),), width) for i in range(2)]
    enc_attn = reduction(
        "enc_attention",
        enc_attn_grads,
        [weight((part, width)), weight((part, 3 * width))]
        + [weight((len(rows), part)) for rows in vectors]
        + [weight((width,))] * 2,
        vector_rows,
    )
    enc_ffn_sum.turn()
    reg_ffn.add()
    reg_attn.join()
    bin_of_image = pl.BlockSpec((None, size, width), lambda i, m: (m[HEAD + i], 0, 0))
    image_out = pl.BlockSpec((None, band_rows, width), lambda i, m: (i, 0, 0))
    prediction, query_grad, patch_grad = pl.pallas_call(
        unpack_kernel,
        name="unpack",
        out_shape=[jax.ShapeDtypeStruct(patches.shape, F32)] * 3,
        grid_spec=pltpu.PrefetchScalarGridSpec(
            num_scalar_prefetch=1,
            grid=(images,),
            in_specs=[IN_HBM, whole(keep_place), whole(pick_place), bin_of_image, bin_of_image, bin_of_image],
            out_specs=[image_out] * 3,
        ),
        compiler_params=pltpu.CompilerParams(vmem_limit_bytes=VMEM_LIMIT),
        cost_estimate=LONG,
    )(meta, chain.last, keep_place, pick_place, final_rows, query_grad, patch_grad)

    chain.last = prediction
    enc_attn.turn()
    enc_ffn_sum.join()
    reg_ffn.part()
    reg_attn.add()
    enc_attn.join()
    enc_ffn_sum.add()
    reg_ffn.widen()
    reg_attn.part()
    enc_attn.add()
    enc_ffn_sum.part()
    reg_reduce_grad, reg_expand_grad = reg_ffn.finish()
    reg_attn.widen()
    enc_attn.part()
    enc_ffn_sum.widen()
    enc_attn.widen()
    reg_query_grad, reg_output_grad, reg_keyval_grad = reg_attn.finish()
    enc_reduce_grad, enc_expand_grad = enc_ffn_sum.finish()
    (
        enc_output_grad,
        enc_project_grad,
        enc_gains_grad,
        enc_shifts_grad,
        enc_scales_grad,
        reg_gains_grad,
        reg_shifts_grad,
        reg_scales_grad,
        reg_wide_grad,
        enc_wide_grad,
    ) = enc_attn.finish()
    return (
        prediction,
        patch_grad,
        query_grad,
        enc_gains_grad,
        enc_shifts_grad,
        enc_wide_grad,
        enc_scales_grad,
        enc_project_grad,
        enc_output_grad,
        enc_expand_grad,
        enc_reduce_grad,
        reg_gains_grad,
        reg_shifts_grad,
        reg_wide_grad,
        reg_scales_grad,
        reg_query_grad,
        reg_keyval_grad,
        reg_output_grad,
        reg_expand_grad,
        reg_reduce_grad,
    )


def solution(mesh):
    token = P("batch", "band", None)
    in_specs = (token, token, token, P("batch"), P("batch", "band")) + (P(),) * 17
    by_row, by_col = P("band", None), P(None, "band")
    out_specs = (
        token,
        token,
        token,
        by_col,
        by_col,
        P("band"),
        by_col,
        by_row,
        by_row,
        by_row,
        by_row,
        by_col,
        by_col,
        P("band"),
        by_col,
        by_row,
        by_row,
        by_row,
        by_row,
        by_row,
    )
    return jax.shard_map(
        functools.partial(body, mesh.shape["batch"], mesh.shape["band"]),
        mesh=mesh,
        in_specs=in_specs,
        out_specs=out_specs,
        check_vma=False,
    )
```
